256 devices in a mesh: row: 16 (over x, z_hi), col: 16 (over y, z_lo, core).
Axes of the slice: x: 4, y: 4, z: 8 (z_hi: 4, z_lo: 2; z = z_hi * 2 + z_lo), core: 2. Of those that a mesh axis runs over, the one named last changes fastest.
Arguments:
- image_feats: bfloat16 [32768, 1408], P(('row', 'col')), may hold values from -6 to 6
- text_emb: bfloat16 [32768, 1024], P(('row', 'col')), may hold values from -6 to 6
- projection: bfloat16 [1408, 1024], replicated, may hold values from -0.15625 to 0.15625
- clip_norms: float32 [4096], P(('row', 'col')), may hold values from 10 to 200
- user_ids: int32 [32768], P(('row', 'col')), may hold values from 0 to 4095, as said below
- grad_sum: float32 [11264, 128], P(('row', 'col')), may hold values from -8 to 8
- init_weights: float32 [11264, 128], P(('row', 'col')), may hold values from -0.15625 to 0.15625
- tree_noise: float32 [11264, 128], P(('row', 'col')), may hold values from -20 to 20
Outputs:
- new_weights: bfloat16 [1408, 1024], replicated
- new_grad_sum: float32 [11264, 128], P(('row', 'col'))
The draws below stay inside these ranges and needn't reach their ends.
Inputs may be any that keep to these rules, and one draw needn't show every extreme that they name: `user_ids`: the pairs of rows b * 128 to (b + 1) * 128 - 1 (the pairs of one device) carry the user ids b * 16 to (b + 1) * 16 - 1, each at least once, so all pairs of a user lie in one such block.
All inputs are finite; a program needn't handle non-finite values.
Results may differ from the reference program's by a relative error of at most 0.0049.
The reference program's roundings to bfloat16 on the way (of `image_unit`, `text_unit`, `pair_weight` and `clipped`) count: a program that leaves them out, or rounds other values in their place, can miss the bound.
Values may be sent and summed in bfloat16 or wider, within the bound.
A program may use at most 64 MiB of HBM per device.

```python
import math
import jax
import jax.numpy as jnp
from jax import lax

W = 1408
E = 1024
P_DEV = 128
USR_DEV = 16
PAIRS = 32768
USERS = 4096
FLAT = 11264


def draw_user_ids(key, part):
    key = jax.random.fold_in(key, 11)
    blocks = PAIRS // P_DEV

    def one_block(block_key, block_index):
        extra = jax.random.randint(block_key, (P_DEV - USR_DEV,), 0, USR_DEV).astype(jnp.int32)
        listed = jnp.concatenate([jnp.arange(USR_DEV, dtype=jnp.int32), extra])
        shuffled = jax.random.permutation(jax.random.fold_in(block_key, 1), listed)
        return shuffled + block_index * USR_DEV
    block_keys = jax.random.split(key, blocks)
    return jax.vmap(one_block)(block_keys, jnp.arange(blocks, dtype=jnp.int32)).reshape(PAIRS)


def draw_grad_sum(key, part):
    key = jax.random.fold_in(key, 7)
    position = (jnp.arange(FLAT, dtype=jnp.float32) / (FLAT - 1))[:, None]
    sample = jax.random.truncated_normal(key, -5.0, 5.0, (FLAT, 128), jnp.float32)
    spread = 1.0 + 4.0 * position
    return 0.3 * sample * spread


def draw_tree_noise(key, part):
    key = jax.random.fold_in(key, 13)
    position = (jnp.arange(FLAT, dtype=jnp.float32) / (FLAT - 1))[:, None]
    sample = jax.random.truncated_normal(key, -5.0, 5.0, (FLAT, 128), jnp.float32)
    spread = 1.0 + 3.0 * position
    return sample * spread


def block_scale(own_key, extent, pieces, smallest, top_value):
    level, own = 1.0, jax.random.fold_in(own_key, 6)
    for axis_at, blocks in pieces:
        draws = jnp.exp(jax.random.uniform(jax.random.fold_in(own, axis_at), (blocks,), jnp.float32, smallest / len(pieces), top_value / len(pieces)))
        level = level * jnp.repeat(draws, extent[axis_at] // blocks).reshape([-1 if axis == axis_at else 1 for axis in range(len(extent))])
    return level


def normal_values(stream_key, shape, scale, most, cuts=(), kind=jnp.bfloat16):
    entries = jax.random.normal(stream_key, shape, jnp.float32) * scale
    if len(cuts) > 0:
        entries = block_scale(stream_key, shape, cuts, -0.22, 0.18) * entries
    return jnp.clip(entries, min=-most, max=most).astype(kind)


def setup_inputs(seed: int = 0) -> dict:
    splits = jax.random.split(jax.random.key(seed), 9)
    image_feats = normal_values(splits[0], (PAIRS, W), 1.0, 6.0, ((0, 256),))
    text_emb = normal_values(splits[1], (PAIRS, E), 1.0, 6.0, ((0, 256),))
    projection = normal_values(splits[2], (W, E), W ** -0.5, 0.15625)
    clip_norms = jnp.clip(jnp.exp(math.log(200.0) - 2.9957323 * jax.random.uniform(splits[3], (USERS,), jnp.float32) ** block_scale(splits[3], (USERS,), ((0, 256),), -0.2, 0.2)), 10.0, 200.0)
    user_ids = draw_user_ids(jax.random.fold_in(splits[8], 71), 0)
    grad_sum = draw_grad_sum(jax.random.fold_in(splits[8], 71), 0)
    init_weights = normal_values(splits[6], (FLAT, 128), W ** -0.5, 0.15625, ((0, 256),), jnp.float32)
    tree_noise = draw_tree_noise(jax.random.fold_in(splits[8], 71), 0)
    return {"image_feats": image_feats, "text_emb": text_emb, "projection": projection, "clip_norms": clip_norms, "user_ids": user_ids, "grad_sum": grad_sum, "init_weights": init_weights, "tree_noise": tree_noise}


LOGIT_SCALE = 32.0
LOGIT_BIAS = -5.0
RATE = 0.5
EPSILON = 1e-06

def reference(image_feats, text_emb, projection, clip_norms, user_ids, grad_sum, init_weights, tree_noise):
    image_raw = jnp.dot(image_feats, projection, preferred_element_type=jnp.float32)
    inverse = lax.rsqrt(lax.optimization_barrier(jnp.sum(image_raw * image_raw, axis=1, keepdims=True)) + EPSILON)
    image_unit = (image_raw * inverse).astype(jnp.bfloat16)
    text_float = text_emb.astype(jnp.float32)
    text_unit = (text_float * lax.rsqrt(lax.optimization_barrier(jnp.sum(text_float * text_float, axis=1, keepdims=True)) + EPSILON)).astype(jnp.bfloat16)
    blocks = PAIRS // P_DEV
    text_index = lax.broadcasted_iota(jnp.int32, (1, PAIRS), 1)

    def block_grad(block_index):
        image_rows = lax.dynamic_slice_in_dim(image_unit, block_index * P_DEV, P_DEV, 0)
        logits = LOGIT_SCALE * jnp.dot(image_rows, text_unit.T, preferred_element_type=jnp.float32) + LOGIT_BIAS
        own_index = block_index * P_DEV + lax.broadcasted_iota(jnp.int32, (P_DEV, 1), 0)
        positive = (own_index == text_index).astype(jnp.float32)
        pair_weight = (jax.nn.sigmoid(logits) - positive).astype(jnp.bfloat16)
        return LOGIT_SCALE * jnp.dot(pair_weight, text_unit, preferred_element_type=jnp.float32)
    unit_grad = lax.map(block_grad, jnp.arange(blocks, dtype=jnp.int32)).reshape(PAIRS, E)
    inner = lax.optimization_barrier(jnp.sum(image_raw * unit_grad, axis=1, keepdims=True))
    embed_grad = inverse * unit_grad - inverse * inverse * inverse * image_raw * inner

    def block_clip(block_index):
        features = lax.dynamic_slice_in_dim(image_feats, block_index * P_DEV, P_DEV, 0)
        grads = lax.dynamic_slice_in_dim(embed_grad, block_index * P_DEV, P_DEV, 0)
        owners = lax.dynamic_slice_in_dim(user_ids, block_index * P_DEV, P_DEV, 0)
        user_bound = clip_norms[owners]
        feat_gram = jnp.dot(features, features.T, preferred_element_type=jnp.float32)
        grad_gram = jnp.dot(grads, grads.T, precision=lax.Precision.HIGHEST)
        same_user = owners[:, None] == owners[None, :]
        row_terms = lax.optimization_barrier(jnp.sum(jnp.where(same_user, feat_gram * grad_gram, jnp.float32(0.0)), axis=1))
        user_sq = lax.optimization_barrier(jnp.sum(jnp.where(same_user, row_terms[None, :], jnp.float32(0.0)), axis=1))
        factor = user_bound / jnp.maximum(jnp.sqrt(user_sq), user_bound)
        return (factor[:, None] * grads).astype(jnp.bfloat16)
    clipped = lax.map(block_clip, jnp.arange(blocks, dtype=jnp.int32)).reshape(PAIRS, E)
    batch_grad = jnp.dot(image_feats.T, clipped, preferred_element_type=jnp.float32)
    new_grad_sum = grad_sum + batch_grad.reshape(FLAT, 128)
    update = new_grad_sum + tree_noise
    norm_cap = math.sqrt(W * E)
    shrink = norm_cap / jnp.maximum(jnp.sqrt(jnp.sum(update * update)), norm_cap)
    new_weights = (init_weights - RATE * shrink * update).astype(jnp.bfloat16).reshape(W, E)
    return (new_weights, new_grad_sum)
```

```python
import math

import jax
import jax.numpy as jnp
from jax import lax
from jax.experimental import pallas as pl
from jax.experimental.pallas import tpu as pltpu
from jax.sharding import PartitionSpec as P

LOGIT_SCALE = 32.0
LOGIT_BIAS = -5.0
RATE = 0.5
EPSILON = 1e-06

MESH = pl.DeviceIdType.MESH
X, Y, Z = 4, 4, 8
W, E, PAIRS, USERS = 1408, 1024, 128, 16
SHARE = W // X
BLOCK = SHARE // Z
PADDED = 48
WIDE = Z * PADDED
TEXTS = 2 * X * Y * PAIRS
CHUNK = 512
IMAGES = 2 * PAIRS
SLOT = E + 128
COPIES = 224
F32, BF16 = jnp.float32, jnp.bfloat16


def place():
    row, col = lax.axis_index("row"), lax.axis_index("col")
    x, zh = lax.div(row, 4), lax.rem(row, 4)
    y, zl, c = lax.div(col, 4), lax.rem(lax.div(col, 2), 2), lax.rem(col, 2)
    return x, y, zh * 2 + zl, c


def device(x, y, z, c):
    return (x * 4 + lax.div(z, 2), y * 4 + lax.rem(z, 2) * 2 + c)


def shift(value, by, size):
    return lax.rem(value + by, size)


class Copies:
    def __init__(self, send_sems, recv_sems):
        self.send_sems, self.recv_sems, self.used, self.all = send_sems, recv_sems, 0, []

    def reserve(self, count):
        self.used += count
        return self.used - count

    def make(self, src, dst, target, send_at, recv_at):
        return pltpu.make_async_remote_copy(
            src_ref=src,
            dst_ref=dst,
            send_sem=self.send_sems.at[send_at],
            recv_sem=self.recv_sems.at[recv_at],
            device_id=target,
            device_id_type=MESH,
        )

    def plan(self, src, dst, target):
        at = self.reserve(1)
        copy = self.make(src, dst, target, at, at)
        self.all.append(copy)
        return copy

    def push(self, src, dst, target):
        copy = self.plan(src, dst, target)
        copy.start()
        return copy

    def finish(self):
        for copy in self.all:
            copy.wait_send()


class Scatter:
    def __init__(self, net, src, dst, targets, is_self, mine):
        self.net, self.src, self.dst, self.targets, self.is_self, self.mine = net, src, dst, targets, is_self, mine
        self.at = net.reserve(8)

    def remote(self, i):
        return self.net.make(
            self.src.at[i], self.dst.at[self.mine], self.targets[i], self.at + i, self.at + self.mine
        )

    def local(self, i):
        sem = self.net.recv_sems.at[self.at + self.mine]
        return pltpu.make_async_copy(self.src.at[i], self.dst.at[self.mine], sem)

    def start(self):
        for i in range(8):
            pl.when(jnp.logical_not(self.is_self[i]))(self.remote(i).start)
            pl.when(self.is_self[i])(self.local(i).start)

    def wait(self):
        for i in range(8):
            self.net.make(self.src.at[i], self.dst.at[i], self.targets[i], self.at + i, self.at + i).wait_recv()

    def wait_sent(self):
        for i in range(8):
            pl.when(jnp.logical_not(self.is_self[i]))(self.remote(i).wait_send)


def kernel(
    feats_ref, text_ref, proj_hbm, norms_ref, ids_column, ids_row, state_ref,
    weights_ref, sums_ref,
    proj, texts, images, raw_ref, acc, own_grad, weigh0, weigh1,
    send_up, send_down, recv_up, recv_down,
    feats_all, clipped, clipped_all, spread, x_send, x_recv, z_part, z_recv, z_tiles,
    state_recv, state_tile, sums_send, sq_send, sq_recv,
    proj_sem, send_sems, recv_sems,
):
    x, y, z, c = place()
    col = lax.axis_index("col")
    k = c * 4 + y
    other = 1 - c
    zl = lax.rem(z, 2)
    at_x = [device(shift(x, o, X), y, z, c) for o in range(1, X)]
    at_y = [device(x, shift(y, o, Y), z, c) for o in range(1, Y)]
    at_z = [device(x, y, shift(z, o, Z), c) for o in range(1, Z)]
    across = device(x, y, z, other)
    at_y_across = [device(x, shift(y, o, Y), z, other) for o in range(1, Y)]
    flip = z + 1 - 2 * zl
    at_flip = [device(x, shift(y, o, Y), flip, cc) for o in range(Y) for cc in (c, other)][1:]
    x_up, x_down, y_up, y_down, z_up, z_down = at_x[0], at_x[2], at_y[0], at_y[2], at_z[0], at_z[6]

    load = pltpu.make_async_copy(proj_hbm, proj, proj_sem)
    load.start()
    text = text_ref[...].astype(F32)
    texts[0:PAIRS, :] = (
        text * lax.rsqrt(jnp.sum(text * text, axis=1, keepdims=True) + EPSILON)
    ).astype(BF16)

    barrier = pltpu.get_barrier_semaphore()
    partners = at_x + at_y + at_z + [across] + at_y_across + at_flip
    for target in partners:
        pl.semaphore_signal(barrier, inc=1, device_id=target, device_id_type=MESH)
    pl.semaphore_wait(barrier, len(partners))
    net = Copies(send_sems, recv_sems)

    def lanes(index, width=128):
        return pl.ds(pl.multiple_of(index * width, width), width)

    def slot(rx, ry, rows, core=0):
        base = (core * 16 + rx * 4 + ry) * PAIRS
        return texts.at[base + rows[0]:base + rows[1], :]

    def hop(axis, up, rx, ry, rows):
        step = 3 if up else 1
        if axis == "x":
            return net.plan(slot(rx, ry, rows), slot((rx + step) % 4, ry, rows), x_up if up else x_down)
        return net.plan(slot(rx, ry, rows), slot(rx, (ry + step) % 4, rows), y_up if up else y_down)

    crossings = []

    def cross(rx, ry, rows):
        crossings.append(net.push(slot(rx, ry, rows), slot(rx, ry, rows, 1), across))

    class Half:
        def __init__(self, first, second, low):
            self.rows, self.swap = (low, low + 64), first == "y"
            self.parts = ((low, low + 32), (low + 32, low + 64))
            r, p = self.rows, self.parts
            self.first = [hop(first, up, 0, 0, r) for up in (True, False)]
            self.relay = [hop(first, up, *self.at(3 if up else 1, 0), p[0 if up else 1]) for up in (True, False)]
            self.second = [[hop(second, up, *self.at(a, 0), r) for up in (True, False)] for a in range(4)]
            self.last = [
                [hop(second, up, *self.at(a, 3 if up else 1), p[0 if up else 1]) for up in (True, False)]
                for a in range(4)
            ]

        def at(self, a, b):
            return (b, a) if self.swap else (a, b)

        def open(self, a):
            for copy in self.second[a]:
                copy.start()

        def got_first(self, i):
            a = (3, 1)[i]
            self.first[i].wait_recv()
            self.relay[i].start()
            self.open(a)
            cross(*self.at(a, 0), self.rows)

        def got_relay(self):
            for copy in self.relay:
                copy.wait_recv()
            self.open(2)
            cross(*self.at(2, 0), self.rows)

        def got_second(self, a):
            for i in range(2):
                self.second[a][i].wait_recv()
                self.last[a][i].start()
                cross(*self.at(a, (3, 1)[i]), self.rows)

        def got_last(self, a):
            for copy in self.last[a]:
                copy.wait_recv()
            cross(*self.at(a, 2), self.rows)

    low, high = Half("x", "y", 0), Half("y", "x", 64)
    halves = (low, high)
    for half in halves:
        for copy in half.first:
            copy.start()
    for half in halves:
        half.open(0)
    cross(0, 0, (0, PAIRS))

    load.wait()
    raw = jnp.dot(feats_ref[...], proj[...], preferred_element_type=F32)
    raw_ref[...] = raw
    inverse = lax.rsqrt(jnp.sum(raw * raw, axis=1, keepdims=True) + EPSILON)

    def image(index, rows=(0, PAIRS)):
        return images.at[index * PAIRS + rows[0]:index * PAIRS + rows[1], :]

    images[PAIRS:2 * PAIRS, :] = (raw * inverse).astype(BF16)
    up = [net.plan(image(a), image(b), z_up) for a, b in ((1, 7), (7, 5), (5, 3))]
    down = [net.plan(image(a), image(b), z_down) for a, b in ((1, 6), (6, 4), (4, 2))]
    up.append(net.plan(image(3, (0, 64)), image(0, (0, 64)), z_up))
    down.append(net.plan(image(2, (64, 128)), image(0, (64, 128)), z_down))
    up[0].start()
    down[0].start()

    def turn(step):
        for ring in (up, down):
            ring[step].wait_recv()
            if step < 3:
                ring[step + 1].start()

    owner_slot = (lax.rem(y, 2) * 2 + zl) * 2 + c
    zh2 = z - zl
    half_y = lax.div(y, 2)
    state_out = Scatter(
        net, state_ref, state_recv,
        [device(x, i % 4, zh2 + half_y, i // 4) for i in range(8)],
        [jnp.logical_and(zl == half_y, k == i) for i in range(8)],
        owner_slot,
    )

    for half in halves:
        half.got_first(0)
        half.got_first(1)
    for half in halves:
        half.got_second(0)
    turn(0)
    for half in halves:
        half.got_relay()
    for half in halves:
        half.got_last(0)
    for a in (3, 1):
        for half in halves:
            half.got_second(a)
    turn(1)
    for half in halves:
        half.got_second(2)
    for a in (3, 1):
        for half in halves:
            half.got_last(a)
    turn(2)
    for half in halves:
        half.got_last(2)
    turn(3)
    for copy in crossings:
        copy.wait_recv()

    def feats_slot(ry, rows=(0, W)):
        return feats_all.at[rows[0]:rows[1], ry * PAIRS:(ry + 1) * PAIRS]

    feats_all[:, 0:PAIRS] = feats_ref[...].T
    feats_near = [net.plan(feats_slot(0), feats_slot(3), y_up), net.plan(feats_slot(0), feats_slot(1), y_down)]
    feats_far = [
        net.plan(feats_slot(3, (0, W // 2)), feats_slot(2, (0, W // 2)), y_up),
        net.plan(feats_slot(1, (W // 2, W)), feats_slot(2, (W // 2, W)), y_down),
    ]
    feats_cross = net.plan(feats_all.at[:, 0:512], feats_all.at[:, 512:1024], across)
    for copy in feats_near:
        copy.start()
    state_out.start()

    grads_up = [net.plan(send_up.at[0, 0:64], recv_up.at[0, 0:64], z_up)]
    grads_down = [net.plan(send_down.at[0, 0:64], recv_down.at[0, 0:64], z_down)]
    for i in range(1, 4):
        grads_up.append(net.plan(send_up.at[i], recv_up.at[i], z_up))
        grads_down.append(net.plan(send_down.at[i], recv_down.at[i], z_down))

    def pack(dst, full, unit):
        along = jnp.sum(full * unit, axis=1, keepdims=True).astype(BF16).astype(F32)
        dst[:, 0:E] = (full - along * unit).astype(BF16)
        dst[:, E:SLOT] = jnp.broadcast_to(along, (full.shape[0], 128)).astype(BF16)

    def unpack(src, unit):
        return src[:, 0:E].astype(F32) + src[:, E:SLOT].astype(F32)[:, 0:1] * unit

    def grid_step(step, carry):
        rows = pl.ds(pl.multiple_of(step * IMAGES, IMAGES), IMAGES)

        def chunk(n):
            return texts[pl.ds(pl.multiple_of(n * CHUNK, CHUNK), CHUNK), :]

        def weigh(n):
            cosine = lax.dot_general(
                images[rows, :], chunk(n), (((1,), (1,)), ((), ())), preferred_element_type=F32
            )
            return (0.5 + 0.5 * jnp.tanh(0.5 * LOGIT_SCALE * cosine + 0.5 * LOGIT_BIAS)).astype(BF16)

        def fold(weights, n):
            acc[...] += jnp.dot(weights[...], chunk(n), preferred_element_type=F32)

        weigh0[...] = weigh(0)
        acc[...] = jnp.zeros_like(acc)

        def two(h, carry):
            weigh1[...] = weigh(2 * h + 1)
            fold(weigh0, 2 * h)
            weigh0[...] = weigh(2 * h + 2)
            fold(weigh1, 2 * h + 1)
            return carry

        last = TEXTS // CHUNK - 1
        lax.fori_loop(0, last // 2, two, 0)
        weigh1[...] = weigh(last)
        fold(weigh0, last - 1)
        fold(weigh1, last)

        @pl.when(step == 0)
        def _():
            far = LOGIT_SCALE * acc[0:PAIRS, :]
            unit = images[0:PAIRS, :].astype(F32)
            pack(send_up.at[0, 0:64], far[0:64], unit[0:64])
            pack(send_down.at[0, 0:64], far[64:128], unit[64:128])
            grads_up[0].start()
            grads_down[0].start()
            unit = images[PAIRS:2 * PAIRS, :].astype(F32)
            text = texts[0:PAIRS, :].astype(F32)
            cosine = jnp.sum(unit * text, axis=1, keepdims=True)
            sigmoid = 0.5 + 0.5 * jnp.tanh(0.5 * LOGIT_SCALE * cosine + 0.5 * LOGIT_BIAS)
            change = (sigmoid - 1.0).astype(BF16).astype(F32) - sigmoid.astype(BF16).astype(F32)
            own_grad[...] = LOGIT_SCALE * (acc[PAIRS:2 * PAIRS, :] + change * text)
            for near, far_copy in zip(feats_near, feats_far):
                near.wait_recv()
                far_copy.start()

        for at in range(1, 4):

            @pl.when(step == at)
            def _(at=at):
                for side, sends, recvs, grads in (
                    (0, send_up, recv_up, grads_up), (1, send_down, recv_down, grads_down)
                ):
                    grads[at - 1].wait_recv()
                    first = (2 * at + side) * PAIRS
                    full = LOGIT_SCALE * acc[side * PAIRS:(side + 1) * PAIRS, :]
                    unit = images[first:first + PAIRS, :].astype(F32)
                    if at > 1:
                        pack(sends.at[at], full + unpack(recvs.at[at - 1], unit), unit)
                    else:
                        come = slice(64 * side, 64 * side + 64)
                        kept = slice(64 - 64 * side, 128 - 64 * side)
                        both = full[come] + unpack(recvs.at[0, 0:64], unit[come])
                        pack(sends.at[at, come], both, unit[come])
                        pack(sends.at[at, kept], full[kept], unit[kept])
                    grads[at].start()
                if at == 1:
                    for copy in feats_far:
                        copy.wait_recv()
                    feats_cross.start()

        return carry

    lax.fori_loop(0, 4, grid_step, 0)

    state_out.wait()
    state_tile[...] = jnp.zeros_like(state_tile)
    for piece in range(8):
        first = 11 * (piece // 2) + 5 * (piece % 2)
        for a in range(3):
            state_tile[a, first:first + 6, :] += state_recv[piece, a, 0:6, :]

    raw = raw_ref[...]
    inverse = lax.rsqrt(jnp.sum(raw * raw, axis=1, keepdims=True) + EPSILON)
    feat_gram = lax.dot_general(
        feats_ref[...], feats_ref[...], (((1,), (1,)), ((), ())), preferred_element_type=F32
    )
    same_user = ids_column[...] == ids_row[...]
    first_user = (lax.axis_index("row") * 16 + col) * USERS
    one_hot = (ids_column[...] - first_user) == lax.broadcasted_iota(jnp.int32, (PAIRS, USERS), 1)
    bound = jnp.sum(jnp.where(one_hot, norms_ref[...], 0.0), axis=1, keepdims=True)
    unit = images[PAIRS:2 * PAIRS, :].astype(F32)
    grads_up[3].wait_recv()
    grads_down[3].wait_recv()
    unit_grad = own_grad[...] + unpack(recv_up.at[3], unit) + unpack(recv_down.at[3], unit)
    inner = jnp.sum(raw * unit_grad, axis=1, keepdims=True)
    embed_grad = inverse * unit_grad - inverse * inverse * inverse * raw * inner
    grad_gram = lax.dot_general(
        embed_grad, embed_grad, (((1,), (1,)), ((), ())),
        precision=lax.Precision.HIGHEST, preferred_element_type=F32,
    )
    terms = jnp.sum(jnp.where(same_user, feat_gram * grad_gram, 0.0), axis=0, keepdims=True)
    user_sq = jnp.sum(jnp.where(same_user, terms, 0.0), axis=1, keepdims=True)
    factor = bound / jnp.maximum(jnp.sqrt(user_sq), bound)
    clipped[...] = (factor * embed_grad).astype(BF16)

    def rows_of(core, ry):
        return clipped_all.at[(core * 4 + ry) * PAIRS:(core * 4 + ry + 1) * PAIRS, :]

    parts = []
    for o in range(1, Y):
        parts.append(net.push(clipped.at[:, lanes(c * 4 + shift(y, o, Y))], rows_of(0, 4 - o), at_y[o - 1]))
        parts.append(net.push(clipped.at[:, lanes(other * 4 + shift(y, o, Y))], rows_of(1, 4 - o), at_y_across[o - 1]))
    parts.append(net.push(clipped.at[:, lanes(other * 4 + y)], rows_of(1, 0), across))
    clipped_all[0:PAIRS, :] = clipped[:, lanes(k)]
    spread[...] = jnp.zeros_like(spread)
    feats_cross.wait_recv()
    for copy in parts:
        copy.wait_recv()

    def share(index):
        block = feats_all[pl.ds(pl.multiple_of(index * SHARE, 16), SHARE), :]
        part = jnp.dot(block, clipped_all[...], preferred_element_type=F32)
        for piece in range(Z):
            spread[piece * PADDED:piece * PADDED + BLOCK, :] = part[piece * BLOCK:(piece + 1) * BLOCK]
        return spread[...]

    moves = []
    for o in range(1, X):
        x_send[o - 1] = share(shift(x, o, X)).astype(BF16)
        moves.append(net.push(x_send.at[o - 1], x_recv.at[o - 1], at_x[o - 1]))
    total = share(x)
    for o in range(1, X):
        moves[o - 1].wait_recv()
        total = total + x_recv[o - 1].astype(F32)
    z_part[...] = total

    def rows(index):
        return pl.ds(pl.multiple_of(index * PADDED, 16), PADDED)

    moves = [
        net.push(z_part.at[rows(shift(z, o, Z)), :], z_recv.at[o - 1], at_z[o - 1])
        for o in range(1, Z)
    ]
    grad = z_part[rows(z), :]
    for o in range(1, Z):
        moves[o - 1].wait_recv()
        grad = grad + z_recv[o - 1]

    new_sum = state_tile[0] + grad
    update = new_sum + state_tile[1]
    for piece in range(8):
        first = 11 * (piece // 2) + 5 * (piece % 2)
        sums_send[piece] = new_sum[first:first + 8]

    square = jnp.sum((update * update).reshape(PADDED // 8, 8, 128), axis=0)
    at = 0
    for stage, targets in enumerate((at_z, at_x, at_y + [across] + at_y_across)):
        sq_send[stage] = square
        moves = [
            net.push(sq_send.at[stage], sq_recv.at[at + i], target)
            for i, target in enumerate(targets)
        ]
        for i, copy in enumerate(moves):
            copy.wait_recv()
            square = square + sq_recv[at + i]
        at += len(targets)
    norm = jnp.sqrt(jnp.sum(square, keepdims=True))
    cap = math.sqrt(W * E)
    shrink = cap / jnp.maximum(norm, cap)
    tile = (state_tile[2] - RATE * shrink * update).astype(BF16)

    z_tiles[rows(z), :] = tile
    moves = [net.push(z_tiles.at[rows(z), :], z_tiles.at[rows(z), :], target) for target in at_z]
    sums_out = Scatter(
        net, sums_send, sums_ref,
        [device(x, 2 * zl + i // 4, zh2 + (i // 2) % 2, i % 2) for i in range(8)],
        [
            jnp.logical_and(half_y == zl, owner_slot == i) for i in range(8)
        ],
        k,
    )
    sums_out.start()
    for copy in moves:
        copy.wait_recv()
    whole = z_tiles[...].astype(F32)
    whole = jnp.concatenate([whole[piece * PADDED:piece * PADDED + BLOCK] for piece in range(Z)], axis=0)
    share_rows = pl.ds(pl.multiple_of(x * SHARE, 16), SHARE)
    weights_ref[share_rows, lanes(k)] = whole.astype(BF16)

    half_rows = SHARE // 2

    def part_rows(index, upper):
        return pl.ds(pl.multiple_of(index * SHARE + upper * half_rows, 16), half_rows)

    first = weights_ref.at[part_rows(x, 0), lanes(k)]
    second = weights_ref.at[part_rows(x, 1), lanes(k)]
    moves_y = [net.push(first, first, target) for target in at_y]
    moves_x = [net.push(second, second, target) for target in at_x]
    for copy in moves_y:
        copy.wait_recv()
    first = weights_ref.at[part_rows(x, 0), lanes(c, 512)]
    moves = [net.push(first, first, target) for target in at_x + [across]]
    for copy in moves_x:
        copy.wait_recv()
    for o in range(X):
        second = weights_ref.at[part_rows(shift(x, o, X), 1), lanes(k)]
        moves += [net.push(second, second, target) for target in at_y + [across]]
    for copy in moves:
        copy.wait_recv()
    last = []
    for o in range(1, X):
        piece = weights_ref.at[part_rows(shift(x, o, X), 0), lanes(c, 512)]
        last.append(net.push(piece, piece, across))
    for o in range(1, Y):
        for a in range(X):
            piece = weights_ref.at[part_rows(shift(x, a, X), 1), lanes(c * 4 + shift(y, o, Y))]
            last.append(net.push(piece, piece, across))
    for copy in last:
        copy.wait_recv()
    sums_out.wait()
    state_out.wait_sent()
    sums_out.wait_sent()
    net.finish()


def body(
    image_feats, text_emb, projection, clip_norms, user_ids, grad_sum, init_weights, tree_noise
):
    c = lax.rem(lax.axis_index("col"), 2)
    state = jnp.pad(jnp.stack([grad_sum, tree_noise, init_weights]), ((0, 0), (4, 4), (0, 0)))
    state = lax.dynamic_slice(state, (0, 4 - 4 * c, 0), (3, 48, 128))
    state = state.reshape(3, 6, 8, 128).transpose(2, 0, 1, 3)
    state = jnp.pad(state, ((0, 0), (0, 0), (0, 2), (0, 0)))
    vmem = pl.BlockSpec(memory_space=pltpu.VMEM)
    weights, sums = pl.pallas_call(
        kernel,
        out_shape=(
            jax.ShapeDtypeStruct((W, E), BF16),
            jax.ShapeDtypeStruct((8, 8, 128), F32),
        ),
        in_specs=[vmem, vmem, pl.BlockSpec(memory_space=pl.ANY), vmem, vmem, vmem, vmem],
        out_specs=(vmem, vmem),
        scratch_shapes=[
            pltpu.VMEM((W, E), BF16),
            pltpu.VMEM((TEXTS, E), BF16),
            pltpu.VMEM((Z * PAIRS, E), BF16),
            pltpu.VMEM((PAIRS, E), F32),
            pltpu.VMEM((IMAGES, E), F32),
            pltpu.VMEM((PAIRS, E), F32),
            pltpu.VMEM((IMAGES, CHUNK), BF16),
            pltpu.VMEM((IMAGES, CHUNK), BF16),
            pltpu.VMEM((4, PAIRS, SLOT), BF16),
            pltpu.VMEM((4, PAIRS, SLOT), BF16),
            pltpu.VMEM((4, PAIRS, SLOT), BF16),
            pltpu.VMEM((4, PAIRS, SLOT), BF16),
            pltpu.VMEM((W, 8 * PAIRS), BF16),
            pltpu.VMEM((PAIRS, E), BF16),
            pltpu.VMEM((8 * PAIRS, 128), BF16),
            pltpu.VMEM((WIDE, 128), F32),
            pltpu.VMEM((X - 1, WIDE, 128), BF16),
            pltpu.VMEM((X - 1, WIDE, 128), BF16),
            pltpu.VMEM((WIDE, 128), F32),
            pltpu.VMEM((Z - 1, PADDED, 128), F32),
            pltpu.VMEM((WIDE, 128), BF16),
            pltpu.VMEM((8, 3, 8, 128), F32),
            pltpu.VMEM((3, PADDED, 128), F32),
            pltpu.VMEM((8, 8, 128), F32),
            pltpu.VMEM((3, 8, 128), F32),
            pltpu.VMEM((17, 8, 128), F32),
            pltpu.SemaphoreType.DMA,
            pltpu.SemaphoreType.DMA((COPIES,)),
            pltpu.SemaphoreType.DMA((COPIES,)),
        ],
        compiler_params=pltpu.CompilerParams(
            collective_id=1, has_side_effects=True, vmem_limit_bytes=48 * 1024 * 1024
        ),
    )(
        image_feats, text_emb, projection, clip_norms.reshape(1, USERS),
        user_ids.reshape(PAIRS, 1), user_ids.reshape(1, PAIRS), state,
    )
    sums = sums[:, :6].transpose(1, 0, 2).reshape(48, 128)
    return weights, lax.dynamic_slice(sums, (4 * c, 0), (44, 128))


def solution(mesh):
    in_specs = (
        P(("row", "col"), None),
        P(("row", "col"), None),
        P(),
        P(("row", "col")),
        P(("row", "col")),
        P(("row", "col"), None),
        P(("row", "col"), None),
        P(("row", "col"), None),
    )
    out_specs = (P(), P(("row", "col"), None))
    return jax.shard_map(body, mesh=mesh, in_specs=in_specs, out_specs=out_specs, check_vma=False)
```

```python
import math

import jax
import jax.numpy as jnp
from jax import lax
from jax.experimental import pallas as pl
from jax.experimental.pallas import tpu as pltpu
from jax.sharding import PartitionSpec as P

LOGIT_SCALE = 32.0
LOGIT_BIAS = -5.0
RATE = 0.5
EPSILON = 1e-06

MESH = pl.DeviceIdType.MESH
X, Y, Z = 4, 4, 8
W, E, PAIRS, USERS = 1408, 1024, 128, 16
SHARE = W // X
BLOCK = SHARE // Z
PADDED = 48
WIDE = Z * PADDED
TEXTS = 2 * X * Y * PAIRS
CHUNK = 2048
IMAGES = 2 * PAIRS
SLOT = E + 128
COPIES = 240
F32, BF16 = jnp.float32, jnp.bfloat16


def place():
    row, col = lax.axis_index("row"), lax.axis_index("col")
    x, zh = lax.div(row, 4), lax.rem(row, 4)
    y, zl, c = lax.div(col, 4), lax.rem(lax.div(col, 2), 2), lax.rem(col, 2)
    return x, y, zh * 2 + zl, c


def device(x, y, z, c):
    return (x * 4 + lax.div(z, 2), y * 4 + lax.rem(z, 2) * 2 + c)


def shift(value, by, size):
    return lax.rem(value + by, size)


class Copies:
    def __init__(self, send_sems, recv_sems):
        self.send_sems, self.recv_sems, self.used, self.all = send_sems, recv_sems, 0, []

    def reserve(self, count):
        self.used += count
        return self.used - count

    def make(self, src, dst, target, send_at, recv_at):
        return pltpu.make_async_remote_copy(
            src_ref=src,
            dst_ref=dst,
            send_sem=self.send_sems.at[send_at],
            recv_sem=self.recv_sems.at[recv_at],
            device_id=target,
            device_id_type=MESH,
        )

    def plan(self, src, dst, target):
        at = self.reserve(1)
        copy = self.make(src, dst, target, at, at)
        self.all.append(copy)
        return copy

    def push(self, src, dst, target):
        copy = self.plan(src, dst, target)
        copy.start()
        return copy

    def finish(self):
        for copy in self.all:
            copy.wait_send()


class Scatter:
    def __init__(self, net, src, dst, targets, is_self, mine):
        self.net, self.src, self.dst, self.targets, self.is_self, self.mine = net, src, dst, targets, is_self, mine
        self.at = net.reserve(8)

    def remote(self, i):
        return self.net.make(
            self.src.at[i], self.dst.at[self.mine], self.targets[i], self.at + i, self.at + self.mine
        )

    def local(self, i):
        sem = self.net.recv_sems.at[self.at + self.mine]
        return pltpu.make_async_copy(self.src.at[i], self.dst.at[self.mine], sem)

    def start(self):
        for i in range(8):
            pl.when(jnp.logical_not(self.is_self[i]))(self.remote(i).start)
            pl.when(self.is_self[i])(self.local(i).start)

    def wait(self):
        for i in range(8):
            self.net.make(self.src.at[i], self.dst.at[i], self.targets[i], self.at + i, self.at + i).wait_recv()

    def wait_sent(self):
        for i in range(8):
            pl.when(jnp.logical_not(self.is_self[i]))(self.remote(i).wait_send)


def kernel(
    feats_hbm, text_hbm, proj_hbm, norms_hbm, ids_hbm, state_hbm,
    weights_ref, sums_ref,
    feats_ref, text_ref, norms_ref, ids_row, state_ref, proj, texts, images, raw_ref, acc, own_grad, weigh0, weigh1,
    send_up, send_down, recv_up, recv_down,
    feats_all, clipped, clipped_all, spread, x_send, x_recv, z_part, z_recv, z_tiles,
    state_recv, state_tile, sums_send, sq_send, sq_recv,
    load_sems, send_sems, recv_sems,
):
    x, y, z, c = place()
    col = lax.axis_index("col")
    k = c * 4 + y
    other = 1 - c
    zl = lax.rem(z, 2)
    at_x = [device(shift(x, o, X), y, z, c) for o in range(1, X)]
    at_y = [device(x, shift(y, o, Y), z, c) for o in range(1, Y)]
    at_z = [device(x, y, shift(z, o, Z), c) for o in range(1, Z)]
    across = device(x, y, z, other)
    at_y_across = [device(x, shift(y, o, Y), z, other) for o in range(1, Y)]
    flip = z + 1 - 2 * zl
    at_flip = [device(x, shift(y, o, Y), flip, cc) for o in range(Y) for cc in (c, other)][1:]
    x_up, x_down, y_up, y_down, z_up, z_down = at_x[0], at_x[2], at_y[0], at_y[2], at_z[0], at_z[6]

    loads = [
        pltpu.make_async_copy(src, dst, load_sems.at[i])
        for i, (src, dst) in enumerate((
            (text_hbm, text_ref), (feats_hbm, feats_ref), (proj_hbm, proj),
            (state_hbm, state_ref), (norms_hbm, norms_ref), (ids_hbm, ids_row),
        ))
    ]
    for load in loads:
        load.start()
    loads[0].wait()
    text = text_ref[...].astype(F32)
    texts[0:PAIRS, :] = (
        text * lax.rsqrt(jnp.sum(text * text, axis=1, keepdims=True) + EPSILON)
    ).astype(BF16)

    barrier = pltpu.get_barrier_semaphore()
    partners = at_x + at_y + at_z + [across] + at_y_across + at_flip
    for target in partners:
        pl.semaphore_signal(barrier, inc=1, device_id=target, device_id_type=MESH)
    pl.semaphore_wait(barrier, len(partners))
    net = Copies(send_sems, recv_sems)

    def lanes(index, width=128):
        return pl.ds(pl.multiple_of(index * width, width), width)

    def slot(rx, ry, rows, core=0):
        base = (core * 16 + rx * 4 + ry) * PAIRS
        return texts.at[base + rows[0]:base + rows[1], :]

    def hop(axis, up, rx, ry, rows):
        step = 3 if up else 1
        if axis == "x":
            return net.plan(slot(rx, ry, rows), slot((rx + step) % 4, ry, rows), x_up if up else x_down)
        return net.plan(slot(rx, ry, rows), slot(rx, (ry + step) % 4, rows), y_up if up else y_down)

    crossings = []

    def cross(rx, ry, rows):
        crossings.append(net.push(slot(rx, ry, rows), slot(rx, ry, rows, 1), across))

    class Half:
        def __init__(self, first, second, low):
            self.rows, self.swap = (low, low + 64), first == "y"
            self.parts = ((low, low + 32), (low + 32, low + 64))
            r, p = self.rows, self.parts
            self.first = [hop(first, up, 0, 0, r) for up in (True, False)]
            self.relay = [hop(first, up, *self.at(3 if up else 1, 0), p[0 if up else 1]) for up in (True, False)]
            self.second = [[hop(second, up, *self.at(a, 0), r) for up in (True, False)] for a in range(4)]
            self.last = [
                [hop(second, up, *self.at(a, 3 if up else 1), p[0 if up else 1]) for up in (True, False)]
                for a in range(4)
            ]

        def at(self, a, b):
            return (b, a) if self.swap else (a, b)

        def open(self, a):
            for copy in self.second[a]:
                copy.start()

        def got_first(self, i):
            a = (3, 1)[i]
            self.first[i].wait_recv()
            self.relay[i].start()
            self.open(a)
            cross(*self.at(a, 0), self.rows)

        def got_relay(self):
            for copy in self.relay:
                copy.wait_recv()
            self.open(2)
            cross(*self.at(2, 0), self.rows)

        def got_second(self, a):
            for i in range(2):
                self.second[a][i].wait_recv()
                self.last[a][i].start()
                cross(*self.at(a, (3, 1)[i]), self.rows)

        def got_last(self, a):
            for copy in self.last[a]:
                copy.wait_recv()
            cross(*self.at(a, 2), self.rows)

    low, high = Half("x", "y", 0), Half("y", "x", 64)
    halves = (low, high)
    for half in halves:
        for copy in half.first:
            copy.start()
    for half in halves:
        half.open(0)
    cross(0, 0, (0, PAIRS))

    for load in loads[1:]:
        load.wait()
    raw = jnp.dot(feats_ref[...], proj[...], preferred_element_type=F32)
    raw_ref[...] = raw
    inverse = lax.rsqrt(jnp.sum(raw * raw, axis=1, keepdims=True) + EPSILON)

    def image(index, rows=(0, PAIRS)):
        return images.at[index * PAIRS + rows[0]:index * PAIRS + rows[1], :]

    images[PAIRS:2 * PAIRS, :] = (raw * inverse).astype(BF16)
    up = [net.plan(image(a), image(b), z_up) for a, b in ((1, 7), (7, 5), (5, 3))]
    down = [net.plan(image(a), image(b), z_down) for a, b in ((1, 6), (6, 4), (4, 2))]
    up.append(net.plan(image(3, (0, 64)), image(0, (0, 64)), z_up))
    down.append(net.plan(image(2, (64, 128)), image(0, (64, 128)), z_down))
    up[0].start()
    down[0].start()

    def turn(step):
        for ring in (up, down):
            ring[step].wait_recv()
            if step < 3:
                ring[step + 1].start()

    owner_slot = (lax.rem(y, 2) * 2 + zl) * 2 + c
    zh2 = z - zl
    half_y = lax.div(y, 2)
    state_out = Scatter(
        net, state_ref, state_recv,
        [device(x, i % 4, zh2 + half_y, i // 4) for i in range(8)],
        [jnp.logical_and(zl == half_y, k == i) for i in range(8)],
        owner_slot,
    )

    for half in halves:
        half.got_first(0)
        half.got_first(1)
    for half in halves:
        half.got_second(0)
    turn(0)
    for half in halves:
        half.got_relay()
    for half in halves:
        half.got_last(0)
    for a in (3, 1):
        for half in halves:
            half.got_second(a)
    turn(1)
    for half in halves:
        half.got_second(2)
    for a in (3, 1):
        for half in halves:
            half.got_last(a)
    turn(2)
    for half in halves:
        half.got_last(2)
    turn(3)
    for copy in crossings:
        copy.wait_recv()

    def feats_slot(ry, rows=(0, W)):
        return feats_all.at[rows[0]:rows[1], ry * PAIRS:(ry + 1) * PAIRS]

    feats_all[:, 0:PAIRS] = feats_ref[...].T
    feats_near = [net.plan(feats_slot(0), feats_slot(3), y_up), net.plan(feats_slot(0), feats_slot(1), y_down)]
    feats_far = [
        net.plan(feats_slot(3, (0, W // 2)), feats_slot(2, (0, W // 2)), y_up),
        net.plan(feats_slot(1, (W // 2, W)), feats_slot(2, (W // 2, W)), y_down),
    ]
    feats_cross = net.plan(feats_all.at[:, 0:512], feats_all.at[:, 512:1024], across)
    for copy in feats_near:
        copy.start()
    state_out.start()

    grads_up = [net.plan(send_up.at[0, 0:64], recv_up.at[0, 0:64], z_up)]
    grads_down = [net.plan(send_down.at[0, 0:64], recv_down.at[0, 0:64], z_down)]
    for i in range(1, 4):
        grads_up.append(net.plan(send_up.at[i], recv_up.at[i], z_up))
        grads_down.append(net.plan(send_down.at[i], recv_down.at[i], z_down))

    def pack(dst, full, unit):
        along = jnp.sum(full * unit, axis=1, keepdims=True).astype(BF16).astype(F32)
        dst[:, 0:E] = (full - along * unit).astype(BF16)
        dst[:, E:SLOT] = jnp.broadcast_to(along, (full.shape[0], 128)).astype(BF16)

    def unpack(src, unit):
        return src[:, 0:E].astype(F32) + src[:, E:SLOT].astype(F32)[:, 0:1] * unit

    def weigh(step, n):
        rows = slice(step * IMAGES, (step + 1) * IMAGES)
        cosine = lax.dot_general(
            images[rows, :], texts[pl.ds(pl.multiple_of(n * CHUNK, CHUNK), CHUNK), :],
            (((1,), (1,)), ((), ())), preferred_element_type=F32,
        )
        pair = 0.5 + 0.5 * jnp.tanh(0.5 * LOGIT_SCALE * cosine + 0.5 * LOGIT_BIAS)
        (weigh0, weigh1)[step % 2][:, lanes(n, CHUNK)] = pair.astype(BF16)

    def fold(step, n):
        acc[...] += jnp.dot(
            (weigh0, weigh1)[step % 2][:, lanes(n, CHUNK)],
            texts[pl.ds(pl.multiple_of(n * CHUNK, CHUNK), CHUNK), :],
            preferred_element_type=F32,
        )

    def first_weights(n, carry):
        weigh(0, n)
        return carry

    lax.fori_loop(0, TEXTS // CHUNK, first_weights, 0)
    for step in range(4):
        acc[...] = jnp.zeros_like(acc)

        def part(n, carry, step=step):
            if step < 3:
                weigh(step + 1, n)
            fold(step, n)
            return carry

        lax.fori_loop(0, TEXTS // CHUNK, part, 0)
        if step == 0:
            far = LOGIT_SCALE * acc[0:PAIRS, :]
            unit = images[0:PAIRS, :].astype(F32)
            pack(send_up.at[0, 0:64], far[0:64], unit[0:64])
            pack(send_down.at[0, 0:64], far[64:128], unit[64:128])
            grads_up[0].start()
            grads_down[0].start()
            unit = images[PAIRS:2 * PAIRS, :].astype(F32)
            text = texts[0:PAIRS, :].astype(F32)
            cosine = jnp.sum(unit * text, axis=1, keepdims=True)
            sigmoid = 0.5 + 0.5 * jnp.tanh(0.5 * LOGIT_SCALE * cosine + 0.5 * LOGIT_BIAS)
            change = (sigmoid - 1.0).astype(BF16).astype(F32) - sigmoid.astype(BF16).astype(F32)
            own_grad[...] = LOGIT_SCALE * (acc[PAIRS:2 * PAIRS, :] + change * text)
            for near, far_copy in zip(feats_near, feats_far):
                near.wait_recv()
                far_copy.start()
            continue
        for side, sends, recvs, grads in (
            (0, send_up, recv_up, grads_up), (1, send_down, recv_down, grads_down)
        ):
            grads[step - 1].wait_recv()
            first = (2 * step + side) * PAIRS
            full = LOGIT_SCALE * acc[side * PAIRS:(side + 1) * PAIRS, :]
            unit = images[first:first + PAIRS, :].astype(F32)
            if step > 1:
                pack(sends.at[step], full + unpack(recvs.at[step - 1], unit), unit)
            else:
                come = slice(64 * side, 64 * side + 64)
                kept = slice(64 - 64 * side, 128 - 64 * side)
                both = full[come] + unpack(recvs.at[0, 0:64], unit[come])
                pack(sends.at[step, come], both, unit[come])
                pack(sends.at[step, kept], full[kept], unit[kept])
            grads[step].start()
        if step == 1:
            for copy in feats_far:
                copy.wait_recv()
            feats_cross.start()

    state_out.wait()
    state_tile[...] = jnp.zeros_like(state_tile)
    for piece in range(8):
        first = 11 * (piece // 2) + 5 * (piece % 2)
        for a in range(3):
            state_tile[a, first:first + 6, :] += state_recv[piece, a, 0:6, :]

    raw = raw_ref[...]
    inverse = lax.rsqrt(jnp.sum(raw * raw, axis=1, keepdims=True) + EPSILON)
    feat_gram = lax.dot_general(
        feats_ref[...], feats_ref[...], (((1,), (1,)), ((), ())), preferred_element_type=F32
    )
    local_row = (ids_row[...] - (lax.axis_index("row") * 16 + col) * USERS).astype(F32)
    square_shape = (PAIRS, PAIRS)
    diagonal = lax.broadcasted_iota(jnp.int32, square_shape, 0) == lax.broadcasted_iota(
        jnp.int32, square_shape, 1
    )
    local_column = jnp.sum(jnp.where(diagonal, local_row, 0.0), axis=1, keepdims=True)
    same_user = local_column == local_row
    users = lax.broadcasted_iota(jnp.int32, (PAIRS, USERS), 1).astype(F32)
    bound = jnp.sum(jnp.where(local_column == users, norms_ref[...], 0.0), axis=1, keepdims=True)
    unit = images[PAIRS:2 * PAIRS, :].astype(F32)
    grads_up[3].wait_recv()
    grads_down[3].wait_recv()
    unit_grad = own_grad[...] + unpack(recv_up.at[3], unit) + unpack(recv_down.at[3], unit)
    inner = jnp.sum(raw * unit_grad, axis=1, keepdims=True)
    embed_grad = inverse * unit_grad - inverse * inverse * inverse * raw * inner
    grad_gram = lax.dot_general(
        embed_grad, embed_grad, (((1,), (1,)), ((), ())),
        precision=lax.Precision.HIGHEST, preferred_element_type=F32,
    )
    terms = jnp.sum(jnp.where(same_user, feat_gram * grad_gram, 0.0), axis=0, keepdims=True)
    user_sq = jnp.sum(jnp.where(same_user, terms, 0.0), axis=1, keepdims=True)
    factor = bound / jnp.maximum(jnp.sqrt(user_sq), bound)
    clipped[...] = (factor * embed_grad).astype(BF16)

    def rows_of(core, ry):
        return clipped_all.at[(core * 4 + ry) * PAIRS:(core * 4 + ry + 1) * PAIRS, :]

    parts = []
    for o in range(1, Y):
        parts.append(net.push(clipped.at[:, lanes(c * 4 + shift(y, o, Y))], rows_of(0, 4 - o), at_y[o - 1]))
        parts.append(net.push(clipped.at[:, lanes(other * 4 + shift(y, o, Y))], rows_of(1, 4 - o), at_y_across[o - 1]))
    parts.append(net.push(clipped.at[:, lanes(other * 4 + y)], rows_of(1, 0), across))
    clipped_all[0:PAIRS, :] = clipped[:, lanes(k)]
    spread[...] = jnp.zeros_like(spread)
    feats_cross.wait_recv()
    for copy in parts:
        copy.wait_recv()

    def share(index):
        block = feats_all[pl.ds(pl.multiple_of(index * SHARE, 16), SHARE), :]
        part = jnp.dot(block, clipped_all[...], preferred_element_type=F32)
        for piece in range(Z):
            spread[piece * PADDED:piece * PADDED + BLOCK, :] = part[piece * BLOCK:(piece + 1) * BLOCK]
        return spread[...]

    moves = []
    for o in range(1, X):
        x_send[o - 1] = share(shift(x, o, X)).astype(BF16)
        moves.append(net.push(x_send.at[o - 1], x_recv.at[o - 1], at_x[o - 1]))
    total = share(x)
    for o in range(1, X):
        moves[o - 1].wait_recv()
        total = total + x_recv[o - 1].astype(F32)
    z_part[...] = total

    def rows(index):
        return pl.ds(pl.multiple_of(index * PADDED, 16), PADDED)

    moves = [
        net.push(z_part.at[rows(shift(z, o, Z)), :], z_recv.at[o - 1], at_z[o - 1])
        for o in range(1, Z)
    ]
    grad = z_part[rows(z), :]
    for o in range(1, Z):
        moves[o - 1].wait_recv()
        grad = grad + z_recv[o - 1]

    new_sum = state_tile[0] + grad
    update = new_sum + state_tile[1]
    for piece in range(8):
        first = 11 * (piece // 2) + 5 * (piece % 2)
        sums_send[piece] = new_sum[first:first + 8]

    square = jnp.sum((update * update).reshape(PADDED // 8, 8, 128), axis=0)
    at = 0
    for stage, targets in enumerate((at_z, at_x, at_y + [across] + at_y_across)):
        sq_send[stage] = square
        moves = [
            net.push(sq_send.at[stage], sq_recv.at[at + i], target)
            for i, target in enumerate(targets)
        ]
        for i, copy in enumerate(moves):
            copy.wait_recv()
            square = square + sq_recv[at + i]
        at += len(targets)
    norm = jnp.sqrt(jnp.sum(square, keepdims=True))
    cap = math.sqrt(W * E)
    shrink = cap / jnp.maximum(norm, cap)
    tile = (state_tile[2] - RATE * shrink * update).astype(BF16)

    z_tiles[rows(z), :] = tile
    moves = [net.push(z_tiles.at[rows(z), :], z_tiles.at[rows(z), :], target) for target in at_z]
    sums_out = Scatter(
        net, sums_send, sums_ref,
        [device(x, 2 * zl + i // 4, zh2 + (i // 2) % 2, i % 2) for i in range(8)],
        [
            jnp.logical_and(half_y == zl, owner_slot == i) for i in range(8)
        ],
        k,
    )
    sums_out.start()
    for copy in moves:
        copy.wait_recv()
    whole = z_tiles[...].astype(F32)
    whole = jnp.concatenate([whole[piece * PADDED:piece * PADDED + BLOCK] for piece in range(Z)], axis=0)
    share_rows = pl.ds(pl.multiple_of(x * SHARE, 16), SHARE)
    weights_ref[share_rows, lanes(k)] = whole.astype(BF16)

    half_rows = SHARE // 2

    def part_rows(index, upper):
        return pl.ds(pl.multiple_of(index * SHARE + upper * half_rows, 16), half_rows)

    first = weights_ref.at[part_rows(x, 0), lanes(k)]
    second = weights_ref.at[part_rows(x, 1), lanes(k)]
    moves_y = [net.push(first, first, target) for target in at_y]
    moves_x = [net.push(second, second, target) for target in at_x]
    for copy in moves_y:
        copy.wait_recv()
    crossings = []

    def give(piece):
        crossings.append(net.push(piece, piece, across))

    def low_piece(index, rows=(0, half_rows)):
        start = pl.multiple_of(index * SHARE + rows[0], 16)
        return weights_ref.at[pl.ds(start, rows[1] - rows[0]), lanes(c, 512)]

    def high_piece(index, away):
        return weights_ref.at[part_rows(shift(x, index, X), 1), lanes(c * 4 + shift(y, away, Y))]

    low_moves = [net.push(low_piece(x), low_piece(x), target) for target in (x_up, x_down)]
    give(low_piece(x))
    for copy in moves_x:
        copy.wait_recv()
    high_moves = [
        [net.push(high_piece(a, 0), high_piece(a, 0), target) for a in range(X)]
        for target in (y_up, y_down)
    ]
    for a in range(X):
        give(high_piece(a, 0))
    low_relays, high_relays = [], []
    for copy, away, rows_sent, target in (
        (low_moves[0], 3, (0, 96), x_up), (low_moves[1], 1, (96, half_rows), x_down)
    ):
        copy.wait_recv()
        index = shift(x, away, X)
        low_relays.append(net.push(low_piece(index, rows_sent), low_piece(index, rows_sent), target))
        give(low_piece(index))
    for copies, away, sent, target in ((high_moves[0], 3, (0, 1), y_up), (high_moves[1], 1, (2, 3), y_down)):
        for copy in copies:
            copy.wait_recv()
        for a in sent:
            high_relays.append(net.push(high_piece(a, away), high_piece(a, away), target))
        for a in range(X):
            give(high_piece(a, away))
    for copy in low_relays:
        copy.wait_recv()
    give(low_piece(shift(x, 2, X)))
    for copy in high_relays:
        copy.wait_recv()
    for a in range(X):
        give(high_piece(a, 2))
    for copy in crossings:
        copy.wait_recv()
    sums_out.wait()
    state_out.wait_sent()
    sums_out.wait_sent()
    net.finish()


def body(
    image_feats, text_emb, projection, clip_norms, user_ids, grad_sum, init_weights, tree_noise
):
    c = lax.rem(lax.axis_index("col"), 2)
    state = jnp.pad(jnp.stack([grad_sum, tree_noise, init_weights]), ((0, 0), (4, 4), (0, 0)))
    state = lax.dynamic_slice(state, (0, 4 - 4 * c, 0), (3, 48, 128))
    state = state.reshape(3, 6, 8, 128).transpose(2, 0, 1, 3)
    state = jnp.pad(state, ((0, 0), (0, 0), (0, 2), (0, 0)))
    vmem = pl.BlockSpec(memory_space=pltpu.VMEM)
    weights, sums = pl.pallas_call(
        kernel,
        out_shape=(
            jax.ShapeDtypeStruct((W, E), BF16),
            jax.ShapeDtypeStruct((8, 8, 128), F32),
        ),
        in_specs=[pl.BlockSpec(memory_space=pl.ANY)] * 6,
        out_specs=(vmem, vmem),
        scratch_shapes=[
            pltpu.VMEM((PAIRS, W), BF16),
            pltpu.VMEM((PAIRS, E), BF16),
            pltpu.VMEM((1, USERS), F32),
            pltpu.VMEM((1, PAIRS), jnp.int32),
            pltpu.VMEM((8, 3, 8, 128), F32),
            pltpu.VMEM((W, E), BF16),
            pltpu.VMEM((TEXTS, E), BF16),
            pltpu.VMEM((Z * PAIRS, E), BF16),
            pltpu.VMEM((PAIRS, E), F32),
            pltpu.VMEM((IMAGES, E), F32),
            pltpu.VMEM((PAIRS, E), F32),
            pltpu.VMEM((IMAGES, TEXTS), BF16),
            pltpu.VMEM((IMAGES, TEXTS), BF16),
            pltpu.VMEM((4, PAIRS, SLOT), BF16),
            pltpu.VMEM((4, PAIRS, SLOT), BF16),
            pltpu.VMEM((4, PAIRS, SLOT), BF16),
            pltpu.VMEM((4, PAIRS, SLOT), BF16),
            pltpu.VMEM((W, 8 * PAIRS), BF16),
            pltpu.VMEM((PAIRS, E), BF16),
            pltpu.VMEM((8 * PAIRS, 128), BF16),
            pltpu.VMEM((WIDE, 128), F32),
            pltpu.VMEM((X - 1, WIDE, 128), BF16),
            pltpu.VMEM((X - 1, WIDE, 128), BF16),
            pltpu.VMEM((WIDE, 128), F32),
            pltpu.VMEM((Z - 1, PADDED, 128), F32),
            pltpu.VMEM((WIDE, 128), BF16),
            pltpu.VMEM((8, 3, 8, 128), F32),
            pltpu.VMEM((3, PADDED, 128), F32),
            pltpu.VMEM((8, 8, 128), F32),
            pltpu.VMEM((3, 8, 128), F32),
            pltpu.VMEM((17, 8, 128), F32),
            pltpu.SemaphoreType.DMA((6,)),
            pltpu.SemaphoreType.DMA((COPIES,)),
            pltpu.SemaphoreType.DMA((COPIES,)),
        ],
        compiler_params=pltpu.CompilerParams(
            collective_id=1, has_side_effects=True, vmem_limit_bytes=48 * 1024 * 1024
        ),
    )(
        image_feats, text_emb, projection, clip_norms.reshape(1, USERS),
        user_ids.reshape(1, PAIRS), state,
    )
    sums = sums[:, :6].transpose(1, 0, 2).reshape(48, 128)
    return weights, lax.dynamic_slice(sums, (4 * c, 0), (44, 128))


def solution(mesh):
    in_specs = (
        P(("row", "col"), None),
        P(("row", "col"), None),
        P(),
        P(("row", "col")),
        P(("row", "col")),
        P(("row", "col"), None),
        P(("row", "col"), None),
        P(("row", "col"), None),
    )
    out_specs = (P(), P(("row", "col"), None))
    return jax.shard_map(body, mesh=mesh, in_specs=in_specs, out_specs=out_specs, check_vma=False)
```

```python
import math

import jax
import jax.numpy as jnp
from jax import lax
from jax.experimental import pallas as pl
from jax.experimental.pallas import tpu as pltpu
from jax.sharding import PartitionSpec as P

LOGIT_SCALE = 32.0
LOGIT_BIAS = -5.0
RATE = 0.5
EPSILON = 1e-06
LOG2_E = math.log2(math.e)

MESH = pl.DeviceIdType.MESH
X, Y, Z = 4, 4, 8
W, E, PAIRS, USERS = 1408, 1024, 128, 16
SHARE = W // X
BLOCK = SHARE // Z
PADDED = 48
WIDE = Z * PADDED
TEXTS = 2 * X * Y * PAIRS
CHUNK = 512
IMAGES = 4 * PAIRS
SLOT = E + 128
COPIES = 240
F32, BF16 = jnp.float32, jnp.bfloat16


def place():
    row, col = lax.axis_index("row"), lax.axis_index("col")
    x, zh = lax.div(row, 4), lax.rem(row, 4)
    y, zl, c = lax.div(col, 4), lax.rem(lax.div(col, 2), 2), lax.rem(col, 2)
    return x, y, zh * 2 + zl, c


def sigmoid_of(cosine):
    power = cosine * (-LOGIT_SCALE * LOG2_E) + (-LOGIT_BIAS * LOG2_E)
    return pl.reciprocal(1.0 + jnp.exp2(power), approx=True)


def device(x, y, z, c):
    return (x * 4 + lax.div(z, 2), y * 4 + lax.rem(z, 2) * 2 + c)


def shift(value, by, size):
    return lax.rem(value + by, size)


class Copies:
    def __init__(self, send_sems, recv_sems):
        self.send_sems, self.recv_sems, self.used, self.all = send_sems, recv_sems, 0, []

    def reserve(self, count):
        self.used += count
        return self.used - count

    def make(self, src, dst, target, send_at, recv_at):
        return pltpu.make_async_remote_copy(
            src_ref=src,
            dst_ref=dst,
            send_sem=self.send_sems.at[send_at],
            recv_sem=self.recv_sems.at[recv_at],
            device_id=target,
            device_id_type=MESH,
        )

    def plan(self, src, dst, target):
        at = self.reserve(1)
        copy = self.make(src, dst, target, at, at)
        self.all.append(copy)
        return copy

    def push(self, src, dst, target):
        copy = self.plan(src, dst, target)
        copy.start()
        return copy

    def finish(self):
        for copy in self.all:
            copy.wait_send()


class Scatter:
    def __init__(self, net, src, dst, targets, is_self, mine):
        self.net, self.src, self.dst, self.targets, self.is_self, self.mine = net, src, dst, targets, is_self, mine
        self.at = net.reserve(8)

    def remote(self, i):
        return self.net.make(
            self.src.at[i], self.dst.at[self.mine], self.targets[i], self.at + i, self.at + self.mine
        )

    def local(self, i):
        sem = self.net.recv_sems.at[self.at + self.mine]
        return pltpu.make_async_copy(self.src.at[i], self.dst.at[self.mine], sem)

    def start(self):
        for i in range(8):
            pl.when(jnp.logical_not(self.is_self[i]))(self.remote(i).start)
            pl.when(self.is_self[i])(self.local(i).start)

    def wait(self):
        for i in range(8):
            self.net.make(self.src.at[i], self.dst.at[i], self.targets[i], self.at + i, self.at + i).wait_recv()

    def wait_sent(self):
        for i in range(8):
            pl.when(jnp.logical_not(self.is_self[i]))(self.remote(i).wait_send)


def kernel(
    feats_hbm, text_hbm, proj_hbm, norms_hbm, ids_hbm, state_hbm,
    weights_ref, sums_ref,
    feats_ref, text_ref, norms_ref, ids_row, state_ref, proj, texts, images, raw_ref, acc, own_grad, weigh0, weigh1,
    send_up, send_down, recv_up, recv_down,
    feats_all, clipped, clipped_all, spread, x_send, x_recv, z_part, z_recv, z_tiles,
    state_recv, state_tile, sums_send, sq_send, sq_recv,
    load_sems, send_sems, recv_sems,
):
    x, y, z, c = place()
    col = lax.axis_index("col")
    k = c * 4 + y
    other = 1 - c
    zl = lax.rem(z, 2)
    at_x = [device(shift(x, o, X), y, z, c) for o in range(1, X)]
    at_y = [device(x, shift(y, o, Y), z, c) for o in range(1, Y)]
    at_z = [device(x, y, shift(z, o, Z), c) for o in range(1, Z)]
    across = device(x, y, z, other)
    at_y_across = [device(x, shift(y, o, Y), z, other) for o in range(1, Y)]
    flip = z + 1 - 2 * zl
    at_flip = [device(x, shift(y, o, Y), flip, cc) for o in range(Y) for cc in (c, other)][1:]
    x_up, x_down, y_up, y_down, z_up, z_down = at_x[0], at_x[2], at_y[0], at_y[2], at_z[0], at_z[6]

    loads = [
        pltpu.make_async_copy(src, dst, load_sems.at[i])
        for i, (src, dst) in enumerate((
            (text_hbm, text_ref), (feats_hbm, feats_ref), (proj_hbm, proj),
            (state_hbm, state_ref), (norms_hbm, norms_ref), (ids_hbm, ids_row),
        ))
    ]
    for load in loads:
        load.start()
    loads[0].wait()
    text = text_ref[...].astype(F32)
    texts[0:PAIRS, :] = (
        text * lax.rsqrt(jnp.sum(text * text, axis=1, keepdims=True) + EPSILON)
    ).astype(BF16)

    barrier = pltpu.get_barrier_semaphore()
    partners = at_x + at_y + at_z + [across] + at_y_across + at_flip
    for target in partners:
        pl.semaphore_signal(barrier, inc=1, device_id=target, device_id_type=MESH)
    pl.semaphore_wait(barrier, len(partners))
    net = Copies(send_sems, recv_sems)

    def lanes(index, width=128):
        return pl.ds(pl.multiple_of(index * width, width), width)

    def slot(rx, ry, rows, core=0):
        base = (core * 16 + rx * 4 + ry) * PAIRS
        return texts.at[base + rows[0]:base + rows[1], :]

    def hop(axis, up, rx, ry, rows):
        step = 3 if up else 1
        if axis == "x":
            return net.plan(slot(rx, ry, rows), slot((rx + step) % 4, ry, rows), x_up if up else x_down)
        return net.plan(slot(rx, ry, rows), slot(rx, (ry + step) % 4, rows), y_up if up else y_down)

    crossings = [[] for _ in range(X)]

    def cross(rx, ry, rows):
        crossings[rx].append(net.plan(slot(rx, ry, rows), slot(rx, ry, rows, 1), across))
        return crossings[rx][-1]

    class Half:
        def __init__(self, first, second, low):
            self.rows, self.swap = (low, low + 64), first == "y"
            self.parts = ((low, low + 32), (low + 32, low + 64))
            r, p = self.rows, self.parts
            self.first = [hop(first, up, 0, 0, r) for up in (True, False)]
            self.relay = [hop(first, up, *self.at(3 if up else 1, 0), p[0 if up else 1]) for up in (True, False)]
            self.second = [[hop(second, up, *self.at(a, 0), r) for up in (True, False)] for a in range(4)]
            self.last = [
                [hop(second, up, *self.at(a, 3 if up else 1), p[0 if up else 1]) for up in (True, False)]
                for a in range(4)
            ]
            self.cross = [
                [cross(*self.at(a, b), r) if a or b else None for b in range(4)] for a in range(4)
            ]

        def at(self, a, b):
            return (b, a) if self.swap else (a, b)

        def open(self, a):
            for copy in self.second[a]:
                copy.start()

        def got_first(self, i):
            a = (3, 1)[i]
            self.first[i].wait_recv()
            self.relay[i].start()
            self.open(a)
            self.cross[a][0].start()

        def got_relay(self):
            for copy in self.relay:
                copy.wait_recv()
            self.open(2)
            self.cross[2][0].start()

        def got_second(self, a):
            for i in range(2):
                self.second[a][i].wait_recv()
                self.last[a][i].start()
                self.cross[a][(3, 1)[i]].start()

        def got_last(self, a):
            for copy in self.last[a]:
                copy.wait_recv()
            self.cross[a][2].start()

    low, high = Half("x", "y", 0), Half("y", "x", 64)
    halves = (low, high)
    for half in halves:
        for copy in half.first:
            copy.start()
    for half in halves:
        half.open(0)
    cross(0, 0, (0, PAIRS)).start()

    for load in loads[1:]:
        load.wait()
    raw = jnp.dot(feats_ref[...], proj[...], preferred_element_type=F32)
    raw_ref[...] = raw
    inverse = lax.rsqrt(jnp.sum(raw * raw, axis=1, keepdims=True) + EPSILON)

    def image(index, rows=(0, PAIRS)):
        return images.at[index * PAIRS + rows[0]:index * PAIRS + rows[1], :]

    images[PAIRS:2 * PAIRS, :] = (raw * inverse).astype(BF16)
    up = [net.plan(image(a), image(b), z_up) for a, b in ((1, 7), (7, 5), (5, 3))]
    down = [net.plan(image(a), image(b), z_down) for a, b in ((1, 6), (6, 4), (4, 2))]
    up.append(net.plan(image(3, (0, 64)), image(0, (0, 64)), z_up))
    down.append(net.plan(image(2, (64, 128)), image(0, (64, 128)), z_down))
    up[0].start()
    down[0].start()

    def turn(step):
        for ring in (up, down):
            ring[step].wait_recv()
            if step < 3:
                ring[step + 1].start()

    owner_slot = (lax.rem(y, 2) * 2 + zl) * 2 + c
    zh2 = z - zl
    half_y = lax.div(y, 2)
    state_out = Scatter(
        net, state_ref, state_recv,
        [device(x, i % 4, zh2 + half_y, i // 4) for i in range(8)],
        [jnp.logical_and(zl == half_y, k == i) for i in range(8)],
        owner_slot,
    )

    for half in halves:
        half.got_first(0)
        half.got_first(1)
    for half in halves:
        half.got_second(0)
    turn(0)
    for half in halves:
        half.got_relay()
    for half in halves:
        half.got_last(0)
    for a in (3, 1):
        for half in halves:
            half.got_second(a)
    turn(1)
    for half in halves:
        half.got_second(2)
    turn(2)

    def got_last(a):
        for half in halves:
            half.got_last(a)

    def got_cross(rx):
        for copy in crossings[rx]:
            copy.wait_recv()

    def feats_slot(ry, rows=(0, W)):
        return feats_all.at[rows[0]:rows[1], ry * PAIRS:(ry + 1) * PAIRS]

    feats_all[:, 0:PAIRS] = feats_ref[...].T
    feats_near = [net.plan(feats_slot(0), feats_slot(3), y_up), net.plan(feats_slot(0), feats_slot(1), y_down)]
    feats_far = [
        net.plan(feats_slot(3, (0, W // 2)), feats_slot(2, (0, W // 2)), y_up),
        net.plan(feats_slot(1, (W // 2, W)), feats_slot(2, (W // 2, W)), y_down),
    ]
    feats_cross = net.plan(feats_all.at[:, 0:512], feats_all.at[:, 512:1024], across)
    def feats_on():
        for near, far in zip(feats_near, feats_far):
            near.wait_recv()
            far.start()

    def feats_over():
        for copy in feats_far:
            copy.wait_recv()
        feats_cross.start()

    def pack(dst, full, unit):
        along = jnp.sum(full * unit, axis=1, keepdims=True).astype(BF16).astype(F32)
        dst[:, 0:E] = (full - along * unit).astype(BF16)
        dst[:, E:SLOT] = jnp.broadcast_to(along, (full.shape[0], 128)).astype(BF16)

    def unpack(src, unit):
        return src[:, 0:E].astype(F32) + src[:, E:SLOT].astype(F32)[:, 0:1] * unit

    class Side:
        def __init__(self, first, come, sends, recvs, target):
            self.blocks, self.sends, self.recvs = (0, first, first + 2, first + 4), sends, recvs
            self.rows = ((64 - come, 128 - come), (come, come + 64))
            self.copies = [net.plan(sends.at[i], recvs.at[i], target) for i in range(7)]

        def give(self, hop, late):
            i = 2 * hop - 1 + late
            base = self.blocks[hop] * PAIRS
            start, stop = self.rows[late]
            unit = images[base + start:base + stop, :].astype(F32)
            full = LOGIT_SCALE * acc[base + start:base + stop, :]
            if hop > 1 or (hop == 1 and late):
                come = i - 2
                self.copies[come].wait_recv()
                full = full + unpack(self.recvs.at[come], unit)
            pack(self.sends.at[i], full, unit)
            self.copies[i].start()

    sides = (Side(2, 0, send_up, recv_up, z_up), Side(3, 64, send_down, recv_down, z_down))

    def give(hop, late):
        for side in sides:
            side.give(hop, late)

    def open_sums():
        give(0, 1)
        give(1, 0)

    schedule = {
        1: [lambda: got_last(3), lambda: got_last(1)],
        3: [lambda: got_last(2)],
        4: [lambda: turn(3), lambda: [copy.start() for copy in feats_near], state_out.start],
        8: [lambda: got_cross(0), feats_on],
        9: [lambda: got_cross(3)],
        10: [lambda: got_cross(1)],
        11: [lambda: got_cross(2)],
        13: [open_sums, feats_over],
        15: [lambda: give(1, 1)],
    }
    acc[...] = jnp.zeros_like(acc)

    def run_events(s, which):
        for at in which:
            if at in schedule:

                @pl.when(s == at)
                def _(events=schedule[at]):
                    for event in events:
                        event()

    def where(s):
        quarter, turn_at = lax.div(s, 4), lax.rem(s, 4)
        near = jnp.logical_or(quarter == 0, quarter == 3)
        rx = lax.select(turn_at == 0, 0, lax.select(turn_at == 1, 3, turn_at - 1))
        rows = pl.ds(pl.multiple_of(lax.select(near, IMAGES, 0), IMAGES), IMAGES)
        base = (lax.div(quarter, 2) * 4 + rx) * CHUNK
        return rows, pl.ds(pl.multiple_of(base, CHUNK), CHUNK)

    def weigh(s, dst):
        rows, block = where(s)
        cosine = lax.dot_general(
            images[rows, :], texts[block, :], (((1,), (1,)), ((), ())), preferred_element_type=F32
        )
        dst[...] = sigmoid_of(cosine).astype(BF16)

    def fold(s, src):
        rows, block = where(s)
        acc[rows, :] += jnp.dot(src[...], texts[block, :], preferred_element_type=F32)

    def two_parts(t, carry):
        s = 2 * t
        run_events(s + 1, range(1, 15, 2))
        weigh(s + 1, weigh1)
        fold(s, weigh0)
        run_events(s + 2, range(2, 16, 2))
        weigh(s + 2, weigh0)
        fold(s + 1, weigh1)
        return carry

    weigh(jnp.int32(0), weigh0)
    lax.fori_loop(0, 7, two_parts, 0)
    for event in schedule[15]:
        event()
    weigh(jnp.int32(15), weigh1)
    fold(jnp.int32(14), weigh0)
    fold(jnp.int32(15), weigh1)
    for hop in (2, 3):
        give(hop, 0)
        give(hop, 1)
    unit = images[PAIRS:2 * PAIRS, :].astype(F32)
    text = texts[0:PAIRS, :].astype(F32)
    cosine = jnp.sum(unit * text, axis=1, keepdims=True)
    sigmoid = sigmoid_of(cosine)
    change = (sigmoid - 1.0).astype(BF16).astype(F32) - sigmoid.astype(BF16).astype(F32)
    own_grad[...] = LOGIT_SCALE * (acc[PAIRS:2 * PAIRS, :] + change * text)

    state_out.wait()
    state_tile[...] = jnp.zeros_like(state_tile)
    for piece in range(8):
        first = 11 * (piece // 2) + 5 * (piece % 2)
        for a in range(3):
            state_tile[a, first:first + 6, :] += state_recv[piece, a, 0:6, :]

    raw = raw_ref[...]
    inverse = lax.rsqrt(jnp.sum(raw * raw, axis=1, keepdims=True) + EPSILON)
    feat_gram = lax.dot_general(
        feats_ref[...], feats_ref[...], (((1,), (1,)), ((), ())), preferred_element_type=F32
    )
    local_row = (ids_row[...] - (lax.axis_index("row") * 16 + col) * USERS).astype(F32)
    square_shape = (PAIRS, PAIRS)
    diagonal = lax.broadcasted_iota(jnp.int32, square_shape, 0) == lax.broadcasted_iota(
        jnp.int32, square_shape, 1
    )
    local_column = jnp.sum(jnp.where(diagonal, local_row, 0.0), axis=1, keepdims=True)
    same_user = local_column == local_row
    users = lax.broadcasted_iota(jnp.int32, (PAIRS, USERS), 1).astype(F32)
    bound = jnp.sum(jnp.where(local_column == users, norms_ref[...], 0.0), axis=1, keepdims=True)
    unit = images[PAIRS:2 * PAIRS, :].astype(F32)
    for late in range(2):
        for side in sides:
            side.copies[5 + late].wait_recv()
            start, stop = side.rows[late]
            own_grad[start:stop, :] += unpack(side.recvs.at[5 + late], unit[start:stop])
    unit_grad = own_grad[...]
    inner = jnp.sum(raw * unit_grad, axis=1, keepdims=True)
    embed_grad = inverse * unit_grad - inverse * inverse * inverse * raw * inner
    grad_gram = lax.dot_general(
        embed_grad, embed_grad, (((1,), (1,)), ((), ())),
        precision=lax.Precision.HIGHEST, preferred_element_type=F32,
    )
    terms = jnp.sum(jnp.where(same_user, feat_gram * grad_gram, 0.0), axis=0, keepdims=True)
    user_sq = jnp.sum(jnp.where(same_user, terms, 0.0), axis=1, keepdims=True)
    factor = bound / jnp.maximum(jnp.sqrt(user_sq), bound)
    clipped[...] = (factor * embed_grad).astype(BF16)

    def rows_of(core, ry):
        return clipped_all.at[(core * 4 + ry) * PAIRS:(core * 4 + ry + 1) * PAIRS, :]

    parts = []
    for o in range(1, Y):
        parts.append(net.push(clipped.at[:, lanes(c * 4 + shift(y, o, Y))], rows_of(0, 4 - o), at_y[o - 1]))
        parts.append(net.push(clipped.at[:, lanes(other * 4 + shift(y, o, Y))], rows_of(1, 4 - o), at_y_across[o - 1]))
    parts.append(net.push(clipped.at[:, lanes(other * 4 + y)], rows_of(1, 0), across))
    clipped_all[0:PAIRS, :] = clipped[:, lanes(k)]
    spread[...] = jnp.zeros_like(spread)
    feats_cross.wait_recv()
    for copy in parts:
        copy.wait_recv()

    def share(index):
        block = feats_all[pl.ds(pl.multiple_of(index * SHARE, 16), SHARE), :]
        part = jnp.dot(block, clipped_all[...], preferred_element_type=F32)
        for piece in range(Z):
            spread[piece * PADDED:piece * PADDED + BLOCK, :] = part[piece * BLOCK:(piece + 1) * BLOCK]
        return spread[...]

    moves = []
    for o in range(1, X):
        x_send[o - 1] = share(shift(x, o, X)).astype(BF16)
        moves.append(net.push(x_send.at[o - 1], x_recv.at[o - 1], at_x[o - 1]))
    total = share(x)
    for o in range(1, X):
        moves[o - 1].wait_recv()
        total = total + x_recv[o - 1].astype(F32)
    z_part[...] = total

    def rows(index):
        return pl.ds(pl.multiple_of(index * PADDED, 16), PADDED)

    moves = [
        net.push(z_part.at[rows(shift(z, o, Z)), :], z_recv.at[o - 1], at_z[o - 1])
        for o in range(1, Z)
    ]
    grad = z_part[rows(z), :]
    for o in range(1, Z):
        moves[o - 1].wait_recv()
        grad = grad + z_recv[o - 1]

    new_sum = state_tile[0] + grad
    update = new_sum + state_tile[1]
    for piece in range(8):
        first = 11 * (piece // 2) + 5 * (piece % 2)
        sums_send[piece] = new_sum[first:first + 8]

    square = jnp.sum((update * update).reshape(PADDED // 8, 8, 128), axis=0)
    at = 0
    for stage, targets in enumerate((at_z, at_x, at_y + [across] + at_y_across)):
        sq_send[stage] = square
        moves = [
            net.push(sq_send.at[stage], sq_recv.at[at + i], target)
            for i, target in enumerate(targets)
        ]
        for i, copy in enumerate(moves):
            copy.wait_recv()
            square = square + sq_recv[at + i]
        at += len(targets)
    norm = jnp.sqrt(jnp.sum(square, keepdims=True))
    cap = math.sqrt(W * E)
    shrink = cap / jnp.maximum(norm, cap)
    tile = (state_tile[2] - RATE * shrink * update).astype(BF16)

    z_tiles[rows(z), :] = tile
    moves = [net.push(z_tiles.at[rows(z), :], z_tiles.at[rows(z), :], target) for target in at_z]
    sums_out = Scatter(
        net, sums_send, sums_ref,
        [device(x, 2 * zl + i // 4, zh2 + (i // 2) % 2, i % 2) for i in range(8)],
        [
            jnp.logical_and(half_y == zl, owner_slot == i) for i in range(8)
        ],
        k,
    )
    sums_out.start()
    for copy in moves:
        copy.wait_recv()
    whole = z_tiles[...].astype(F32)
    whole = jnp.concatenate([whole[piece * PADDED:piece * PADDED + BLOCK] for piece in range(Z)], axis=0)
    share_rows = pl.ds(pl.multiple_of(x * SHARE, 16), SHARE)
    weights_ref[share_rows, lanes(k)] = whole.astype(BF16)

    half_rows = SHARE // 2

    def part_rows(index, upper):
        return pl.ds(pl.multiple_of(index * SHARE + upper * half_rows, 16), half_rows)

    first = weights_ref.at[part_rows(x, 0), lanes(k)]
    second = weights_ref.at[part_rows(x, 1), lanes(k)]
    moves_y = [net.push(first, first, target) for target in at_y]
    moves_x = [net.push(second, second, target) for target in at_x]
    for copy in moves_y:
        copy.wait_recv()
    crossings = []

    def give(piece):
        crossings.append(net.push(piece, piece, across))

    def low_piece(index, rows=(0, half_rows)):
        start = pl.multiple_of(index * SHARE + rows[0], 16)
        return weights_ref.at[pl.ds(start, rows[1] - rows[0]), lanes(c, 512)]

    def high_piece(index, away):
        return weights_ref.at[part_rows(shift(x, index, X), 1), lanes(c * 4 + shift(y, away, Y))]

    low_moves = [net.push(low_piece(x), low_piece(x), target) for target in (x_up, x_down)]
    give(low_piece(x))
    for copy in moves_x:
        copy.wait_recv()
    high_moves = [
        [net.push(high_piece(a, 0), high_piece(a, 0), target) for a in range(X)]
        for target in (y_up, y_down)
    ]
    for a in range(X):
        give(high_piece(a, 0))
    low_relays, high_relays = [], []
    for copy, away, rows_sent, target in (
        (low_moves[0], 3, (0, 96), x_up), (low_moves[1], 1, (96, half_rows), x_down)
    ):
        copy.wait_recv()
        index = shift(x, away, X)
        low_relays.append(net.push(low_piece(index, rows_sent), low_piece(index, rows_sent), target))
        give(low_piece(index))
    for copies, away, sent, target in ((high_moves[0], 3, (0, 1), y_up), (high_moves[1], 1, (2, 3), y_down)):
        for copy in copies:
            copy.wait_recv()
        for a in sent:
            high_relays.append(net.push(high_piece(a, away), high_piece(a, away), target))
        for a in range(X):
            give(high_piece(a, away))
    for copy in low_relays:
        copy.wait_recv()
    give(low_piece(shift(x, 2, X)))
    for copy in high_relays:
        copy.wait_recv()
    for a in range(X):
        give(high_piece(a, 2))
    for copy in crossings:
        copy.wait_recv()
    sums_out.wait()
    state_out.wait_sent()
    sums_out.wait_sent()
    net.finish()


def body(
    image_feats, text_emb, projection, clip_norms, user_ids, grad_sum, init_weights, tree_noise
):
    c = lax.rem(lax.axis_index("col"), 2)
    state = jnp.pad(jnp.stack([grad_sum, tree_noise, init_weights]), ((0, 0), (4, 4), (0, 0)))
    state = lax.dynamic_slice(state, (0, 4 - 4 * c, 0), (3, 48, 128))
    state = state.reshape(3, 6, 8, 128).transpose(2, 0, 1, 3)
    state = jnp.pad(state, ((0, 0), (0, 0), (0, 2), (0, 0)))
    vmem = pl.BlockSpec(memory_space=pltpu.VMEM)
    weights, sums = pl.pallas_call(
        kernel,
        out_shape=(
            jax.ShapeDtypeStruct((W, E), BF16),
            jax.ShapeDtypeStruct((8, 8, 128), F32),
        ),
        in_specs=[pl.BlockSpec(memory_space=pl.ANY)] * 6,
        out_specs=(vmem, vmem),
        scratch_shapes=[
            pltpu.VMEM((PAIRS, W), BF16),
            pltpu.VMEM((PAIRS, E), BF16),
            pltpu.VMEM((1, USERS), F32),
            pltpu.VMEM((1, PAIRS), jnp.int32),
            pltpu.VMEM((8, 3, 8, 128), F32),
            pltpu.VMEM((W, E), BF16),
            pltpu.VMEM((TEXTS, E), BF16),
            pltpu.VMEM((Z * PAIRS, E), BF16),
            pltpu.VMEM((PAIRS, E), F32),
            pltpu.VMEM((Z * PAIRS, E), F32),
            pltpu.VMEM((PAIRS, E), F32),
            pltpu.VMEM((IMAGES, CHUNK), BF16),
            pltpu.VMEM((IMAGES, CHUNK), BF16),
            pltpu.VMEM((7, PAIRS // 2, SLOT), BF16),
            pltpu.VMEM((7, PAIRS // 2, SLOT), BF16),
            pltpu.VMEM((7, PAIRS // 2, SLOT), BF16),
            pltpu.VMEM((7, PAIRS // 2, SLOT), BF16),
            pltpu.VMEM((W, 8 * PAIRS), BF16),
            pltpu.VMEM((PAIRS, E), BF16),
            pltpu.VMEM((8 * PAIRS, 128), BF16),
            pltpu.VMEM((WIDE, 128), F32),
            pltpu.VMEM((X - 1, WIDE, 128), BF16),
            pltpu.VMEM((X - 1, WIDE, 128), BF16),
            pltpu.VMEM((WIDE, 128), F32),
            pltpu.VMEM((Z - 1, PADDED, 128), F32),
            pltpu.VMEM((WIDE, 128), BF16),
            pltpu.VMEM((8, 3, 8, 128), F32),
            pltpu.VMEM((3, PADDED, 128), F32),
            pltpu.VMEM((8, 8, 128), F32),
            pltpu.VMEM((3, 8, 128), F32),
            pltpu.VMEM((17, 8, 128), F32),
            pltpu.SemaphoreType.DMA((6,)),
            pltpu.SemaphoreType.DMA((COPIES,)),
            pltpu.SemaphoreType.DMA((COPIES,)),
        ],
        compiler_params=pltpu.CompilerParams(
            collective_id=1, has_side_effects=True, vmem_limit_bytes=48 * 1024 * 1024
        ),
    )(
        image_feats, text_emb, projection, clip_norms.reshape(1, USERS),
        user_ids.reshape(1, PAIRS), state,
    )
    sums = sums[:, :6].transpose(1, 0, 2).reshape(48, 128)
    return weights, lax.dynamic_slice(sums, (4 * c, 0), (44, 128))


def solution(mesh):
    in_specs = (
        P(("row", "col"), None),
        P(("row", "col"), None),
        P(),
        P(("row", "col")),
        P(("row", "col")),
        P(("row", "col"), None),
        P(("row", "col"), None),
        P(("row", "col"), None),
    )
    out_specs = (P(), P(("row", "col"), None))
    return jax.shard_map(body, mesh=mesh, in_specs=in_specs, out_specs=out_specs, check_vma=False)
```

```python
import math

import jax
import jax.numpy as jnp
from jax import lax
from jax.experimental import pallas as pl
from jax.experimental.pallas import tpu as pltpu
from jax.sharding import PartitionSpec as P

LOGIT_SCALE = 32.0
LOGIT_BIAS = -5.0
RATE = 0.5
EPSILON = 1e-06

MESH = pl.DeviceIdType.MESH
X, Y, Z = 4, 4, 8
W, E, PAIRS, USERS = 1408, 1024, 128, 16
SHARE = W // X
BLOCK = SHARE // Z
PADDED = 48
WIDE = Z * PADDED
TEXTS = 2 * X * Y * PAIRS
CHUNK = 2048
IMAGES = 2 * PAIRS
SLOT = E + 128
COPIES = 240
F32, BF16 = jnp.float32, jnp.bfloat16


def place():
    row, col = lax.axis_index("row"), lax.axis_index("col")
    x, zh = lax.div(row, 4), lax.rem(row, 4)
    y, zl, c = lax.div(col, 4), lax.rem(lax.div(col, 2), 2), lax.rem(col, 2)
    return x, y, zh * 2 + zl, c


def device(x, y, z, c):
    return (x * 4 + lax.div(z, 2), y * 4 + lax.rem(z, 2) * 2 + c)


def shift(value, by, size):
    return lax.rem(value + by, size)


class Copies:
    def __init__(self, send_sems, recv_sems):
        self.send_sems, self.recv_sems, self.used, self.all = send_sems, recv_sems, 0, []

    def reserve(self, count):
        self.used += count
        return self.used - count

    def make(self, src, dst, target, send_at, recv_at):
        return pltpu.make_async_remote_copy(
            src_ref=src,
            dst_ref=dst,
            send_sem=self.send_sems.at[send_at],
            recv_sem=self.recv_sems.at[recv_at],
            device_id=target,
            device_id_type=MESH,
        )

    def plan(self, src, dst, target):
        at = self.reserve(1)
        copy = self.make(src, dst, target, at, at)
        self.all.append(copy)
        return copy

    def push(self, src, dst, target):
        copy = self.plan(src, dst, target)
        copy.start()
        return copy

    def finish(self):
        for copy in self.all:
            copy.wait_send()


class Scatter:
    def __init__(self, net, src, dst, targets, is_self, mine):
        self.net, self.src, self.dst, self.targets, self.is_self, self.mine = net, src, dst, targets, is_self, mine
        self.at = net.reserve(8)

    def remote(self, i):
        return self.net.make(
            self.src.at[i], self.dst.at[self.mine], self.targets[i], self.at + i, self.at + self.mine
        )

    def local(self, i):
        sem = self.net.recv_sems.at[self.at + self.mine]
        return pltpu.make_async_copy(self.src.at[i], self.dst.at[self.mine], sem)

    def start(self):
        for i in range(8):
            pl.when(jnp.logical_not(self.is_self[i]))(self.remote(i).start)
            pl.when(self.is_self[i])(self.local(i).start)

    def wait(self):
        for i in range(8):
            self.net.make(self.src.at[i], self.dst.at[i], self.targets[i], self.at + i, self.at + i).wait_recv()

    def wait_sent(self):
        for i in range(8):
            pl.when(jnp.logical_not(self.is_self[i]))(self.remote(i).wait_send)


def kernel(
    feats_hbm, text_hbm, proj_hbm, norms_hbm, ids_hbm, state_hbm,
    weights_ref, sums_ref,
    feats_ref, text_ref, norms_ref, ids_row, state_ref, proj, texts, images, raw_ref, acc, own_grad, weigh0, weigh1,
    send_up, send_down, recv_up, recv_down,
    feats_all, clipped, clipped_all, spread, x_send, x_recv, z_part, z_recv, z_tiles,
    state_recv, state_tile, sums_send, sq_send, sq_recv,
    load_sems, send_sems, recv_sems,
):
    x, y, z, c = place()
    col = lax.axis_index("col")
    k = c * 4 + y
    other = 1 - c
    zl = lax.rem(z, 2)
    at_x = [device(shift(x, o, X), y, z, c) for o in range(1, X)]
    at_y = [device(x, shift(y, o, Y), z, c) for o in range(1, Y)]
    at_z = [device(x, y, shift(z, o, Z), c) for o in range(1, Z)]
    across = device(x, y, z, other)
    at_y_across = [device(x, shift(y, o, Y), z, other) for o in range(1, Y)]
    flip = z + 1 - 2 * zl
    at_flip = [device(x, shift(y, o, Y), flip, cc) for o in range(Y) for cc in (c, other)][1:]
    x_up, x_down, y_up, y_down, z_up, z_down = at_x[0], at_x[2], at_y[0], at_y[2], at_z[0], at_z[6]

    loads = [
        pltpu.make_async_copy(src, dst, load_sems.at[i])
        for i, (src, dst) in enumerate((
            (text_hbm, text_ref), (feats_hbm, feats_ref), (proj_hbm, proj),
            (state_hbm, state_ref), (norms_hbm, norms_ref), (ids_hbm, ids_row),
        ))
    ]
    for load in loads:
        load.start()
    loads[0].wait()
    text = text_ref[...].astype(F32)
    texts[0, 0, 0] = (
        text * lax.rsqrt(jnp.sum(text * text, axis=1, keepdims=True) + EPSILON)
    ).astype(BF16)

    barrier = pltpu.get_barrier_semaphore()
    partners = at_x + at_y + at_z + [across] + at_y_across + at_flip
    for target in partners:
        pl.semaphore_signal(barrier, inc=1, device_id=target, device_id_type=MESH)
    pl.semaphore_wait(barrier, len(partners))
    net = Copies(send_sems, recv_sems)

    def lanes(index, width=128):
        return pl.ds(pl.multiple_of(index * width, width), width)

    low, high = (0, 64), (64, 128)

    def unit_of(rx, ry, rows, core=0):
        return texts.at[core, rx, ry, rows[0]:rows[1], :]

    def along(axis, up, rx, ry, rows):
        step = 3 if up else 1
        if axis == "x":
            return net.plan(unit_of(rx, ry, rows), unit_of((rx + step) % 4, ry, rows), x_up if up else x_down)
        return net.plan(unit_of(rx, ry, rows), unit_of(rx, (ry + step) % 4, rows), y_up if up else y_down)

    every, front, back = slice(0, 4), slice(0, 2), slice(2, 4)
    first = [
        [along("x", up, 0, 0, low) for up in (True, False)],
        [along("y", up, 0, 0, high) for up in (True, False)],
    ]
    first_far = [
        [along("x", True, 3, 0, (0, 32)), along("x", False, 1, 0, (32, 64))],
        [along("y", True, 0, 3, (64, 96)), along("y", False, 0, 1, (96, 128))],
    ]
    second = [
        [along("y", up, every, 0, low) for up in (True, False)],
        [along("x", up, 0, every, high) for up in (True, False)],
    ]
    second_far = [
        [along("y", True, front, 3, low), along("y", False, back, 1, low)],
        [along("x", True, 3, front, high), along("x", False, 1, back, high)],
    ]
    crossings = []

    def cross(rx, ry, rows):
        crossings.append(net.push(unit_of(rx, ry, rows), unit_of(rx, ry, rows, 1), across))

    def start(copies):
        for copy in copies:
            copy.start()

    def arrive(copies):
        for copy in copies:
            copy.wait_recv()

    start(first[0] + first[1])

    for load in loads[1:]:
        load.wait()
    raw = jnp.dot(feats_ref[...], proj[...], preferred_element_type=F32)
    raw_ref[...] = raw
    inverse = lax.rsqrt(jnp.sum(raw * raw, axis=1, keepdims=True) + EPSILON)

    def image(index, rows=(0, PAIRS)):
        return images.at[index * PAIRS + rows[0]:index * PAIRS + rows[1], :]

    images[PAIRS:2 * PAIRS, :] = (raw * inverse).astype(BF16)
    up = [net.plan(image(a), image(b), z_up) for a, b in ((1, 7), (7, 5), (5, 3))]
    down = [net.plan(image(a), image(b), z_down) for a, b in ((1, 6), (6, 4), (4, 2))]
    up.append(net.plan(image(3, (0, 64)), image(0, (0, 64)), z_up))
    down.append(net.plan(image(2, (64, 128)), image(0, (64, 128)), z_down))
    up[0].start()
    down[0].start()

    def turn(step):
        for ring in (up, down):
            ring[step].wait_recv()
            if step < 3:
                ring[step + 1].start()

    owner_slot = (lax.rem(y, 2) * 2 + zl) * 2 + c
    zh2 = z - zl
    half_y = lax.div(y, 2)
    state_out = Scatter(
        net, state_ref, state_recv,
        [device(x, i % 4, zh2 + half_y, i // 4) for i in range(8)],
        [jnp.logical_and(zl == half_y, k == i) for i in range(8)],
        owner_slot,
    )

    for i in range(2):
        for near, far in zip(first[i], first_far[i]):
            near.wait_recv()
            far.start()
    for i in range(2):
        arrive(first_far[i])
        start(second[i])
    cross(every, 0, low)
    cross(0, every, high)
    turn(0)
    turn(1)
    for j in range(2):
        for i in range(2):
            second[i][j].wait_recv()
            second_far[i][j].start()
            at = 3 if j == 0 else 1
            cross(*((every, at, low), (at, every, high))[i])
    turn(2)
    for i in range(2):
        arrive(second_far[i])
        cross(*((every, 2, low), (2, every, high))[i])
    turn(3)

    def feats_slot(ry, rows=(0, W)):
        return feats_all.at[rows[0]:rows[1], ry * PAIRS:(ry + 1) * PAIRS]

    feats_all[:, 0:PAIRS] = feats_ref[...].T
    feats_near = [net.plan(feats_slot(0), feats_slot(3), y_up), net.plan(feats_slot(0), feats_slot(1), y_down)]
    feats_far = [
        net.plan(feats_slot(3, (0, W // 2)), feats_slot(2, (0, W // 2)), y_up),
        net.plan(feats_slot(1, (W // 2, W)), feats_slot(2, (W // 2, W)), y_down),
    ]
    feats_cross = net.plan(feats_all.at[:, 0:512], feats_all.at[:, 512:1024], across)
    for copy in feats_near:
        copy.start()
    state_out.start()

    grads_up = [net.plan(send_up.at[0, 0:64], recv_up.at[0, 0:64], z_up)]
    grads_down = [net.plan(send_down.at[0, 0:64], recv_down.at[0, 0:64], z_down)]
    for i in range(1, 4):
        grads_up.append(net.plan(send_up.at[i], recv_up.at[i], z_up))
        grads_down.append(net.plan(send_down.at[i], recv_down.at[i], z_down))

    def pack(dst, full, unit):
        along = jnp.sum(full * unit, axis=1, keepdims=True).astype(BF16).astype(F32)
        dst[:, 0:E] = (full - along * unit).astype(BF16)
        dst[:, E:SLOT] = jnp.broadcast_to(along, (full.shape[0], 128)).astype(BF16)

    def unpack(src, unit):
        return src[:, 0:E].astype(F32) + src[:, E:SLOT].astype(F32)[:, 0:1] * unit

    def texts_of(core):
        return texts[core].reshape(CHUNK, E)

    def weigh(step, n):
        rows = slice(step * IMAGES, (step + 1) * IMAGES)
        cosine = lax.dot_general(
            images[rows, :], texts_of(n), (((1,), (1,)), ((), ())), preferred_element_type=F32
        )
        pair = 0.5 + 0.5 * jnp.tanh(0.5 * LOGIT_SCALE * cosine + 0.5 * LOGIT_BIAS)
        (weigh0, weigh1)[step % 2][:, lanes(n, CHUNK)] = pair.astype(BF16)

    def fold(step, n):
        acc[...] += jnp.dot(
            (weigh0, weigh1)[step % 2][:, lanes(n, CHUNK)], texts_of(n), preferred_element_type=F32
        )

    def first_weights(n, carry):
        @pl.when(n == 1)
        def _():
            arrive(crossings)

        weigh(0, n)
        return carry

    lax.fori_loop(0, TEXTS // CHUNK, first_weights, 0)
    for step in range(4):
        acc[...] = jnp.zeros_like(acc)

        def part(n, carry, step=step):
            if step < 3:
                weigh(step + 1, n)
            fold(step, n)
            return carry

        lax.fori_loop(0, TEXTS // CHUNK, part, 0)
        if step == 0:
            far = LOGIT_SCALE * acc[0:PAIRS, :]
            unit = images[0:PAIRS, :].astype(F32)
            pack(send_up.at[0, 0:64], far[0:64], unit[0:64])
            pack(send_down.at[0, 0:64], far[64:128], unit[64:128])
            grads_up[0].start()
            grads_down[0].start()
            unit = images[PAIRS:2 * PAIRS, :].astype(F32)
            text = texts[0, 0, 0].astype(F32)
            cosine = jnp.sum(unit * text, axis=1, keepdims=True)
            sigmoid = 0.5 + 0.5 * jnp.tanh(0.5 * LOGIT_SCALE * cosine + 0.5 * LOGIT_BIAS)
            change = (sigmoid - 1.0).astype(BF16).astype(F32) - sigmoid.astype(BF16).astype(F32)
            own_grad[...] = LOGIT_SCALE * (acc[PAIRS:2 * PAIRS, :] + change * text)
            for near, far_copy in zip(feats_near, feats_far):
                near.wait_recv()
                far_copy.start()
            continue
        for side, sends, recvs, grads in (
            (0, send_up, recv_up, grads_up), (1, send_down, recv_down, grads_down)
        ):
            grads[step - 1].wait_recv()
            first = (2 * step + side) * PAIRS
            full = LOGIT_SCALE * acc[side * PAIRS:(side + 1) * PAIRS, :]
            unit = images[first:first + PAIRS, :].astype(F32)
            if step > 1:
                pack(sends.at[step], full + unpack(recvs.at[step - 1], unit), unit)
            else:
                come = slice(64 * side, 64 * side + 64)
                kept = slice(64 - 64 * side, 128 - 64 * side)
                both = full[come] + unpack(recvs.at[0, 0:64], unit[come])
                pack(sends.at[step, come], both, unit[come])
                pack(sends.at[step, kept], full[kept], unit[kept])
            grads[step].start()
        if step == 1:
            for copy in feats_far:
                copy.wait_recv()
            feats_cross.start()

    state_out.wait()
    state_tile[...] = jnp.zeros_like(state_tile)
    for piece in range(8):
        first = 11 * (piece // 2) + 5 * (piece % 2)
        for a in range(3):
            state_tile[a, first:first + 6, :] += state_recv[piece, a, 0:6, :]

    raw = raw_ref[...]
    inverse = lax.rsqrt(jnp.sum(raw * raw, axis=1, keepdims=True) + EPSILON)
    feat_gram = lax.dot_general(
        feats_ref[...], feats_ref[...], (((1,), (1,)), ((), ())), preferred_element_type=F32
    )
    local_row = (ids_row[...] - (lax.axis_index("row") * 16 + col) * USERS).astype(F32)
    square_shape = (PAIRS, PAIRS)
    diagonal = lax.broadcasted_iota(jnp.int32, square_shape, 0) == lax.broadcasted_iota(
        jnp.int32, square_shape, 1
    )
    local_column = jnp.sum(jnp.where(diagonal, local_row, 0.0), axis=1, keepdims=True)
    same_user = local_column == local_row
    users = lax.broadcasted_iota(jnp.int32, (PAIRS, USERS), 1).astype(F32)
    bound = jnp.sum(jnp.where(local_column == users, norms_ref[...], 0.0), axis=1, keepdims=True)
    unit = images[PAIRS:2 * PAIRS, :].astype(F32)
    grads_up[3].wait_recv()
    grads_down[3].wait_recv()
    unit_grad = own_grad[...] + unpack(recv_up.at[3], unit) + unpack(recv_down.at[3], unit)
    inner = jnp.sum(raw * unit_grad, axis=1, keepdims=True)
    embed_grad = inverse * unit_grad - inverse * inverse * inverse * raw * inner
    grad_gram = lax.dot_general(
        embed_grad, embed_grad, (((1,), (1,)), ((), ())),
        precision=lax.Precision.HIGHEST, preferred_element_type=F32,
    )
    terms = jnp.sum(jnp.where(same_user, feat_gram * grad_gram, 0.0), axis=0, keepdims=True)
    user_sq = jnp.sum(jnp.where(same_user, terms, 0.0), axis=1, keepdims=True)
    factor = bound / jnp.maximum(jnp.sqrt(user_sq), bound)
    clipped[...] = (factor * embed_grad).astype(BF16)

    def rows_of(core, ry):
        return clipped_all.at[(core * 4 + ry) * PAIRS:(core * 4 + ry + 1) * PAIRS, :]

    parts = []
    for o in range(1, Y):
        parts.append(net.push(clipped.at[:, lanes(c * 4 + shift(y, o, Y))], rows_of(0, 4 - o), at_y[o - 1]))
        parts.append(net.push(clipped.at[:, lanes(other * 4 + shift(y, o, Y))], rows_of(1, 4 - o), at_y_across[o - 1]))
    parts.append(net.push(clipped.at[:, lanes(other * 4 + y)], rows_of(1, 0), across))
    clipped_all[0:PAIRS, :] = clipped[:, lanes(k)]
    spread[...] = jnp.zeros_like(spread)
    feats_cross.wait_recv()
    for copy in parts:
        copy.wait_recv()

    def share(index):
        block = feats_all[pl.ds(pl.multiple_of(index * SHARE, 16), SHARE), :]
        part = jnp.dot(block, clipped_all[...], preferred_element_type=F32)
        for piece in range(Z):
            spread[piece * PADDED:piece * PADDED + BLOCK, :] = part[piece * BLOCK:(piece + 1) * BLOCK]
        return spread[...]

    moves = []
    for o in range(1, X):
        x_send[o - 1] = share(shift(x, o, X)).astype(BF16)
        moves.append(net.push(x_send.at[o - 1], x_recv.at[o - 1], at_x[o - 1]))
    total = share(x)
    for o in range(1, X):
        moves[o - 1].wait_recv()
        total = total + x_recv[o - 1].astype(F32)
    z_part[...] = total

    def rows(index):
        return pl.ds(pl.multiple_of(index * PADDED, 16), PADDED)

    moves = [
        net.push(z_part.at[rows(shift(z, o, Z)), :], z_recv.at[o - 1], at_z[o - 1])
        for o in range(1, Z)
    ]
    grad = z_part[rows(z), :]
    for o in range(1, Z):
        moves[o - 1].wait_recv()
        grad = grad + z_recv[o - 1]

    new_sum = state_tile[0] + grad
    update = new_sum + state_tile[1]
    for piece in range(8):
        first = 11 * (piece // 2) + 5 * (piece % 2)
        sums_send[piece] = new_sum[first:first + 8]

    square = jnp.sum((update * update).reshape(PADDED // 8, 8, 128), axis=0)
    at = 0
    for stage, targets in enumerate((at_z, at_x, at_y + [across] + at_y_across)):
        sq_send[stage] = square
        moves = [
            net.push(sq_send.at[stage], sq_recv.at[at + i], target)
            for i, target in enumerate(targets)
        ]
        for i, copy in enumerate(moves):
            copy.wait_recv()
            square = square + sq_recv[at + i]
        at += len(targets)
    norm = jnp.sqrt(jnp.sum(square, keepdims=True))
    cap = math.sqrt(W * E)
    shrink = cap / jnp.maximum(norm, cap)
    tile = (state_tile[2] - RATE * shrink * update).astype(BF16)

    z_tiles[rows(z), :] = tile
    moves = [net.push(z_tiles.at[rows(z), :], z_tiles.at[rows(z), :], target) for target in at_z]
    sums_out = Scatter(
        net, sums_send, sums_ref,
        [device(x, 2 * zl + i // 4, zh2 + (i // 2) % 2, i % 2) for i in range(8)],
        [
            jnp.logical_and(half_y == zl, owner_slot == i) for i in range(8)
        ],
        k,
    )
    sums_out.start()
    for copy in moves:
        copy.wait_recv()
    whole = z_tiles[...].astype(F32)
    whole = jnp.concatenate([whole[piece * PADDED:piece * PADDED + BLOCK] for piece in range(Z)], axis=0)
    weights_ref[x, :, lanes(k)] = whole.astype(BF16)

    half = SHARE // 2

    def low_piece(index, rows=(0, half)):
        return weights_ref.at[index, rows[0]:rows[1], lanes(c, 512)]

    def high_piece(away, shares=slice(0, X)):
        return weights_ref.at[shares, half:SHARE, lanes(c * 4 + shift(y, away, Y))]

    def send(piece, target):
        return net.push(piece, piece, target)

    moves_y = [send(weights_ref.at[x, 0:half, lanes(k)], target) for target in at_y]
    moves_x = [send(weights_ref.at[x, half:SHARE, lanes(k)], target) for target in at_x]
    arrive(moves_y)
    low_moves = [send(low_piece(x), target) for target in (x_up, x_down)]
    arrive(moves_x)
    high_moves = [send(high_piece(0), target) for target in (y_up, y_down)]
    given = [send(low_piece(x), across), send(high_piece(0), across)]
    far = []
    for copy, away, rows_sent, target in (
        (low_moves[0], 3, (0, 96), x_up), (low_moves[1], 1, (96, half), x_down)
    ):
        copy.wait_recv()
        index = shift(x, away, X)
        far.append(send(low_piece(index, rows_sent), target))
        given.append(send(low_piece(index), across))
    for copy, away, shares, target in (
        (high_moves[0], 3, slice(0, 2), y_up), (high_moves[1], 1, slice(2, 4), y_down)
    ):
        copy.wait_recv()
        far.append(send(high_piece(away, shares), target))
        given.append(send(high_piece(away), across))
    arrive(far)
    given += [send(low_piece(shift(x, 2, X)), across), send(high_piece(2), across)]
    arrive(given)
    sums_out.wait()
    state_out.wait_sent()
    sums_out.wait_sent()
    net.finish()


def body(
    image_feats, text_emb, projection, clip_norms, user_ids, grad_sum, init_weights, tree_noise
):
    c = lax.rem(lax.axis_index("col"), 2)
    state = jnp.pad(jnp.stack([grad_sum, tree_noise, init_weights]), ((0, 0), (4, 4), (0, 0)))
    state = lax.dynamic_slice(state, (0, 4 - 4 * c, 0), (3, 48, 128))
    state = state.reshape(3, 6, 8, 128).transpose(2, 0, 1, 3)
    state = jnp.pad(state, ((0, 0), (0, 0), (0, 2), (0, 0)))
    vmem = pl.BlockSpec(memory_space=pltpu.VMEM)
    weights, sums = pl.pallas_call(
        kernel,
        out_shape=(
            jax.ShapeDtypeStruct((X, SHARE, E), BF16),
            jax.ShapeDtypeStruct((8, 8, 128), F32),
        ),
        in_specs=[pl.BlockSpec(memory_space=pl.ANY)] * 6,
        out_specs=(vmem, vmem),
        scratch_shapes=[
            pltpu.VMEM((PAIRS, W), BF16),
            pltpu.VMEM((PAIRS, E), BF16),
            pltpu.VMEM((1, USERS), F32),
            pltpu.VMEM((1, PAIRS), jnp.int32),
            pltpu.VMEM((8, 3, 8, 128), F32),
            pltpu.VMEM((W, E), BF16),
            pltpu.VMEM((2, X, Y, PAIRS, E), BF16),
            pltpu.VMEM((Z * PAIRS, E), BF16),
            pltpu.VMEM((PAIRS, E), F32),
            pltpu.VMEM((IMAGES, E), F32),
            pltpu.VMEM((PAIRS, E), F32),
            pltpu.VMEM((IMAGES, TEXTS), BF16),
            pltpu.VMEM((IMAGES, TEXTS), BF16),
            pltpu.VMEM((4, PAIRS, SLOT), BF16),
            pltpu.VMEM((4, PAIRS, SLOT), BF16),
            pltpu.VMEM((4, PAIRS, SLOT), BF16),
            pltpu.VMEM((4, PAIRS, SLOT), BF16),
            pltpu.VMEM((W, 8 * PAIRS), BF16),
            pltpu.VMEM((PAIRS, E), BF16),
            pltpu.VMEM((8 * PAIRS, 128), BF16),
            pltpu.VMEM((WIDE, 128), F32),
            pltpu.VMEM((X - 1, WIDE, 128), BF16),
            pltpu.VMEM((X - 1, WIDE, 128), BF16),
            pltpu.VMEM((WIDE, 128), F32),
            pltpu.VMEM((Z - 1, PADDED, 128), F32),
            pltpu.VMEM((WIDE, 128), BF16),
            pltpu.VMEM((8, 3, 8, 128), F32),
            pltpu.VMEM((3, PADDED, 128), F32),
            pltpu.VMEM((8, 8, 128), F32),
            pltpu.VMEM((3, 8, 128), F32),
            pltpu.VMEM((17, 8, 128), F32),
            pltpu.SemaphoreType.DMA((6,)),
            pltpu.SemaphoreType.DMA((COPIES,)),
            pltpu.SemaphoreType.DMA((COPIES,)),
        ],
        compiler_params=pltpu.CompilerParams(
            collective_id=1, has_side_effects=True, vmem_limit_bytes=48 * 1024 * 1024
        ),
    )(
        image_feats, text_emb, projection, clip_norms.reshape(1, USERS),
        user_ids.reshape(1, PAIRS), state,
    )
    sums = sums[:, :6].transpose(1, 0, 2).reshape(48, 128)
    return weights.reshape(W, E), lax.dynamic_slice(sums, (4 * c, 0), (44, 128))


def solution(mesh):
    in_specs = (
        P(("row", "col"), None),
        P(("row", "col"), None),
        P(),
        P(("row", "col")),
        P(("row", "col")),
        P(("row", "col"), None),
        P(("row", "col"), None),
        P(("row", "col"), None),
    )
    out_specs = (P(), P(("row", "col"), None))
    return jax.shard_map(body, mesh=mesh, in_specs=in_specs, out_specs=out_specs, check_vma=False)
```

```python
import math

import jax
import jax.numpy as jnp
from jax import lax
from jax.experimental import pallas as pl
from jax.experimental.pallas import tpu as pltpu
from jax.sharding import PartitionSpec as P

LOGIT_SCALE = 32.0
LOGIT_BIAS = -5.0
RATE = 0.5
EPSILON = 1e-06

MESH = pl.DeviceIdType.MESH
X, Y, Z = 4, 4, 8
W, E, PAIRS, USERS = 1408, 1024, 128, 16
SHARE = W // X
BLOCK = SHARE // Z
PADDED = 48
WIDE = Z * PADDED
TEXTS = 2 * X * Y * PAIRS
CHUNK = 1024
IMAGES = 2 * PAIRS
HALF = PAIRS // 2
COPIES = 256
F32, BF16 = jnp.float32, jnp.bfloat16


def place():
    row, col = lax.axis_index("row"), lax.axis_index("col")
    x, zh = lax.div(row, 4), lax.rem(row, 4)
    y, zl, c = lax.div(col, 4), lax.rem(lax.div(col, 2), 2), lax.rem(col, 2)
    return x, y, zh * 2 + zl, c


def device(x, y, z, c):
    return (x * 4 + lax.div(z, 2), y * 4 + lax.rem(z, 2) * 2 + c)


def shift(value, by, size):
    return lax.rem(value + by, size)


class Copies:
    def __init__(self, send_sems, recv_sems):
        self.send_sems, self.recv_sems, self.used, self.all = send_sems, recv_sems, 0, []

    def reserve(self, count):
        self.used += count
        return self.used - count

    def make(self, src, dst, target, send_at, recv_at):
        return pltpu.make_async_remote_copy(
            src_ref=src,
            dst_ref=dst,
            send_sem=self.send_sems.at[send_at],
            recv_sem=self.recv_sems.at[recv_at],
            device_id=target,
            device_id_type=MESH,
        )

    def plan(self, src, dst, target):
        at = self.reserve(1)
        copy = self.make(src, dst, target, at, at)
        self.all.append(copy)
        return copy

    def push(self, src, dst, target):
        copy = self.plan(src, dst, target)
        copy.start()
        return copy

    def finish(self):
        for copy in self.all:
            copy.wait_send()


class Scatter:
    def __init__(self, net, src, dst, targets, is_self, mine):
        self.net, self.src, self.dst, self.targets, self.is_self, self.mine = net, src, dst, targets, is_self, mine
        self.at = net.reserve(8)

    def remote(self, i):
        return self.net.make(
            self.src.at[i], self.dst.at[self.mine], self.targets[i], self.at + i, self.at + self.mine
        )

    def local(self, i):
        sem = self.net.recv_sems.at[self.at + self.mine]
        return pltpu.make_async_copy(self.src.at[i], self.dst.at[self.mine], sem)

    def start(self):
        for i in range(8):
            pl.when(jnp.logical_not(self.is_self[i]))(self.remote(i).start)
            pl.when(self.is_self[i])(self.local(i).start)

    def wait(self):
        for i in range(8):
            self.net.make(self.src.at[i], self.dst.at[i], self.targets[i], self.at + i, self.at + i).wait_recv()

    def wait_sent(self):
        for i in range(8):
            pl.when(jnp.logical_not(self.is_self[i]))(self.remote(i).wait_send)


def kernel(
    feats_hbm, text_hbm, proj_hbm, norms_hbm, ids_hbm, state_hbm,
    weights_ref, sums_ref,
    feats_ref, text_ref, norms_ref, ids_row, state_ref, proj, texts, images, raw_ref, acc, own_grad, weigh0, weigh1,
    send_up, send_down, recv_up, recv_down, send_up_row, send_down_row, recv_up_row, recv_down_row,
    feats_all, clipped, clipped_all, spread, x_send, x_recv, z_part, z_send, z_recv, z_tiles,
    state_recv, state_tile, sums_send, sq_send, sq_recv,
    load_sems, send_sems, recv_sems,
):
    x, y, z, c = place()
    col = lax.axis_index("col")
    k = c * 4 + y
    other = 1 - c
    zl = lax.rem(z, 2)
    at_x = [device(shift(x, o, X), y, z, c) for o in range(1, X)]
    at_y = [device(x, shift(y, o, Y), z, c) for o in range(1, Y)]
    at_z = [device(x, y, shift(z, o, Z), c) for o in range(1, Z)]
    across = device(x, y, z, other)
    at_y_across = [device(x, shift(y, o, Y), z, other) for o in range(1, Y)]
    flip = z + 1 - 2 * zl
    at_flip = [device(x, shift(y, o, Y), flip, cc) for o in range(Y) for cc in (c, other)][1:]
    x_up, x_down, y_up, y_down, z_up, z_down = at_x[0], at_x[2], at_y[0], at_y[2], at_z[0], at_z[6]

    loads = [
        pltpu.make_async_copy(src, dst, load_sems.at[i])
        for i, (src, dst) in enumerate((
            (text_hbm, text_ref), (feats_hbm, feats_ref), (proj_hbm, proj),
            (state_hbm, state_ref), (norms_hbm, norms_ref), (ids_hbm, ids_row),
        ))
    ]
    for load in loads:
        load.start()
    loads[0].wait()
    text = text_ref[...].astype(F32)
    texts[0:PAIRS, :] = (
        text * lax.rsqrt(jnp.sum(text * text, axis=1, keepdims=True) + EPSILON)
    ).astype(BF16)

    barrier = pltpu.get_barrier_semaphore()
    partners = at_x + at_y + at_z + [across] + at_y_across + at_flip
    for target in partners:
        pl.semaphore_signal(barrier, inc=1, device_id=target, device_id_type=MESH)
    pl.semaphore_wait(barrier, len(partners))
    net = Copies(send_sems, recv_sems)

    def lanes(index, width=128):
        return pl.ds(pl.multiple_of(index * width, width), width)

    def slot(rx, ry, rows, core=0):
        base = (core * 16 + rx * 4 + ry) * PAIRS
        return texts.at[base + rows[0]:base + rows[1], :]

    def hop(axis, up, rx, ry, rows):
        step = 3 if up else 1
        if axis == "x":
            return net.plan(slot(rx, ry, rows), slot((rx + step) % 4, ry, rows), x_up if up else x_down)
        return net.plan(slot(rx, ry, rows), slot(rx, (ry + step) % 4, rows), y_up if up else y_down)

    text_crossings = []

    def cross(rx, ry, rows):
        text_crossings.append(net.push(slot(rx, ry, rows), slot(rx, ry, rows, 1), across))

    class Half:
        def __init__(self, first, second, low):
            self.rows, self.swap = (low, low + 64), first == "y"
            self.parts = ((low, low + 32), (low + 32, low + 64))
            r, p = self.rows, self.parts
            self.first = [hop(first, up, 0, 0, r) for up in (True, False)]
            self.relay = [hop(first, up, *self.at(3 if up else 1, 0), p[0 if up else 1]) for up in (True, False)]
            self.second = [[hop(second, up, *self.at(a, 0), r) for up in (True, False)] for a in range(4)]
            self.last = [
                [hop(second, up, *self.at(a, 3 if up else 1), p[0 if up else 1]) for up in (True, False)]
                for a in range(4)
            ]

        def at(self, a, b):
            return (b, a) if self.swap else (a, b)

        def open(self, a):
            for copy in self.second[a]:
                copy.start()

        def got_first(self, i):
            a = (3, 1)[i]
            self.first[i].wait_recv()
            self.relay[i].start()
            self.open(a)
            cross(*self.at(a, 0), self.rows)

        def got_relay(self):
            for copy in self.relay:
                copy.wait_recv()
            self.open(2)
            cross(*self.at(2, 0), self.rows)

        def got_second(self, a):
            for i in range(2):
                self.second[a][i].wait_recv()
                self.last[a][i].start()
                cross(*self.at(a, (3, 1)[i]), self.rows)

        def got_last(self, a):
            for copy in self.last[a]:
                copy.wait_recv()
            cross(*self.at(a, 2), self.rows)

    def arrive(copies):
        for copy in copies:
            copy.wait_recv()

    low, high = Half("x", "y", 0), Half("y", "x", 64)
    halves = (low, high)
    for half in halves:
        for copy in half.first:
            copy.start()
    for half in halves:
        half.open(0)
    cross(0, 0, (0, PAIRS))

    for load in loads[1:]:
        load.wait()
    raw = jnp.dot(feats_ref[...], proj[...], preferred_element_type=F32)
    raw_ref[...] = raw
    inverse = lax.rsqrt(jnp.sum(raw * raw, axis=1, keepdims=True) + EPSILON)

    def image(index, rows=(0, PAIRS)):
        return images.at[index * PAIRS + rows[0]:index * PAIRS + rows[1], :]

    images[PAIRS:2 * PAIRS, :] = (raw * inverse).astype(BF16)
    up = [net.plan(image(a), image(b), z_up) for a, b in ((1, 7), (7, 5), (5, 3))]
    down = [net.plan(image(a), image(b), z_down) for a, b in ((1, 6), (6, 4), (4, 2))]
    up.append(net.plan(image(3, (0, 64)), image(0, (0, 64)), z_up))
    down.append(net.plan(image(2, (64, 128)), image(0, (64, 128)), z_down))
    up[0].start()
    down[0].start()

    def turn(step):
        for ring in (up, down):
            ring[step].wait_recv()
            if step < 3:
                ring[step + 1].start()

    owner_slot = (lax.rem(y, 2) * 2 + zl) * 2 + c
    zh2 = z - zl
    half_y = lax.div(y, 2)
    state_out = Scatter(
        net, state_ref, state_recv,
        [device(x, i % 4, zh2 + half_y, i // 4) for i in range(8)],
        [jnp.logical_and(zl == half_y, k == i) for i in range(8)],
        owner_slot,
    )

    for half in halves:
        half.got_first(0)
        half.got_first(1)
    for half in halves:
        half.got_second(0)
    turn(0)
    for half in halves:
        half.got_relay()
    for half in halves:
        half.got_last(0)
    for a in (3, 1):
        for half in halves:
            half.got_second(a)
    turn(1)
    for half in halves:
        half.got_second(2)
    for a in (3, 1):
        for half in halves:
            half.got_last(a)
    turn(2)
    for half in halves:
        half.got_last(2)
    turn(3)

    def feats_slot(ry, rows=(0, W)):
        return feats_all.at[rows[0]:rows[1], ry * PAIRS:(ry + 1) * PAIRS]

    feats_all[:, 0:PAIRS] = feats_ref[...].T
    feats_near = [net.plan(feats_slot(0), feats_slot(3), y_up), net.plan(feats_slot(0), feats_slot(1), y_down)]
    feats_far = [
        net.plan(feats_slot(3, (0, W // 2)), feats_slot(2, (0, W // 2)), y_up),
        net.plan(feats_slot(1, (W // 2, W)), feats_slot(2, (W // 2, W)), y_down),
    ]
    feats_cross = net.plan(feats_all.at[:, 0:512], feats_all.at[:, 512:1024], across)
    def feats_open():
        for copy in feats_near:
            copy.start()

    def feats_on():
        for near, far in zip(feats_near, feats_far):
            near.wait_recv()
            far.start()

    def feats_over():
        arrive(feats_far)
        feats_cross.start()

    pick = lax.broadcasted_iota(jnp.int32, (HALF, 128), 0) == lax.broadcasted_iota(
        jnp.int32, (HALF, 128), 1
    )

    def pack(dst, dst_row, full, unit):
        coefficient = jnp.sum(full * unit, axis=1, keepdims=True)
        dst[...] = (full - coefficient * unit).astype(BF16)
        row = jnp.sum(jnp.where(pick, coefficient, 0.0), axis=0, keepdims=True)
        dst_row[...] = jnp.broadcast_to(row, (8, 128))

    def unpack(src, src_row, unit):
        coefficient = jnp.sum(jnp.where(pick, src_row[0:1, :], 0.0), axis=1, keepdims=True)
        return src[...].astype(F32) + coefficient * unit

    class Side:
        def __init__(self, first, come, sends, recvs, send_rows, recv_rows, target):
            self.blocks, self.sends, self.recvs = (0, first, first + 2, first + 4), sends, recvs
            self.send_rows, self.recv_rows = send_rows, recv_rows
            self.rows = ((64 - come, 128 - come), (come, come + 64))
            self.copies = [
                (
                    net.plan(sends.at[i], recvs.at[i], target),
                    net.plan(send_rows.at[i], recv_rows.at[i], target),
                )
                for i in range(7)
            ]

        def take(self, i, unit):
            arrive(self.copies[i])
            return unpack(self.recvs.at[i], self.recv_rows.at[i], unit)

        def give(self, hop, late):
            i = 2 * hop - 1 + late
            base = self.blocks[hop] * PAIRS
            start, stop = self.rows[late]
            unit = images[base + start:base + stop, :].astype(F32)
            full = LOGIT_SCALE * acc[base + start:base + stop, :]
            if hop > 1 or (hop == 1 and late):
                full = full + self.take(i - 2, unit)
            pack(self.sends.at[i], self.send_rows.at[i], full, unit)
            for copy in self.copies[i]:
                copy.start()

    sides = (
        Side(2, 0, send_up, recv_up, send_up_row, recv_up_row, z_up),
        Side(3, 64, send_down, recv_down, send_down_row, recv_down_row, z_down),
    )

    def give(hop, late):
        for side in sides:
            side.give(hop, late)

    schedule = {
        (0, 0): [feats_open, state_out.start],
        (0, 2): [lambda: arrive(text_crossings)],
        (1, 0): [lambda: give(0, 1)],
        (1, 2): [feats_on],
        (2, 0): [lambda: give(1, 0), lambda: give(1, 1)],
        (2, 2): [feats_over],
        (3, 0): [lambda: give(2, 0)],
        (3, 1): [lambda: give(2, 1)],
    }
    acc[...] = jnp.zeros_like(acc)

    def grid_step(step, carry):
        rows = pl.ds(pl.multiple_of(step * IMAGES, IMAGES), IMAGES)
        buffers = (weigh0, weigh1)

        def weigh(n):
            cosine = lax.dot_general(
                images[rows, :], texts[n * CHUNK:(n + 1) * CHUNK, :],
                (((1,), (1,)), ((), ())), preferred_element_type=F32,
            )
            pair = 0.5 + 0.5 * jnp.tanh(0.5 * LOGIT_SCALE * cosine + 0.5 * LOGIT_BIAS)
            buffers[n % 2][...] = pair.astype(BF16)

        def fold(n):
            acc[rows, :] += jnp.dot(
                buffers[n % 2][...], texts[n * CHUNK:(n + 1) * CHUNK, :], preferred_element_type=F32
            )

        for n in range(TEXTS // CHUNK):
            for (at, part), events in schedule.items():
                if part == n:

                    @pl.when(step == at)
                    def _(events=events):
                        for event in events:
                            event()

            weigh(n)
            if n > 0:
                fold(n - 1)
        fold(TEXTS // CHUNK - 1)
        return carry

    lax.fori_loop(0, 4, grid_step, 0)
    give(3, 0)
    give(3, 1)
    unit = images[PAIRS:2 * PAIRS, :].astype(F32)
    text = texts[0:PAIRS, :].astype(F32)
    cosine = jnp.sum(unit * text, axis=1, keepdims=True)
    sigmoid = 0.5 + 0.5 * jnp.tanh(0.5 * LOGIT_SCALE * cosine + 0.5 * LOGIT_BIAS)
    change = (sigmoid - 1.0).astype(BF16).astype(F32) - sigmoid.astype(BF16).astype(F32)
    own_grad[...] = LOGIT_SCALE * (acc[PAIRS:2 * PAIRS, :] + change * text)

    state_out.wait()
    state_tile[...] = jnp.zeros_like(state_tile)
    for piece in range(8):
        first = 11 * (piece // 2) + 5 * (piece % 2)
        for a in range(3):
            state_tile[a, first:first + 6, :] += state_recv[piece, a, 0:6, :]

    raw = raw_ref[...]
    inverse = lax.rsqrt(jnp.sum(raw * raw, axis=1, keepdims=True) + EPSILON)
    feat_gram = lax.dot_general(
        feats_ref[...], feats_ref[...], (((1,), (1,)), ((), ())), preferred_element_type=F32
    )
    local_row = (ids_row[...] - (lax.axis_index("row") * 16 + col) * USERS).astype(F32)
    square_shape = (PAIRS, PAIRS)
    diagonal = lax.broadcasted_iota(jnp.int32, square_shape, 0) == lax.broadcasted_iota(
        jnp.int32, square_shape, 1
    )
    local_column = jnp.sum(jnp.where(diagonal, local_row, 0.0), axis=1, keepdims=True)
    same_user = local_column == local_row
    users = lax.broadcasted_iota(jnp.int32, (PAIRS, USERS), 1).astype(F32)
    bound = jnp.sum(jnp.where(local_column == users, norms_ref[...], 0.0), axis=1, keepdims=True)
    unit = images[PAIRS:2 * PAIRS, :].astype(F32)
    for late in range(2):
        for side in sides:
            start, stop = side.rows[late]
            own_grad[start:stop, :] += side.take(5 + late, unit[start:stop])
    unit_grad = own_grad[...]
    inner = jnp.sum(raw * unit_grad, axis=1, keepdims=True)
    embed_grad = inverse * unit_grad - inverse * inverse * inverse * raw * inner
    grad_gram = lax.dot_general(
        embed_grad, embed_grad, (((1,), (1,)), ((), ())),
        precision=lax.Precision.HIGHEST, preferred_element_type=F32,
    )
    terms = jnp.sum(jnp.where(same_user, feat_gram * grad_gram, 0.0), axis=0, keepdims=True)
    user_sq = jnp.sum(jnp.where(same_user, terms, 0.0), axis=1, keepdims=True)
    factor = bound / jnp.maximum(jnp.sqrt(user_sq), bound)
    clipped[...] = (factor * embed_grad).astype(BF16)

    def rows_of(core, ry):
        return clipped_all.at[(core * 4 + ry) * PAIRS:(core * 4 + ry + 1) * PAIRS, :]

    parts = []
    for o in range(1, Y):
        parts.append(net.push(clipped.at[:, lanes(c * 4 + shift(y, o, Y))], rows_of(0, 4 - o), at_y[o - 1]))
        parts.append(net.push(clipped.at[:, lanes(other * 4 + shift(y, o, Y))], rows_of(1, 4 - o), at_y_across[o - 1]))
    parts.append(net.push(clipped.at[:, lanes(other * 4 + y)], rows_of(1, 0), across))
    clipped_all[0:PAIRS, :] = clipped[:, lanes(k)]
    spread[...] = jnp.zeros_like(spread)
    feats_cross.wait_recv()
    for copy in parts:
        copy.wait_recv()

    def share(index):
        block = feats_all[pl.ds(pl.multiple_of(index * SHARE, 16), SHARE), :]
        part = jnp.dot(block, clipped_all[...], preferred_element_type=F32)
        for piece in range(Z):
            spread[piece * PADDED:piece * PADDED + BLOCK, :] = part[piece * BLOCK:(piece + 1) * BLOCK]
        return spread[...]

    moves = []
    for o in range(1, X):
        x_send[o - 1] = share(shift(x, o, X)).astype(BF16)
        moves.append(net.push(x_send.at[o - 1], x_recv.at[o - 1], at_x[o - 1]))
    total = share(x)
    for o in range(1, X):
        moves[o - 1].wait_recv()
        total = total + x_recv[o - 1].astype(F32)
    z_part[...] = total
    z_send[...] = total.astype(BF16)

    def rows(index):
        return pl.ds(pl.multiple_of(index * PADDED, 16), PADDED)

    moves = [
        net.push(z_send.at[rows(shift(z, o, Z)), :], z_recv.at[o - 1], at_z[o - 1])
        for o in range(1, Z)
    ]
    grad = z_part[rows(z), :]
    for o in range(1, Z):
        moves[o - 1].wait_recv()
        grad = grad + z_recv[o - 1].astype(F32)

    new_sum = state_tile[0] + grad
    update = new_sum + state_tile[1]
    for piece in range(8):
        first = 11 * (piece // 2) + 5 * (piece % 2)
        sums_send[piece] = new_sum[first:first + 8]

    square = jnp.sum((update * update).reshape(PADDED // 8, 8, 128), axis=0)
    at = 0
    for stage, targets in enumerate((at_z, at_x, at_y + [across] + at_y_across)):
        sq_send[stage] = square
        moves = [
            net.push(sq_send.at[stage], sq_recv.at[at + i], target)
            for i, target in enumerate(targets)
        ]
        for i, copy in enumerate(moves):
            copy.wait_recv()
            square = square + sq_recv[at + i]
        at += len(targets)
    norm = jnp.sqrt(jnp.sum(square, keepdims=True))
    cap = math.sqrt(W * E)
    shrink = cap / jnp.maximum(norm, cap)
    tile = (state_tile[2] - RATE * shrink * update).astype(BF16)

    z_tiles[rows(z), :] = tile
    moves = [net.push(z_tiles.at[rows(z), :], z_tiles.at[rows(z), :], target) for target in at_z]
    sums_out = Scatter(
        net, sums_send, sums_ref,
        [device(x, 2 * zl + i // 4, zh2 + (i // 2) % 2, i % 2) for i in range(8)],
        [
            jnp.logical_and(half_y == zl, owner_slot == i) for i in range(8)
        ],
        k,
    )
    sums_out.start()
    for copy in moves:
        copy.wait_recv()
    whole = z_tiles[...].astype(F32)
    whole = jnp.concatenate([whole[piece * PADDED:piece * PADDED + BLOCK] for piece in range(Z)], axis=0)
    weights_ref[x, :, lanes(k)] = whole.astype(BF16)

    half = SHARE // 2

    def low_piece(index, rows=(0, half)):
        return weights_ref.at[index, rows[0]:rows[1], lanes(c, 512)]

    def high_piece(away, shares=slice(0, X)):
        return weights_ref.at[shares, half:SHARE, lanes(c * 4 + shift(y, away, Y))]

    def send(piece, target):
        return net.push(piece, piece, target)

    moves_y = [send(weights_ref.at[x, 0:half, lanes(k)], target) for target in at_y]
    moves_x = [send(weights_ref.at[x, half:SHARE, lanes(k)], target) for target in at_x]
    arrive(moves_y)
    low_moves = [send(low_piece(x), target) for target in (x_up, x_down)]
    arrive(moves_x)
    high_moves = [send(high_piece(0), target) for target in (y_up, y_down)]
    given = [send(low_piece(x), across), send(high_piece(0), across)]
    far = []
    for copy, away, rows_sent, target in (
        (low_moves[0], 3, (0, 96), x_up), (low_moves[1], 1, (96, half), x_down)
    ):
        copy.wait_recv()
        index = shift(x, away, X)
        far.append(send(low_piece(index, rows_sent), target))
        given.append(send(low_piece(index), across))
    for copy, away, shares, target in (
        (high_moves[0], 3, slice(0, 2), y_up), (high_moves[1], 1, slice(2, 4), y_down)
    ):
        copy.wait_recv()
        far.append(send(high_piece(away, shares), target))
        given.append(send(high_piece(away), across))
    arrive(far)
    given += [send(low_piece(shift(x, 2, X)), across), send(high_piece(2), across)]
    arrive(given)
    sums_out.wait()
    state_out.wait_sent()
    sums_out.wait_sent()
    net.finish()


def body(
    image_feats, text_emb, projection, clip_norms, user_ids, grad_sum, init_weights, tree_noise
):
    c = lax.rem(lax.axis_index("col"), 2)
    state = jnp.pad(jnp.stack([grad_sum, tree_noise, init_weights]), ((0, 0), (4, 4), (0, 0)))
    state = lax.dynamic_slice(state, (0, 4 - 4 * c, 0), (3, 48, 128))
    state = state.reshape(3, 6, 8, 128).transpose(2, 0, 1, 3)
    state = jnp.pad(state, ((0, 0), (0, 0), (0, 2), (0, 0)))
    vmem = pl.BlockSpec(memory_space=pltpu.VMEM)
    weights, sums = pl.pallas_call(
        kernel,
        out_shape=(
            jax.ShapeDtypeStruct((X, SHARE, E), BF16),
            jax.ShapeDtypeStruct((8, 8, 128), F32),
        ),
        in_specs=[pl.BlockSpec(memory_space=pl.ANY)] * 6,
        out_specs=(vmem, vmem),
        scratch_shapes=[
            pltpu.VMEM((PAIRS, W), BF16),
            pltpu.VMEM((PAIRS, E), BF16),
            pltpu.VMEM((1, USERS), F32),
            pltpu.VMEM((1, PAIRS), jnp.int32),
            pltpu.VMEM((8, 3, 8, 128), F32),
            pltpu.VMEM((W, E), BF16),
            pltpu.VMEM((TEXTS, E), BF16),
            pltpu.VMEM((Z * PAIRS, E), BF16),
            pltpu.VMEM((PAIRS, E), F32),
            pltpu.VMEM((Z * PAIRS, E), F32),
            pltpu.VMEM((PAIRS, E), F32),
            pltpu.VMEM((IMAGES, CHUNK), BF16),
            pltpu.VMEM((IMAGES, CHUNK), BF16),
            pltpu.VMEM((7, HALF, E), BF16),
            pltpu.VMEM((7, HALF, E), BF16),
            pltpu.VMEM((7, HALF, E), BF16),
            pltpu.VMEM((7, HALF, E), BF16),
            pltpu.VMEM((7, 8, 128), F32),
            pltpu.VMEM((7, 8, 128), F32),
            pltpu.VMEM((7, 8, 128), F32),
            pltpu.VMEM((7, 8, 128), F32),
            pltpu.VMEM((W, 8 * PAIRS), BF16),
            pltpu.VMEM((PAIRS, E), BF16),
            pltpu.VMEM((8 * PAIRS, 128), BF16),
            pltpu.VMEM((WIDE, 128), F32),
            pltpu.VMEM((X - 1, WIDE, 128), BF16),
            pltpu.VMEM((X - 1, WIDE, 128), BF16),
            pltpu.VMEM((WIDE, 128), F32),
            pltpu.VMEM((WIDE, 128), BF16),
            pltpu.VMEM((Z - 1, PADDED, 128), BF16),
            pltpu.VMEM((WIDE, 128), BF16),
            pltpu.VMEM((8, 3, 8, 128), F32),
            pltpu.VMEM((3, PADDED, 128), F32),
            pltpu.VMEM((8, 8, 128), F32),
            pltpu.VMEM((3, 8, 128), F32),
            pltpu.VMEM((17, 8, 128), F32),
            pltpu.SemaphoreType.DMA((6,)),
            pltpu.SemaphoreType.DMA((COPIES,)),
            pltpu.SemaphoreType.DMA((COPIES,)),
        ],
        compiler_params=pltpu.CompilerParams(
            collective_id=1, has_side_effects=True, vmem_limit_bytes=48 * 1024 * 1024
        ),
    )(
        image_feats, text_emb, projection, clip_norms.reshape(1, USERS),
        user_ids.reshape(1, PAIRS), state,
    )
    sums = sums[:, :6].transpose(1, 0, 2).reshape(48, 128)
    return weights.reshape(W, E), lax.dynamic_slice(sums, (4 * c, 0), (44, 128))


def solution(mesh):
    in_specs = (
        P(("row", "col"), None),
        P(("row", "col"), None),
        P(),
        P(("row", "col")),
        P(("row", "col")),
        P(("row", "col"), None),
        P(("row", "col"), None),
        P(("row", "col"), None),
    )
    out_specs = (P(), P(("row", "col"), None))
    return jax.shard_map(body, mesh=mesh, in_specs=in_specs, out_specs=out_specs, check_vma=False)
```

```python
import math

import jax
import jax.numpy as jnp
from jax import lax
from jax.experimental import pallas as pl
from jax.experimental.pallas import tpu as pltpu
from jax.sharding import PartitionSpec as P

LOGIT_SCALE = 32.0
LOGIT_BIAS = -5.0
RATE = 0.5
EPSILON = 1e-06

MESH = pl.DeviceIdType.MESH
X, Y, Z = 4, 4, 8
W, E, PAIRS, USERS = 1408, 1024, 128, 16
SHARE = W // X
BLOCK = SHARE // Z
PADDED = 48
WIDE = Z * PADDED
TEXTS = 2 * X * Y * PAIRS
CHUNK = 1024
IMAGES = 2 * PAIRS
HALF = PAIRS // 2
COPIES = 256
F32, BF16 = jnp.float32, jnp.bfloat16


def place():
    row, col = lax.axis_index("row"), lax.axis_index("col")
    x, zh = lax.div(row, 4), lax.rem(row, 4)
    y, zl, c = lax.div(col, 4), lax.rem(lax.div(col, 2), 2), lax.rem(col, 2)
    return x, y, zh * 2 + zl, c


def device(x, y, z, c):
    return (x * 4 + lax.div(z, 2), y * 4 + lax.rem(z, 2) * 2 + c)


def shift(value, by, size):
    return lax.rem(value + by, size)


class Copies:
    def __init__(self, send_sems, recv_sems):
        self.send_sems, self.recv_sems, self.used, self.all = send_sems, recv_sems, 0, []

    def reserve(self, count):
        self.used += count
        return self.used - count

    def make(self, src, dst, target, send_at, recv_at):
        return pltpu.make_async_remote_copy(
            src_ref=src,
            dst_ref=dst,
            send_sem=self.send_sems.at[send_at],
            recv_sem=self.recv_sems.at[recv_at],
            device_id=target,
            device_id_type=MESH,
        )

    def plan(self, src, dst, target):
        at = self.reserve(1)
        copy = self.make(src, dst, target, at, at)
        self.all.append(copy)
        return copy

    def push(self, src, dst, target):
        copy = self.plan(src, dst, target)
        copy.start()
        return copy

    def finish(self):
        for copy in self.all:
            copy.wait_send()


class Scatter:
    def __init__(self, net, src, dst, targets, is_self, mine):
        self.net, self.src, self.dst, self.targets, self.is_self, self.mine = net, src, dst, targets, is_self, mine
        self.at = net.reserve(8)

    def remote(self, i):
        return self.net.make(
            self.src.at[i], self.dst.at[self.mine], self.targets[i], self.at + i, self.at + self.mine
        )

    def local(self, i):
        sem = self.net.recv_sems.at[self.at + self.mine]
        return pltpu.make_async_copy(self.src.at[i], self.dst.at[self.mine], sem)

    def start(self):
        for i in range(8):
            pl.when(jnp.logical_not(self.is_self[i]))(self.remote(i).start)
            pl.when(self.is_self[i])(self.local(i).start)

    def wait(self):
        for i in range(8):
            self.net.make(self.src.at[i], self.dst.at[i], self.targets[i], self.at + i, self.at + i).wait_recv()

    def wait_sent(self):
        for i in range(8):
            pl.when(jnp.logical_not(self.is_self[i]))(self.remote(i).wait_send)


def kernel(
    feats_hbm, text_hbm, proj_hbm, norms_hbm, ids_hbm, state_hbm,
    weights_ref, sums_ref,
    feats_ref, text_ref, norms_ref, ids_row, state_ref, proj, texts, images, raw_ref, acc, own_grad, weigh0, weigh1,
    send_up, send_down, recv_up, recv_down, send_up_row, send_down_row, recv_up_row, recv_down_row,
    feats_all, clipped, clipped_all, shares, shares_send, x_recv, x_part, x_send, x_recv_last,
    z_recv, z_send, z_recv_last, z_tiles,
    state_recv, state_tile, sums_send, sq_send, sq_recv,
    load_sems, send_sems, recv_sems,
):
    x, y, z, c = place()
    col = lax.axis_index("col")
    k = c * 4 + y
    other = 1 - c
    zl = lax.rem(z, 2)
    at_x = [device(shift(x, o, X), y, z, c) for o in range(1, X)]
    at_y = [device(x, shift(y, o, Y), z, c) for o in range(1, Y)]
    at_z = [device(x, y, shift(z, o, Z), c) for o in range(1, Z)]
    across = device(x, y, z, other)
    at_y_across = [device(x, shift(y, o, Y), z, other) for o in range(1, Y)]
    flip = z + 1 - 2 * zl
    at_flip = [device(x, shift(y, o, Y), flip, cc) for o in range(Y) for cc in (c, other)][1:]
    x_up, x_down, y_up, y_down, z_up, z_down = at_x[0], at_x[2], at_y[0], at_y[2], at_z[0], at_z[6]

    loads = [
        pltpu.make_async_copy(src, dst, load_sems.at[i])
        for i, (src, dst) in enumerate((
            (text_hbm, text_ref), (feats_hbm, feats_ref), (proj_hbm, proj),
            (state_hbm, state_ref), (norms_hbm, norms_ref), (ids_hbm, ids_row),
        ))
    ]
    for load in loads:
        load.start()
    loads[0].wait()
    text = text_ref[...].astype(F32)
    texts[0:PAIRS, :] = (
        text * lax.rsqrt(jnp.sum(text * text, axis=1, keepdims=True) + EPSILON)
    ).astype(BF16)

    barrier = pltpu.get_barrier_semaphore()
    partners = at_x + at_y + at_z + [across] + at_y_across + at_flip
    for target in partners:
        pl.semaphore_signal(barrier, inc=1, device_id=target, device_id_type=MESH)
    pl.semaphore_wait(barrier, len(partners))
    net = Copies(send_sems, recv_sems)

    def lanes(index, width=128):
        return pl.ds(pl.multiple_of(index * width, width), width)

    def slot(rx, ry, rows, core=0):
        base = (core * 16 + rx * 4 + ry) * PAIRS
        return texts.at[base + rows[0]:base + rows[1], :]

    def hop(axis, up, rx, ry, rows):
        step = 3 if up else 1
        if axis == "x":
            return net.plan(slot(rx, ry, rows), slot((rx + step) % 4, ry, rows), x_up if up else x_down)
        return net.plan(slot(rx, ry, rows), slot(rx, (ry + step) % 4, rows), y_up if up else y_down)

    text_crossings = []

    def cross(rx, ry, rows):
        text_crossings.append(net.push(slot(rx, ry, rows), slot(rx, ry, rows, 1), across))

    class Half:
        def __init__(self, first, second, low):
            self.rows, self.swap = (low, low + 64), first == "y"
            self.parts = ((low, low + 32), (low + 32, low + 64))
            r, p = self.rows, self.parts
            self.first = [hop(first, up, 0, 0, r) for up in (True, False)]
            self.relay = [hop(first, up, *self.at(3 if up else 1, 0), p[0 if up else 1]) for up in (True, False)]
            self.second = [[hop(second, up, *self.at(a, 0), r) for up in (True, False)] for a in range(4)]
            self.last = [
                [hop(second, up, *self.at(a, 3 if up else 1), p[0 if up else 1]) for up in (True, False)]
                for a in range(4)
            ]

        def at(self, a, b):
            return (b, a) if self.swap else (a, b)

        def open(self, a):
            for copy in self.second[a]:
                copy.start()

        def got_first(self, i):
            a = (3, 1)[i]
            self.first[i].wait_recv()
            self.relay[i].start()
            self.open(a)
            cross(*self.at(a, 0), self.rows)

        def got_relay(self):
            for copy in self.relay:
                copy.wait_recv()
            self.open(2)
            cross(*self.at(2, 0), self.rows)

        def got_second(self, a):
            for i in range(2):
                self.second[a][i].wait_recv()
                self.last[a][i].start()
                cross(*self.at(a, (3, 1)[i]), self.rows)

        def got_last(self, a):
            for copy in self.last[a]:
                copy.wait_recv()
            cross(*self.at(a, 2), self.rows)

    def arrive(copies):
        for copy in copies:
            copy.wait_recv()

    low, high = Half("x", "y", 0), Half("y", "x", 64)
    halves = (low, high)
    for half in halves:
        for copy in half.first:
            copy.start()
    for half in halves:
        half.open(0)
    cross(0, 0, (0, PAIRS))

    for load in loads[1:]:
        load.wait()
    raw = jnp.dot(feats_ref[...], proj[...], preferred_element_type=F32)
    raw_ref[...] = raw
    inverse = lax.rsqrt(jnp.sum(raw * raw, axis=1, keepdims=True) + EPSILON)

    def image(index, rows=(0, PAIRS)):
        return images.at[index * PAIRS + rows[0]:index * PAIRS + rows[1], :]

    images[PAIRS:2 * PAIRS, :] = (raw * inverse).astype(BF16)
    up = [net.plan(image(a), image(b), z_up) for a, b in ((1, 7), (7, 5), (5, 3))]
    down = [net.plan(image(a), image(b), z_down) for a, b in ((1, 6), (6, 4), (4, 2))]
    up.append(net.plan(image(3, (0, 64)), image(0, (0, 64)), z_up))
    down.append(net.plan(image(2, (64, 128)), image(0, (64, 128)), z_down))
    up[0].start()
    down[0].start()

    feats_all[:, 0:PAIRS] = feats_ref[...].T
    acc[...] = jnp.zeros_like(acc)
    shares[...] = jnp.zeros_like(shares)
    feat_gram = lax.dot_general(
        feats_ref[...], feats_ref[...], (((1,), (1,)), ((), ())), preferred_element_type=F32
    )
    local_row = (ids_row[...] - (lax.axis_index("row") * 16 + col) * USERS).astype(F32)
    square_shape = (PAIRS, PAIRS)
    diagonal = lax.broadcasted_iota(jnp.int32, square_shape, 0) == lax.broadcasted_iota(
        jnp.int32, square_shape, 1
    )
    local_column = jnp.sum(jnp.where(diagonal, local_row, 0.0), axis=1, keepdims=True)
    same_user = local_column == local_row
    users = lax.broadcasted_iota(jnp.int32, (PAIRS, USERS), 1).astype(F32)
    bound = jnp.sum(jnp.where(local_column == users, norms_ref[...], 0.0), axis=1, keepdims=True)
    feat_gram = jnp.where(same_user, feat_gram, 0.0)

    def turn(step):
        for ring in (up, down):
            ring[step].wait_recv()
            if step < 3:
                ring[step + 1].start()

    owner_slot = (lax.rem(y, 2) * 2 + zl) * 2 + c
    zh2 = z - zl
    half_y = lax.div(y, 2)
    state_out = Scatter(
        net, state_ref, state_recv,
        [device(x, i % 4, zh2 + half_y, i // 4) for i in range(8)],
        [jnp.logical_and(zl == half_y, k == i) for i in range(8)],
        owner_slot,
    )

    for half in halves:
        half.got_first(0)
        half.got_first(1)
    for half in halves:
        half.got_second(0)
    turn(0)
    for half in halves:
        half.got_relay()
    for half in halves:
        half.got_last(0)
    for a in (3, 1):
        for half in halves:
            half.got_second(a)
    turn(1)
    for half in halves:
        half.got_second(2)
    for a in (3, 1):
        for half in halves:
            half.got_last(a)
    turn(2)
    for half in halves:
        half.got_last(2)
    turn(3)

    def feats_slot(ry, rows=(0, W)):
        return feats_all.at[rows[0]:rows[1], ry * PAIRS:(ry + 1) * PAIRS]

    feats_near = [net.plan(feats_slot(0), feats_slot(3), y_up), net.plan(feats_slot(0), feats_slot(1), y_down)]
    feats_far = [
        net.plan(feats_slot(3, (0, W // 2)), feats_slot(2, (0, W // 2)), y_up),
        net.plan(feats_slot(1, (W // 2, W)), feats_slot(2, (W // 2, W)), y_down),
    ]
    feats_cross = net.plan(feats_all.at[:, 0:512], feats_all.at[:, 512:1024], across)
    def feats_open():
        for copy in feats_near:
            copy.start()

    def feats_on():
        for near, far in zip(feats_near, feats_far):
            near.wait_recv()
            far.start()

    def feats_over():
        arrive(feats_far)
        feats_cross.start()

    pick = lax.broadcasted_iota(jnp.int32, (HALF, 128), 0) == lax.broadcasted_iota(
        jnp.int32, (HALF, 128), 1
    )

    def pack(dst, dst_row, full, unit):
        coefficient = jnp.sum(full * unit, axis=1, keepdims=True)
        dst[...] = (full - coefficient * unit).astype(BF16)
        row = jnp.sum(jnp.where(pick, coefficient, 0.0), axis=0, keepdims=True)
        dst_row[...] = jnp.broadcast_to(row, (8, 128))

    def unpack(src, src_row, unit):
        coefficient = jnp.sum(jnp.where(pick, src_row[0:1, :], 0.0), axis=1, keepdims=True)
        return src[...].astype(F32) + coefficient * unit

    class Side:
        def __init__(self, first, come, sends, recvs, send_rows, recv_rows, target):
            self.blocks, self.sends, self.recvs = (0, first, first + 2, first + 4), sends, recvs
            self.send_rows, self.recv_rows = send_rows, recv_rows
            self.rows = ((64 - come, 128 - come), (come, come + 64))
            self.copies = [
                (
                    net.plan(sends.at[i], recvs.at[i], target),
                    net.plan(send_rows.at[i], recv_rows.at[i], target),
                )
                for i in range(7)
            ]

        def take(self, i, unit):
            arrive(self.copies[i])
            return unpack(self.recvs.at[i], self.recv_rows.at[i], unit)

        def give(self, hop, late):
            i = 2 * hop - 1 + late
            base = self.blocks[hop] * PAIRS
            start, stop = self.rows[late]
            unit = images[base + start:base + stop, :].astype(F32)
            full = LOGIT_SCALE * acc[base + start:base + stop, :]
            if hop > 1 or (hop == 1 and late):
                full = full + self.take(i - 2, unit)
            pack(self.sends.at[i], self.send_rows.at[i], full, unit)
            for copy in self.copies[i]:
                copy.start()

    sides = (
        Side(2, 0, send_up, recv_up, send_up_row, recv_up_row, z_up),
        Side(3, 64, send_down, recv_down, send_down_row, recv_down_row, z_down),
    )

    def give(hop, late):
        for side in sides:
            side.give(hop, late)

    schedule = {
        (0, 0): [feats_open, state_out.start],
        (0, 2): [lambda: arrive(text_crossings)],
        (1, 0): [lambda: give(0, 1)],
        (1, 2): [feats_on],
        (2, 0): [lambda: give(1, 0), lambda: give(1, 1)],
        (2, 2): [feats_over],
        (3, 0): [lambda: give(2, 0)],
        (3, 1): [lambda: give(2, 1)],
    }

    def grid_step(step, carry):
        rows = pl.ds(pl.multiple_of(step * IMAGES, IMAGES), IMAGES)
        buffers = (weigh0, weigh1)

        def weigh(n):
            cosine = lax.dot_general(
                images[rows, :], texts[n * CHUNK:(n + 1) * CHUNK, :],
                (((1,), (1,)), ((), ())), preferred_element_type=F32,
            )
            pair = 0.5 + 0.5 * jnp.tanh(0.5 * LOGIT_SCALE * cosine + 0.5 * LOGIT_BIAS)
            buffers[n % 2][...] = pair.astype(BF16)

        def fold(n):
            acc[rows, :] += jnp.dot(
                buffers[n % 2][...], texts[n * CHUNK:(n + 1) * CHUNK, :], preferred_element_type=F32
            )

        for n in range(TEXTS // CHUNK):
            for (at, part), events in schedule.items():
                if part == n:

                    @pl.when(step == at)
                    def _(events=events):
                        for event in events:
                            event()

            weigh(n)
            if n > 0:
                fold(n - 1)
        fold(TEXTS // CHUNK - 1)
        return carry

    lax.fori_loop(0, 4, grid_step, 0)
    give(3, 0)
    give(3, 1)
    unit = images[PAIRS:2 * PAIRS, :].astype(F32)
    text = texts[0:PAIRS, :].astype(F32)
    cosine = jnp.sum(unit * text, axis=1, keepdims=True)
    sigmoid = 0.5 + 0.5 * jnp.tanh(0.5 * LOGIT_SCALE * cosine + 0.5 * LOGIT_BIAS)
    change = (sigmoid - 1.0).astype(BF16).astype(F32) - sigmoid.astype(BF16).astype(F32)
    own_grad[...] = LOGIT_SCALE * (acc[PAIRS:2 * PAIRS, :] + change * text)

    state_out.wait()
    state_tile[...] = jnp.zeros_like(state_tile)
    for piece in range(8):
        first = 11 * (piece // 2) + 5 * (piece % 2)
        for a in range(3):
            state_tile[a, first:first + 6, :] += state_recv[piece, a, 0:6, :]

    raw = raw_ref[...]
    unit = images[PAIRS:2 * PAIRS, :].astype(F32)
    for late in range(2):
        for side in sides:
            start, stop = side.rows[late]
            own_grad[start:stop, :] += side.take(5 + late, unit[start:stop])
    unit_grad = own_grad[...]
    inner = jnp.sum(raw * unit_grad, axis=1, keepdims=True)
    embed_grad = inverse * unit_grad - inverse * inverse * inverse * raw * inner
    grad_gram = lax.dot_general(
        embed_grad, embed_grad, (((1,), (1,)), ((), ())),
        precision=lax.Precision.HIGHEST, preferred_element_type=F32,
    )
    terms = jnp.sum(feat_gram * grad_gram, axis=0, keepdims=True)
    user_sq = jnp.sum(jnp.where(same_user, terms, 0.0), axis=1, keepdims=True)
    factor = bound / jnp.maximum(jnp.sqrt(user_sq), bound)
    clipped[...] = (factor * embed_grad).astype(BF16)

    def rows_of(core, ry):
        return clipped_all.at[(core * 4 + ry) * PAIRS:(core * 4 + ry + 1) * PAIRS, :]

    parts = []
    for o in range(1, Y):
        parts.append(net.push(clipped.at[:, lanes(c * 4 + shift(y, o, Y))], rows_of(0, 4 - o), at_y[o - 1]))
        parts.append(net.push(clipped.at[:, lanes(other * 4 + shift(y, o, Y))], rows_of(1, 4 - o), at_y_across[o - 1]))
    parts.append(net.push(clipped.at[:, lanes(other * 4 + y)], rows_of(1, 0), across))
    clipped_all[0:PAIRS, :] = clipped[:, lanes(k)]
    feats_cross.wait_recv()
    for copy in parts:
        copy.wait_recv()

    def rows(index):
        return pl.ds(pl.multiple_of(index * PADDED, 16), PADDED)

    x_moves = []
    for o in (1, 2, 3, 0):
        block = feats_all[pl.ds(pl.multiple_of(shift(x, o, X) * SHARE, 16), SHARE), :]
        part = jnp.dot(block, clipped_all[...], preferred_element_type=F32)
        for piece in range(Z):
            shares[o, piece, 0:BLOCK, :] = part[piece * BLOCK:(piece + 1) * BLOCK]
        shares_send[o] = shares[o].astype(BF16)
        if o:
            x_moves.append(net.push(shares_send.at[o, :, 0:32, :], x_recv.at[o - 1], at_x[o - 1]))
    z_moves = [
        net.push(shares_send.at[:, shift(z, o, Z), 32:PADDED, :], z_recv.at[o - 1], at_z[o - 1])
        for o in range(1, Z)
    ]
    total = shares[0, :, 0:32, :]
    for o in range(1, X):
        x_moves[o - 1].wait_recv()
        total = total + x_recv[o - 1].astype(F32)
    x_part[...] = total
    x_send[...] = total.astype(BF16)
    x_moves = [
        net.push(x_send.at[shift(z, o, Z)], x_recv_last.at[o - 1], at_z[o - 1]) for o in range(1, Z)
    ]
    total = shares[:, z, 32:PADDED, :]
    for o in range(1, Z):
        z_moves[o - 1].wait_recv()
        total = total + z_recv[o - 1].astype(F32)
    z_send[...] = total.astype(BF16)
    z_moves = [net.push(z_send.at[o], z_recv_last.at[o - 1], at_x[o - 1]) for o in range(1, X)]
    upper, lower = x_part[z], total[0]
    for o in range(1, X):
        z_moves[o - 1].wait_recv()
        lower = lower + z_recv_last[o - 1].astype(F32)
    for o in range(1, Z):
        x_moves[o - 1].wait_recv()
        upper = upper + x_recv_last[o - 1].astype(F32)
    grad = jnp.concatenate([upper, lower], axis=0)

    new_sum = state_tile[0] + grad
    update = new_sum + state_tile[1]
    for piece in range(8):
        first = 11 * (piece // 2) + 5 * (piece % 2)
        sums_send[piece] = new_sum[first:first + 8]

    square = jnp.sum((update * update).reshape(PADDED // 8, 8, 128), axis=0)
    at = 0
    for stage, targets in enumerate((at_z, at_x, at_y + [across] + at_y_across)):
        sq_send[stage] = square
        moves = [
            net.push(sq_send.at[stage], sq_recv.at[at + i], target)
            for i, target in enumerate(targets)
        ]
        for i, copy in enumerate(moves):
            copy.wait_recv()
            square = square + sq_recv[at + i]
        at += len(targets)
    norm = jnp.sqrt(jnp.sum(square, keepdims=True))
    cap = math.sqrt(W * E)
    shrink = cap / jnp.maximum(norm, cap)
    tile = (state_tile[2] - RATE * shrink * update).astype(BF16)

    z_tiles[rows(z), :] = tile
    moves = [net.push(z_tiles.at[rows(z), :], z_tiles.at[rows(z), :], target) for target in at_z]
    sums_out = Scatter(
        net, sums_send, sums_ref,
        [device(x, 2 * zl + i // 4, zh2 + (i // 2) % 2, i % 2) for i in range(8)],
        [
            jnp.logical_and(half_y == zl, owner_slot == i) for i in range(8)
        ],
        k,
    )
    sums_out.start()
    for copy in moves:
        copy.wait_recv()
    whole = z_tiles[...].astype(F32)
    whole = jnp.concatenate([whole[piece * PADDED:piece * PADDED + BLOCK] for piece in range(Z)], axis=0)
    weights_ref[x, :, lanes(k)] = whole.astype(BF16)

    half = SHARE // 2

    def low_piece(index, rows=(0, half)):
        return weights_ref.at[index, rows[0]:rows[1], lanes(c, 512)]

    def high_piece(away, shares=slice(0, X)):
        return weights_ref.at[shares, half:SHARE, lanes(c * 4 + shift(y, away, Y))]

    def send(piece, target):
        return net.push(piece, piece, target)

    moves_y = [send(weights_ref.at[x, 0:half, lanes(k)], target) for target in at_y]
    moves_x = [send(weights_ref.at[x, half:SHARE, lanes(k)], target) for target in at_x]
    arrive(moves_y)
    low_moves = [send(low_piece(x), target) for target in (x_up, x_down)]
    arrive(moves_x)
    high_moves = [send(high_piece(0), target) for target in (y_up, y_down)]
    given = [send(low_piece(x), across), send(high_piece(0), across)]
    far = []
    for copy, away, rows_sent, target in (
        (low_moves[0], 3, (0, 96), x_up), (low_moves[1], 1, (96, half), x_down)
    ):
        copy.wait_recv()
        index = shift(x, away, X)
        far.append(send(low_piece(index, rows_sent), target))
        given.append(send(low_piece(index), across))
    for copy, away, shares, target in (
        (high_moves[0], 3, slice(0, 2), y_up), (high_moves[1], 1, slice(2, 4), y_down)
    ):
        copy.wait_recv()
        far.append(send(high_piece(away, shares), target))
        given.append(send(high_piece(away), across))
    arrive(far)
    given += [send(low_piece(shift(x, 2, X)), across), send(high_piece(2), across)]
    arrive(given)
    sums_out.wait()
    state_out.wait_sent()
    sums_out.wait_sent()
    net.finish()


def body(
    image_feats, text_emb, projection, clip_norms, user_ids, grad_sum, init_weights, tree_noise
):
    c = lax.rem(lax.axis_index("col"), 2)
    state = jnp.pad(jnp.stack([grad_sum, tree_noise, init_weights]), ((0, 0), (4, 4), (0, 0)))
    state = lax.dynamic_slice(state, (0, 4 - 4 * c, 0), (3, 48, 128))
    state = state.reshape(3, 6, 8, 128).transpose(2, 0, 1, 3)
    state = jnp.pad(state, ((0, 0), (0, 0), (0, 2), (0, 0)))
    vmem = pl.BlockSpec(memory_space=pltpu.VMEM)
    weights, sums = pl.pallas_call(
        kernel,
        out_shape=(
            jax.ShapeDtypeStruct((X, SHARE, E), BF16),
            jax.ShapeDtypeStruct((8, 8, 128), F32),
        ),
        in_specs=[pl.BlockSpec(memory_space=pltpu.HBM)] * 6,
        out_specs=(vmem, vmem),
        scratch_shapes=[
            pltpu.VMEM((PAIRS, W), BF16),
            pltpu.VMEM((PAIRS, E), BF16),
            pltpu.VMEM((1, USERS), F32),
            pltpu.VMEM((1, PAIRS), jnp.int32),
            pltpu.VMEM((8, 3, 8, 128), F32),
            pltpu.VMEM((W, E), BF16),
            pltpu.VMEM((TEXTS, E), BF16),
            pltpu.VMEM((Z * PAIRS, E), BF16),
            pltpu.VMEM((PAIRS, E), F32),
            pltpu.VMEM((Z * PAIRS, E), F32),
            pltpu.VMEM((PAIRS, E), F32),
            pltpu.VMEM((IMAGES, CHUNK), BF16),
            pltpu.VMEM((IMAGES, CHUNK), BF16),
            pltpu.VMEM((7, HALF, E), BF16),
            pltpu.VMEM((7, HALF, E), BF16),
            pltpu.VMEM((7, HALF, E), BF16),
            pltpu.VMEM((7, HALF, E), BF16),
            pltpu.VMEM((7, 8, 128), F32),
            pltpu.VMEM((7, 8, 128), F32),
            pltpu.VMEM((7, 8, 128), F32),
            pltpu.VMEM((7, 8, 128), F32),
            pltpu.VMEM((W, 8 * PAIRS), BF16),
            pltpu.VMEM((PAIRS, E), BF16),
            pltpu.VMEM((8 * PAIRS, 128), BF16),
            pltpu.VMEM((X, Z, PADDED, 128), F32),
            pltpu.VMEM((X, Z, PADDED, 128), BF16),
            pltpu.VMEM((X - 1, Z, 32, 128), BF16),
            pltpu.VMEM((Z, 32, 128), F32),
            pltpu.VMEM((Z, 32, 128), BF16),
            pltpu.VMEM((Z - 1, 32, 128), BF16),
            pltpu.VMEM((Z - 1, X, 16, 128), BF16),
            pltpu.VMEM((X, 16, 128), BF16),
            pltpu.VMEM((X - 1, 16, 128), BF16),
            pltpu.VMEM((WIDE, 128), BF16),
            pltpu.VMEM((8, 3, 8, 128), F32),
            pltpu.VMEM((3, PADDED, 128), F32),
            pltpu.VMEM((8, 8, 128), F32),
            pltpu.VMEM((3, 8, 128), F32),
            pltpu.VMEM((17, 8, 128), F32),
            pltpu.SemaphoreType.DMA((6,)),
            pltpu.SemaphoreType.DMA((COPIES,)),
            pltpu.SemaphoreType.DMA((COPIES,)),
        ],
        compiler_params=pltpu.CompilerParams(
            collective_id=1, has_side_effects=True, vmem_limit_bytes=48 * 1024 * 1024
        ),
    )(
        image_feats, text_emb, projection, clip_norms.reshape(1, USERS),
        user_ids.reshape(1, PAIRS), state,
    )
    sums = sums[:, :6].transpose(1, 0, 2).reshape(48, 128)
    return weights.reshape(W, E), lax.dynamic_slice(sums, (4 * c, 0), (44, 128))


def solution(mesh):
    in_specs = (
        P(("row", "col"), None),
        P(("row", "col"), None),
        P(),
        P(("row", "col")),
        P(("row", "col")),
        P(("row", "col"), None),
        P(("row", "col"), None),
        P(("row", "col"), None),
    )
    out_specs = (P(), P(("row", "col"), None))
    return jax.shard_map(body, mesh=mesh, in_specs=in_specs, out_specs=out_specs, check_vma=False)
```

```python
import math

import jax
import jax.numpy as jnp
from jax import lax
from jax.experimental import pallas as pl
from jax.experimental.pallas import tpu as pltpu
from jax.sharding import PartitionSpec as P

LOGIT_SCALE = 32.0
LOGIT_BIAS = -5.0
RATE = 0.5
EPSILON = 1e-06

MESH = pl.DeviceIdType.MESH
X, Y, Z = 4, 4, 8
W, E, PAIRS, USERS = 1408, 1024, 128, 16
SHARE = W // X
BLOCK = SHARE // Z
PADDED = 48
WIDE = Z * PADDED
TEXTS = 2 * X * Y * PAIRS
CHUNK = 1024
IMAGES = 2 * PAIRS
HALF = PAIRS // 2
COPIES = 256
F32, BF16 = jnp.float32, jnp.bfloat16


def place():
    row, col = lax.axis_index("row"), lax.axis_index("col")
    x, zh = lax.div(row, 4), lax.rem(row, 4)
    y, zl, c = lax.div(col, 4), lax.rem(lax.div(col, 2), 2), lax.rem(col, 2)
    return x, y, zh * 2 + zl, c


def device(x, y, z, c):
    return (x * 4 + lax.div(z, 2), y * 4 + lax.rem(z, 2) * 2 + c)


def shift(value, by, size):
    return lax.rem(value + by, size)


def wide(ref, rows):
    return jnp.concatenate([ref[block, rows, :] for block in range(ref.shape[0])], axis=1)


def put(ref, rows, value):
    for block in range(ref.shape[0]):
        ref[block, rows, :] = value[:, block * 128:(block + 1) * 128]


class Copies:
    def __init__(self, send_sems, recv_sems):
        self.send_sems, self.recv_sems, self.used, self.all = send_sems, recv_sems, 0, []

    def reserve(self, count):
        self.used += count
        return self.used - count

    def make(self, src, dst, target, send_at, recv_at):
        return pltpu.make_async_remote_copy(
            src_ref=src,
            dst_ref=dst,
            send_sem=self.send_sems.at[send_at],
            recv_sem=self.recv_sems.at[recv_at],
            device_id=target,
            device_id_type=MESH,
        )

    def plan(self, src, dst, target):
        at = self.reserve(1)
        copy = self.make(src, dst, target, at, at)
        self.all.append(copy)
        return copy

    def push(self, src, dst, target):
        copy = self.plan(src, dst, target)
        copy.start()
        return copy

    def finish(self):
        for copy in self.all:
            copy.wait_send()


class Scatter:
    def __init__(self, net, src, dst, targets, is_self, mine):
        self.net, self.src, self.dst, self.targets, self.is_self, self.mine = net, src, dst, targets, is_self, mine
        self.at = net.reserve(8)

    def remote(self, i):
        return self.net.make(
            self.src.at[i], self.dst.at[self.mine], self.targets[i], self.at + i, self.at + self.mine
        )

    def local(self, i):
        sem = self.net.recv_sems.at[self.at + self.mine]
        return pltpu.make_async_copy(self.src.at[i], self.dst.at[self.mine], sem)

    def start(self):
        for i in range(8):
            pl.when(jnp.logical_not(self.is_self[i]))(self.remote(i).start)
            pl.when(self.is_self[i])(self.local(i).start)

    def wait(self):
        for i in range(8):
            self.net.make(self.src.at[i], self.dst.at[i], self.targets[i], self.at + i, self.at + i).wait_recv()

    def wait_sent(self):
        for i in range(8):
            pl.when(jnp.logical_not(self.is_self[i]))(self.remote(i).wait_send)


def kernel(
    feats_hbm, text_hbm, proj_hbm, norms_hbm, ids_hbm, state_hbm,
    weights_ref, sums_ref,
    feats_ref, text_ref, norms_ref, ids_row, state_ref, proj, texts, images, raw_ref, acc, own_grad, weigh0, weigh1,
    send_up, send_down, recv_up, recv_down, send_up_row, send_down_row, recv_up_row, recv_down_row,
    feats_all, clipped, clipped_all, shares, shares_send, x_recv, x_part, x_send, x_recv_last,
    z_recv, z_send, z_recv_last, z_tiles,
    state_recv, state_tile, sums_send, sq_send, sq_recv,
    load_sems, send_sems, recv_sems,
):
    x, y, z, c = place()
    col = lax.axis_index("col")
    k = c * 4 + y
    other = 1 - c
    zl = lax.rem(z, 2)
    at_x = [device(shift(x, o, X), y, z, c) for o in range(1, X)]
    at_y = [device(x, shift(y, o, Y), z, c) for o in range(1, Y)]
    at_z = [device(x, y, shift(z, o, Z), c) for o in range(1, Z)]
    across = device(x, y, z, other)
    at_y_across = [device(x, shift(y, o, Y), z, other) for o in range(1, Y)]
    flip = z + 1 - 2 * zl
    at_flip = [device(x, shift(y, o, Y), flip, cc) for o in range(Y) for cc in (c, other)][1:]
    x_up, x_down, y_up, y_down, z_up, z_down = at_x[0], at_x[2], at_y[0], at_y[2], at_z[0], at_z[6]

    loads = [
        pltpu.make_async_copy(src, dst, load_sems.at[i])
        for i, (src, dst) in enumerate((
            (text_hbm, text_ref), (feats_hbm, feats_ref), (proj_hbm, proj),
            (state_hbm, state_ref), (norms_hbm, norms_ref), (ids_hbm, ids_row),
        ))
    ]
    for load in loads:
        load.start()
    loads[0].wait()
    text = text_ref[...].astype(F32)
    text = text * lax.rsqrt(jnp.sum(text * text, axis=1, keepdims=True) + EPSILON)
    put(texts, slice(0, PAIRS), text.astype(BF16))

    barrier = pltpu.get_barrier_semaphore()
    partners = at_x + at_y + at_z + [across] + at_y_across + at_flip
    for target in partners:
        pl.semaphore_signal(barrier, inc=1, device_id=target, device_id_type=MESH)
    pl.semaphore_wait(barrier, len(partners))
    net = Copies(send_sems, recv_sems)

    def lanes(index, width=128):
        return pl.ds(pl.multiple_of(index * width, width), width)

    def slot(rx, ry, rows, core=0):
        base = (core * 16 + rx * 4 + ry) * PAIRS
        return texts.at[:, base + rows[0]:base + rows[1], :]

    def hop(axis, up, rx, ry, rows):
        step = 3 if up else 1
        if axis == "x":
            return net.plan(slot(rx, ry, rows), slot((rx + step) % 4, ry, rows), x_up if up else x_down)
        return net.plan(slot(rx, ry, rows), slot(rx, (ry + step) % 4, rows), y_up if up else y_down)

    text_crossings = []

    def cross(rx, ry, rows):
        text_crossings.append(net.push(slot(rx, ry, rows), slot(rx, ry, rows, 1), across))

    class Half:
        def __init__(self, first, second, low):
            self.rows, self.swap = (low, low + 64), first == "y"
            self.parts = ((low, low + 32), (low + 32, low + 64))
            r, p = self.rows, self.parts
            self.first = [hop(first, up, 0, 0, r) for up in (True, False)]
            self.relay = [hop(first, up, *self.at(3 if up else 1, 0), p[0 if up else 1]) for up in (True, False)]
            self.second = [[hop(second, up, *self.at(a, 0), r) for up in (True, False)] for a in range(4)]
            self.last = [
                [hop(second, up, *self.at(a, 3 if up else 1), p[0 if up else 1]) for up in (True, False)]
                for a in range(4)
            ]

        def at(self, a, b):
            return (b, a) if self.swap else (a, b)

        def open(self, a):
            for copy in self.second[a]:
                copy.start()

        def got_first(self, i):
            a = (3, 1)[i]
            self.first[i].wait_recv()
            self.relay[i].start()
            self.open(a)
            cross(*self.at(a, 0), self.rows)

        def got_relay(self):
            for copy in self.relay:
                copy.wait_recv()
            self.open(2)
            cross(*self.at(2, 0), self.rows)

        def got_second(self, a):
            for i in range(2):
                self.second[a][i].wait_recv()
                self.last[a][i].start()
                cross(*self.at(a, (3, 1)[i]), self.rows)

        def got_last(self, a):
            for copy in self.last[a]:
                copy.wait_recv()
            cross(*self.at(a, 2), self.rows)

    def arrive(copies):
        for copy in copies:
            copy.wait_recv()

    low, high = Half("x", "y", 0), Half("y", "x", 64)
    halves = (low, high)
    for half in halves:
        for copy in half.first:
            copy.start()
    for half in halves:
        half.open(0)
    cross(0, 0, (0, PAIRS))

    for load in loads[1:]:
        load.wait()
    raw = jnp.dot(feats_ref[...], proj[...], preferred_element_type=F32)
    raw_ref[...] = raw
    inverse = lax.rsqrt(jnp.sum(raw * raw, axis=1, keepdims=True) + EPSILON)

    def image(index, rows=(0, PAIRS)):
        return images.at[:, index * PAIRS + rows[0]:index * PAIRS + rows[1], :]

    own_rows = slice(PAIRS, 2 * PAIRS)
    put(images, own_rows, (raw * inverse).astype(BF16))
    up = [net.plan(image(a), image(b), z_up) for a, b in ((1, 7), (7, 5), (5, 3))]
    down = [net.plan(image(a), image(b), z_down) for a, b in ((1, 6), (6, 4), (4, 2))]
    up.append(net.plan(image(3, (0, 64)), image(0, (0, 64)), z_up))
    down.append(net.plan(image(2, (64, 128)), image(0, (64, 128)), z_down))
    up[0].start()
    down[0].start()

    feats_all[:, 0:PAIRS] = feats_ref[...].T
    acc[...] = jnp.zeros_like(acc)
    shares[...] = jnp.zeros_like(shares)
    feat_gram = lax.dot_general(
        feats_ref[...], feats_ref[...], (((1,), (1,)), ((), ())), preferred_element_type=F32
    )
    local_row = (ids_row[...] - (lax.axis_index("row") * 16 + col) * USERS).astype(F32)
    square_shape = (PAIRS, PAIRS)
    diagonal = lax.broadcasted_iota(jnp.int32, square_shape, 0) == lax.broadcasted_iota(
        jnp.int32, square_shape, 1
    )
    local_column = jnp.sum(jnp.where(diagonal, local_row, 0.0), axis=1, keepdims=True)
    same_user = local_column == local_row
    users = lax.broadcasted_iota(jnp.int32, (PAIRS, USERS), 1).astype(F32)
    bound = jnp.sum(jnp.where(local_column == users, norms_ref[...], 0.0), axis=1, keepdims=True)
    feat_gram = jnp.where(same_user, feat_gram, 0.0)

    def turn(step):
        for ring in (up, down):
            ring[step].wait_recv()
            if step < 3:
                ring[step + 1].start()

    owner_slot = (lax.rem(y, 2) * 2 + zl) * 2 + c
    zh2 = z - zl
    half_y = lax.div(y, 2)
    state_out = Scatter(
        net, state_ref, state_recv,
        [device(x, i % 4, zh2 + half_y, i // 4) for i in range(8)],
        [jnp.logical_and(zl == half_y, k == i) for i in range(8)],
        owner_slot,
    )

    for half in halves:
        half.got_first(0)
        half.got_first(1)
    for half in halves:
        half.got_second(0)
    turn(0)
    for half in halves:
        half.got_relay()
    for half in halves:
        half.got_last(0)
    for a in (3, 1):
        for half in halves:
            half.got_second(a)
    turn(1)
    for half in halves:
        half.got_second(2)
    for a in (3, 1):
        for half in halves:
            half.got_last(a)
    turn(2)
    for half in halves:
        half.got_last(2)
    turn(3)

    def feats_slot(ry, rows=(0, W)):
        return feats_all.at[rows[0]:rows[1], ry * PAIRS:(ry + 1) * PAIRS]

    feats_near = [net.plan(feats_slot(0), feats_slot(3), y_up), net.plan(feats_slot(0), feats_slot(1), y_down)]
    feats_far = [
        net.plan(feats_slot(3, (0, W // 2)), feats_slot(2, (0, W // 2)), y_up),
        net.plan(feats_slot(1, (W // 2, W)), feats_slot(2, (W // 2, W)), y_down),
    ]
    feats_cross = net.plan(feats_all.at[:, 0:512], feats_all.at[:, 512:1024], across)
    def feats_open():
        for copy in feats_near:
            copy.start()

    def feats_on():
        for near, far in zip(feats_near, feats_far):
            near.wait_recv()
            far.start()

    def feats_over():
        arrive(feats_far)
        feats_cross.start()

    pick = lax.broadcasted_iota(jnp.int32, (HALF, 128), 0) == lax.broadcasted_iota(
        jnp.int32, (HALF, 128), 1
    )

    def pack(dst, dst_row, full, unit):
        coefficient = jnp.sum(full * unit, axis=1, keepdims=True)
        dst[...] = (full - coefficient * unit).astype(BF16)
        row = jnp.sum(jnp.where(pick, coefficient, 0.0), axis=0, keepdims=True)
        dst_row[...] = jnp.broadcast_to(row, (8, 128))

    def unpack(src, src_row, unit):
        coefficient = jnp.sum(jnp.where(pick, src_row[0:1, :], 0.0), axis=1, keepdims=True)
        return src[...].astype(F32) + coefficient * unit

    class Side:
        def __init__(self, first, come, sends, recvs, send_rows, recv_rows, target):
            self.blocks, self.sends, self.recvs = (0, first, first + 2, first + 4), sends, recvs
            self.send_rows, self.recv_rows = send_rows, recv_rows
            self.rows = ((64 - come, 128 - come), (come, come + 64))
            self.copies = [
                (
                    net.plan(sends.at[i], recvs.at[i], target),
                    net.plan(send_rows.at[i], recv_rows.at[i], target),
                )
                for i in range(7)
            ]

        def take(self, i, unit):
            arrive(self.copies[i])
            return unpack(self.recvs.at[i], self.recv_rows.at[i], unit)

        def give(self, hop, late):
            i = 2 * hop - 1 + late
            base = self.blocks[hop] * PAIRS
            start, stop = self.rows[late]
            unit = wide(images, slice(base + start, base + stop)).astype(F32)
            full = LOGIT_SCALE * acc[base + start:base + stop, :]
            if hop > 1 or (hop == 1 and late):
                full = full + self.take(i - 2, unit)
            pack(self.sends.at[i], self.send_rows.at[i], full, unit)
            for copy in self.copies[i]:
                copy.start()

    sides = (
        Side(2, 0, send_up, recv_up, send_up_row, recv_up_row, z_up),
        Side(3, 64, send_down, recv_down, send_down_row, recv_down_row, z_down),
    )

    def give(hop, late):
        for side in sides:
            side.give(hop, late)

    schedule = {
        (0, 0): [feats_open, state_out.start],
        (0, 2): [lambda: arrive(text_crossings)],
        (1, 0): [lambda: give(0, 1)],
        (1, 2): [feats_on],
        (2, 0): [lambda: give(1, 0), lambda: give(1, 1)],
        (2, 2): [feats_over],
        (3, 0): [lambda: give(2, 0)],
        (3, 1): [lambda: give(2, 1)],
    }

    def grid_step(step, carry):
        rows = pl.ds(pl.multiple_of(step * IMAGES, IMAGES), IMAGES)
        buffers = (weigh0, weigh1)

        def weigh(n):
            cosine = lax.dot_general(
                wide(images, rows), wide(texts, slice(n * CHUNK, (n + 1) * CHUNK)),
                (((1,), (1,)), ((), ())), preferred_element_type=F32,
            )
            pair = 0.5 + 0.5 * jnp.tanh(0.5 * LOGIT_SCALE * cosine + 0.5 * LOGIT_BIAS)
            put(buffers[n % 2], slice(None), pair.astype(BF16))

        def fold(n):
            acc[rows, :] += jnp.dot(
                wide(buffers[n % 2], slice(None)), wide(texts, slice(n * CHUNK, (n + 1) * CHUNK)),
                preferred_element_type=F32,
            )

        for n in range(TEXTS // CHUNK):
            for (at, part), events in schedule.items():
                if part == n:

                    @pl.when(step == at)
                    def _(events=events):
                        for event in events:
                            event()

            weigh(n)
            if n > 0:
                fold(n - 1)
        fold(TEXTS // CHUNK - 1)
        return carry

    lax.fori_loop(0, 4, grid_step, 0)
    give(3, 0)
    give(3, 1)
    unit = wide(images, own_rows).astype(F32)
    text = wide(texts, slice(0, PAIRS)).astype(F32)
    cosine = jnp.sum(unit * text, axis=1, keepdims=True)
    sigmoid = 0.5 + 0.5 * jnp.tanh(0.5 * LOGIT_SCALE * cosine + 0.5 * LOGIT_BIAS)
    change = (sigmoid - 1.0).astype(BF16).astype(F32) - sigmoid.astype(BF16).astype(F32)
    own_grad[...] = LOGIT_SCALE * (acc[PAIRS:2 * PAIRS, :] + change * text)

    state_out.wait()
    state_tile[...] = jnp.zeros_like(state_tile)
    for piece in range(8):
        first = 11 * (piece // 2) + 5 * (piece % 2)
        for a in range(3):
            state_tile[a, first:first + 6, :] += state_recv[piece, a, 0:6, :]

    raw = raw_ref[...]
    unit = wide(images, own_rows).astype(F32)
    for late in range(2):
        for side in sides:
            start, stop = side.rows[late]
            own_grad[start:stop, :] += side.take(5 + late, unit[start:stop])
    unit_grad = own_grad[...]
    inner = jnp.sum(raw * unit_grad, axis=1, keepdims=True)
    embed_grad = inverse * unit_grad - inverse * inverse * inverse * raw * inner
    grad_gram = lax.dot_general(
        embed_grad, embed_grad, (((1,), (1,)), ((), ())),
        precision=lax.Precision.HIGHEST, preferred_element_type=F32,
    )
    terms = jnp.sum(feat_gram * grad_gram, axis=0, keepdims=True)
    user_sq = jnp.sum(jnp.where(same_user, terms, 0.0), axis=1, keepdims=True)
    factor = bound / jnp.maximum(jnp.sqrt(user_sq), bound)
    clipped[...] = (factor * embed_grad).astype(BF16)

    def rows_of(core, ry):
        return clipped_all.at[(core * 4 + ry) * PAIRS:(core * 4 + ry + 1) * PAIRS, :]

    parts = []
    for o in range(1, Y):
        parts.append(net.push(clipped.at[:, lanes(c * 4 + shift(y, o, Y))], rows_of(0, 4 - o), at_y[o - 1]))
        parts.append(net.push(clipped.at[:, lanes(other * 4 + shift(y, o, Y))], rows_of(1, 4 - o), at_y_across[o - 1]))
    parts.append(net.push(clipped.at[:, lanes(other * 4 + y)], rows_of(1, 0), across))
    clipped_all[0:PAIRS, :] = clipped[:, lanes(k)]
    feats_cross.wait_recv()
    for copy in parts:
        copy.wait_recv()

    def rows(index):
        return pl.ds(pl.multiple_of(index * PADDED, 16), PADDED)

    x_moves = []
    for o in (1, 2, 3, 0):
        block = feats_all[pl.ds(pl.multiple_of(shift(x, o, X) * SHARE, 16), SHARE), :]
        part = jnp.dot(block, clipped_all[...], preferred_element_type=F32)
        for piece in range(Z):
            shares[o, piece, 0:BLOCK, :] = part[piece * BLOCK:(piece + 1) * BLOCK]
        shares_send[o] = shares[o].astype(BF16)
        if o:
            x_moves.append(net.push(shares_send.at[o, :, 0:32, :], x_recv.at[o - 1], at_x[o - 1]))
    z_moves = [
        net.push(shares_send.at[:, shift(z, o, Z), 32:PADDED, :], z_recv.at[o - 1], at_z[o - 1])
        for o in range(1, Z)
    ]
    total = shares[0, :, 0:32, :]
    for o in range(1, X):
        x_moves[o - 1].wait_recv()
        total = total + x_recv[o - 1].astype(F32)
    x_part[...] = total
    x_send[...] = total.astype(BF16)
    x_moves = [
        net.push(x_send.at[shift(z, o, Z)], x_recv_last.at[o - 1], at_z[o - 1]) for o in range(1, Z)
    ]
    total = shares[:, z, 32:PADDED, :]
    for o in range(1, Z):
        z_moves[o - 1].wait_recv()
        total = total + z_recv[o - 1].astype(F32)
    z_send[...] = total.astype(BF16)
    z_moves = [net.push(z_send.at[o], z_recv_last.at[o - 1], at_x[o - 1]) for o in range(1, X)]
    upper, lower = x_part[z], total[0]
    for o in range(1, X):
        z_moves[o - 1].wait_recv()
        lower = lower + z_recv_last[o - 1].astype(F32)
    for o in range(1, Z):
        x_moves[o - 1].wait_recv()
        upper = upper + x_recv_last[o - 1].astype(F32)
    grad = jnp.concatenate([upper, lower], axis=0)

    new_sum = state_tile[0] + grad
    update = new_sum + state_tile[1]
    for piece in range(8):
        first = 11 * (piece // 2) + 5 * (piece % 2)
        sums_send[piece] = new_sum[first:first + 8]

    square = jnp.sum((update * update).reshape(PADDED // 8, 8, 128), axis=0)
    at = 0
    for stage, targets in enumerate((at_z, at_x, at_y + [across] + at_y_across)):
        sq_send[stage] = square
        moves = [
            net.push(sq_send.at[stage], sq_recv.at[at + i], target)
            for i, target in enumerate(targets)
        ]
        for i, copy in enumerate(moves):
            copy.wait_recv()
            square = square + sq_recv[at + i]
        at += len(targets)
    norm = jnp.sqrt(jnp.sum(square, keepdims=True))
    cap = math.sqrt(W * E)
    shrink = cap / jnp.maximum(norm, cap)
    tile = (state_tile[2] - RATE * shrink * update).astype(BF16)

    z_tiles[rows(z), :] = tile
    moves = [net.push(z_tiles.at[rows(z), :], z_tiles.at[rows(z), :], target) for target in at_z]
    sums_out = Scatter(
        net, sums_send, sums_ref,
        [device(x, 2 * zl + i // 4, zh2 + (i // 2) % 2, i % 2) for i in range(8)],
        [
            jnp.logical_and(half_y == zl, owner_slot == i) for i in range(8)
        ],
        k,
    )
    sums_out.start()
    for copy in moves:
        copy.wait_recv()
    whole = z_tiles[...].astype(F32)
    whole = jnp.concatenate([whole[piece * PADDED:piece * PADDED + BLOCK] for piece in range(Z)], axis=0)
    weights_ref[x, :, lanes(k)] = whole.astype(BF16)

    half = SHARE // 2

    def low_piece(index, rows=(0, half)):
        return weights_ref.at[index, rows[0]:rows[1], lanes(c, 512)]

    def high_piece(away, shares=slice(0, X)):
        return weights_ref.at[shares, half:SHARE, lanes(c * 4 + shift(y, away, Y))]

    def send(piece, target):
        return net.push(piece, piece, target)

    moves_y = [send(weights_ref.at[x, 0:half, lanes(k)], target) for target in at_y]
    moves_x = [send(weights_ref.at[x, half:SHARE, lanes(k)], target) for target in at_x]
    arrive(moves_y)
    low_moves = [send(low_piece(x), target) for target in (x_up, x_down)]
    arrive(moves_x)
    high_moves = [send(high_piece(0), target) for target in (y_up, y_down)]
    given = [send(low_piece(x), across), send(high_piece(0), across)]
    far = []
    for copy, away, rows_sent, target in (
        (low_moves[0], 3, (0, 96), x_up), (low_moves[1], 1, (96, half), x_down)
    ):
        copy.wait_recv()
        index = shift(x, away, X)
        far.append(send(low_piece(index, rows_sent), target))
        given.append(send(low_piece(index), across))
    for copy, away, shares, target in (
        (high_moves[0], 3, slice(0, 2), y_up), (high_moves[1], 1, slice(2, 4), y_down)
    ):
        copy.wait_recv()
        far.append(send(high_piece(away, shares), target))
        given.append(send(high_piece(away), across))
    arrive(far)
    given += [send(low_piece(shift(x, 2, X)), across), send(high_piece(2), across)]
    arrive(given)
    sums_out.wait()
    state_out.wait_sent()
    sums_out.wait_sent()
    net.finish()


def body(
    image_feats, text_emb, projection, clip_norms, user_ids, grad_sum, init_weights, tree_noise
):
    c = lax.rem(lax.axis_index("col"), 2)
    state = jnp.pad(jnp.stack([grad_sum, tree_noise, init_weights]), ((0, 0), (4, 4), (0, 0)))
    state = lax.dynamic_slice(state, (0, 4 - 4 * c, 0), (3, 48, 128))
    state = state.reshape(3, 6, 8, 128).transpose(2, 0, 1, 3)
    state = jnp.pad(state, ((0, 0), (0, 0), (0, 2), (0, 0)))
    vmem = pl.BlockSpec(memory_space=pltpu.VMEM)
    weights, sums = pl.pallas_call(
        kernel,
        out_shape=(
            jax.ShapeDtypeStruct((X, SHARE, E), BF16),
            jax.ShapeDtypeStruct((8, 8, 128), F32),
        ),
        in_specs=[pl.BlockSpec(memory_space=pltpu.HBM)] * 6,
        out_specs=(vmem, vmem),
        scratch_shapes=[
            pltpu.VMEM((PAIRS, W), BF16),
            pltpu.VMEM((PAIRS, E), BF16),
            pltpu.VMEM((1, USERS), F32),
            pltpu.VMEM((1, PAIRS), jnp.int32),
            pltpu.VMEM((8, 3, 8, 128), F32),
            pltpu.VMEM((W, E), BF16),
            pltpu.VMEM((E // 128, TEXTS, 128), BF16),
            pltpu.VMEM((E // 128, Z * PAIRS, 128), BF16),
            pltpu.VMEM((PAIRS, E), F32),
            pltpu.VMEM((Z * PAIRS, E), F32),
            pltpu.VMEM((PAIRS, E), F32),
            pltpu.VMEM((CHUNK // 128, IMAGES, 128), BF16),
            pltpu.VMEM((CHUNK // 128, IMAGES, 128), BF16),
            pltpu.VMEM((7, HALF, E), BF16),
            pltpu.VMEM((7, HALF, E), BF16),
            pltpu.VMEM((7, HALF, E), BF16),
            pltpu.VMEM((7, HALF, E), BF16),
            pltpu.VMEM((7, 8, 128), F32),
            pltpu.VMEM((7, 8, 128), F32),
            pltpu.VMEM((7, 8, 128), F32),
            pltpu.VMEM((7, 8, 128), F32),
            pltpu.VMEM((W, 8 * PAIRS), BF16),
            pltpu.VMEM((PAIRS, E), BF16),
            pltpu.VMEM((8 * PAIRS, 128), BF16),
            pltpu.VMEM((X, Z, PADDED, 128), F32),
            pltpu.VMEM((X, Z, PADDED, 128), BF16),
            pltpu.VMEM((X - 1, Z, 32, 128), BF16),
            pltpu.VMEM((Z, 32, 128), F32),
            pltpu.VMEM((Z, 32, 128), BF16),
            pltpu.VMEM((Z - 1, 32, 128), BF16),
            pltpu.VMEM((Z - 1, X, 16, 128), BF16),
            pltpu.VMEM((X, 16, 128), BF16),
            pltpu.VMEM((X - 1, 16, 128), BF16),
            pltpu.VMEM((WIDE, 128), BF16),
            pltpu.VMEM((8, 3, 8, 128), F32),
            pltpu.VMEM((3, PADDED, 128), F32),
            pltpu.VMEM((8, 8, 128), F32),
            pltpu.VMEM((3, 8, 128), F32),
            pltpu.VMEM((17, 8, 128), F32),
            pltpu.SemaphoreType.DMA((6,)),
            pltpu.SemaphoreType.DMA((COPIES,)),
            pltpu.SemaphoreType.DMA((COPIES,)),
        ],
        compiler_params=pltpu.CompilerParams(
            collective_id=1, has_side_effects=True, vmem_limit_bytes=48 * 1024 * 1024
        ),
    )(
        image_feats, text_emb, projection, clip_norms.reshape(1, USERS),
        user_ids.reshape(1, PAIRS), state,
    )
    sums = sums[:, :6].transpose(1, 0, 2).reshape(48, 128)
    return weights.reshape(W, E), lax.dynamic_slice(sums, (4 * c, 0), (44, 128))


def solution(mesh):
    in_specs = (
        P(("row", "col"), None),
        P(("row", "col"), None),
        P(),
        P(("row", "col")),
        P(("row", "col")),
        P(("row", "col"), None),
        P(("row", "col"), None),
        P(("row", "col"), None),
    )
    out_specs = (P(), P(("row", "col"), None))
    return jax.shard_map(body, mesh=mesh, in_specs=in_specs, out_specs=out_specs, check_vma=False)
```

```python
import math

import jax
import jax.numpy as jnp
from jax import lax
from jax.experimental import pallas as pl
from jax.experimental.pallas import tpu as pltpu
from jax.sharding import PartitionSpec as P

LOGIT_SCALE = 32.0
LOGIT_BIAS = -5.0
RATE = 0.5
EPSILON = 1e-06

MESH = pl.DeviceIdType.MESH
X, Y, Z = 4, 4, 8
W, E, PAIRS, USERS = 1408, 1024, 128, 16
SHARE = W // X
BLOCK = SHARE // Z
PADDED = 48
WIDE = Z * PADDED
TEXTS = 2 * X * Y * PAIRS
CHUNK = 1024
IMAGES = 2 * PAIRS
HALF = PAIRS // 2
COPIES = 256
F32, BF16 = jnp.float32, jnp.bfloat16


def place():
    row, col = lax.axis_index("row"), lax.axis_index("col")
    x, zh = lax.div(row, 4), lax.rem(row, 4)
    y, zl, c = lax.div(col, 4), lax.rem(lax.div(col, 2), 2), lax.rem(col, 2)
    return x, y, zh * 2 + zl, c


def device(x, y, z, c):
    return (x * 4 + lax.div(z, 2), y * 4 + lax.rem(z, 2) * 2 + c)


def shift(value, by, size):
    return lax.rem(value + by, size)


class Copies:
    def __init__(self, send_sems, recv_sems):
        self.send_sems, self.recv_sems, self.used, self.all = send_sems, recv_sems, 0, []

    def reserve(self, count):
        self.used += count
        return self.used - count

    def make(self, src, dst, target, send_at, recv_at):
        return pltpu.make_async_remote_copy(
            src_ref=src,
            dst_ref=dst,
            send_sem=self.send_sems.at[send_at],
            recv_sem=self.recv_sems.at[recv_at],
            device_id=target,
            device_id_type=MESH,
        )

    def plan(self, src, dst, target):
        at = self.reserve(1)
        copy = self.make(src, dst, target, at, at)
        self.all.append(copy)
        return copy

    def push(self, src, dst, target):
        copy = self.plan(src, dst, target)
        copy.start()
        return copy

    def finish(self):
        for copy in self.all:
            copy.wait_send()


class Scatter:
    def __init__(self, net, src, dst, targets, is_self, mine):
        self.net, self.src, self.dst, self.targets, self.is_self, self.mine = net, src, dst, targets, is_self, mine
        self.at = net.reserve(8)

    def remote(self, i):
        return self.net.make(
            self.src.at[i], self.dst.at[self.mine], self.targets[i], self.at + i, self.at + self.mine
        )

    def local(self, i):
        sem = self.net.recv_sems.at[self.at + self.mine]
        return pltpu.make_async_copy(self.src.at[i], self.dst.at[self.mine], sem)

    def start(self):
        for i in range(8):
            pl.when(jnp.logical_not(self.is_self[i]))(self.remote(i).start)
            pl.when(self.is_self[i])(self.local(i).start)

    def wait(self):
        for i in range(8):
            self.net.make(self.src.at[i], self.dst.at[i], self.targets[i], self.at + i, self.at + i).wait_recv()

    def wait_sent(self):
        for i in range(8):
            pl.when(jnp.logical_not(self.is_self[i]))(self.remote(i).wait_send)


def kernel(
    feats_hbm, text_hbm, proj_hbm, norms_hbm, ids_hbm, state_hbm,
    weights_ref, sums_ref,
    feats_ref, text_ref, norms_ref, ids_row, state_ref, proj, texts, images, raw_ref, acc, own_grad, weigh0, weigh1,
    send_up, send_down, recv_up, recv_down, send_up_row, send_down_row, recv_up_row, recv_down_row,
    feats_all, clipped, clipped_all, shares, shares_send, x_recv, x_part, x_send, x_recv_last,
    z_recv, z_send, z_recv_last, z_tiles,
    state_recv, state_tile, sums_send, sq_send, sq_recv,
    load_sems, send_sems, recv_sems,
):
    x, y, z, c = place()
    col = lax.axis_index("col")
    k = c * 4 + y
    other = 1 - c
    zl = lax.rem(z, 2)
    at_x = [device(shift(x, o, X), y, z, c) for o in range(1, X)]
    at_y = [device(x, shift(y, o, Y), z, c) for o in range(1, Y)]
    at_z = [device(x, y, shift(z, o, Z), c) for o in range(1, Z)]
    across = device(x, y, z, other)
    at_y_across = [device(x, shift(y, o, Y), z, other) for o in range(1, Y)]
    flip = z + 1 - 2 * zl
    at_flip = [device(x, shift(y, o, Y), flip, cc) for o in range(Y) for cc in (c, other)][1:]
    x_up, x_down, y_up, y_down, z_up, z_down = at_x[0], at_x[2], at_y[0], at_y[2], at_z[0], at_z[6]

    loads = [
        pltpu.make_async_copy(src, dst, load_sems.at[i])
        for i, (src, dst) in enumerate((
            (text_hbm, text_ref), (feats_hbm, feats_ref), (proj_hbm, proj),
            (state_hbm, state_ref), (norms_hbm, norms_ref), (ids_hbm, ids_row),
        ))
    ]
    for load in loads:
        load.start()
    loads[0].wait()
    text = text_ref[...].astype(F32)
    texts[0:PAIRS, :] = (
        text * lax.rsqrt(jnp.sum(text * text, axis=1, keepdims=True) + EPSILON)
    ).astype(BF16)

    barrier = pltpu.get_barrier_semaphore()
    partners = at_x + at_y + at_z + [across] + at_y_across + at_flip
    for target in partners:
        pl.semaphore_signal(barrier, inc=1, device_id=target, device_id_type=MESH)
    pl.semaphore_wait(barrier, len(partners))
    net = Copies(send_sems, recv_sems)

    def lanes(index, width=128):
        return pl.ds(pl.multiple_of(index * width, width), width)

    def slot(rx, ry, rows, core=0):
        base = (core * 16 + rx * 4 + ry) * PAIRS
        return texts.at[base + rows[0]:base + rows[1], :]

    def hop(axis, up, rx, ry, rows):
        step = 3 if up else 1
        if axis == "x":
            return net.plan(slot(rx, ry, rows), slot((rx + step) % 4, ry, rows), x_up if up else x_down)
        return net.plan(slot(rx, ry, rows), slot(rx, (ry + step) % 4, rows), y_up if up else y_down)

    text_crossings = []

    def cross(rx, ry, rows):
        text_crossings.append(net.push(slot(rx, ry, rows), slot(rx, ry, rows, 1), across))

    class Half:
        def __init__(self, first, second, low):
            self.rows, self.swap = (low, low + 64), first == "y"
            self.parts = ((low, low + 32), (low + 32, low + 64))
            r, p = self.rows, self.parts
            self.first = [hop(first, up, 0, 0, r) for up in (True, False)]
            self.relay = [hop(first, up, *self.at(3 if up else 1, 0), p[0 if up else 1]) for up in (True, False)]
            self.second = [[hop(second, up, *self.at(a, 0), r) for up in (True, False)] for a in range(4)]
            self.last = [
                [hop(second, up, *self.at(a, 3 if up else 1), p[0 if up else 1]) for up in (True, False)]
                for a in range(4)
            ]

        def at(self, a, b):
            return (b, a) if self.swap else (a, b)

        def open(self, a):
            for copy in self.second[a]:
                copy.start()

        def got_first(self, i):
            a = (3, 1)[i]
            self.first[i].wait_recv()
            self.relay[i].start()
            self.open(a)
            cross(*self.at(a, 0), self.rows)

        def got_relay(self):
            for copy in self.relay:
                copy.wait_recv()
            self.open(2)
            cross(*self.at(2, 0), self.rows)

        def got_second(self, a):
            for i in range(2):
                self.second[a][i].wait_recv()
                self.last[a][i].start()
                cross(*self.at(a, (3, 1)[i]), self.rows)

        def got_last(self, a):
            for copy in self.last[a]:
                copy.wait_recv()
            cross(*self.at(a, 2), self.rows)

    def arrive(copies):
        for copy in copies:
            copy.wait_recv()

    low, high = Half("x", "y", 0), Half("y", "x", 64)
    halves = (low, high)
    for half in halves:
        for copy in half.first:
            copy.start()
    for half in halves:
        half.open(0)
    cross(0, 0, (0, PAIRS))

    for load in loads[1:]:
        load.wait()
    raw = jnp.dot(feats_ref[...], proj[...], preferred_element_type=F32)
    raw_ref[...] = raw
    inverse = lax.rsqrt(jnp.sum(raw * raw, axis=1, keepdims=True) + EPSILON)

    def image(index, rows=(0, PAIRS)):
        return images.at[index * PAIRS + rows[0]:index * PAIRS + rows[1], :]

    images[PAIRS:2 * PAIRS, :] = (raw * inverse).astype(BF16)
    up = [net.plan(image(a), image(b), z_up) for a, b in ((1, 7), (7, 5), (5, 3))]
    down = [net.plan(image(a), image(b), z_down) for a, b in ((1, 6), (6, 4), (4, 2))]
    up.append(net.plan(image(3, (0, 64)), image(0, (0, 64)), z_up))
    down.append(net.plan(image(2, (64, 128)), image(0, (64, 128)), z_down))
    up[0].start()
    down[0].start()

    feats_all[:, 0:PAIRS] = feats_ref[...].T
    acc[...] = jnp.zeros_like(acc)
    shares[...] = jnp.zeros_like(shares)
    feat_gram = lax.dot_general(
        feats_ref[...], feats_ref[...], (((1,), (1,)), ((), ())), preferred_element_type=F32
    )
    local_row = (ids_row[...] - (lax.axis_index("row") * 16 + col) * USERS).astype(F32)
    square_shape = (PAIRS, PAIRS)
    diagonal = lax.broadcasted_iota(jnp.int32, square_shape, 0) == lax.broadcasted_iota(
        jnp.int32, square_shape, 1
    )
    local_column = jnp.sum(jnp.where(diagonal, local_row, 0.0), axis=1, keepdims=True)
    same_user = local_column == local_row
    users = lax.broadcasted_iota(jnp.int32, (PAIRS, USERS), 1).astype(F32)
    bound = jnp.sum(jnp.where(local_column == users, norms_ref[...], 0.0), axis=1, keepdims=True)
    feat_gram = jnp.where(same_user, feat_gram, 0.0)

    def turn(step):
        for ring in (up, down):
            ring[step].wait_recv()
            if step < 3:
                ring[step + 1].start()

    owner_slot = (lax.rem(y, 2) * 2 + zl) * 2 + c
    zh2 = z - zl
    half_y = lax.div(y, 2)
    state_out = Scatter(
        net, state_ref, state_recv,
        [device(x, i % 4, zh2 + half_y, i // 4) for i in range(8)],
        [jnp.logical_and(zl == half_y, k == i) for i in range(8)],
        owner_slot,
    )

    for half in halves:
        half.got_first(0)
        half.got_first(1)
    for half in halves:
        half.got_second(0)
    turn(0)
    for half in halves:
        half.got_relay()
    for half in halves:
        half.got_last(0)
    for a in (3, 1):
        for half in halves:
            half.got_second(a)
    turn(1)
    for half in halves:
        half.got_second(2)
    for a in (3, 1):
        for half in halves:
            half.got_last(a)
    turn(2)
    for half in halves:
        half.got_last(2)
    turn(3)

    def feats_slot(ry, rows=(0, W)):
        return feats_all.at[rows[0]:rows[1], ry * PAIRS:(ry + 1) * PAIRS]

    feats_near = [net.plan(feats_slot(0), feats_slot(3), y_up), net.plan(feats_slot(0), feats_slot(1), y_down)]
    feats_far = [
        net.plan(feats_slot(3, (0, W // 2)), feats_slot(2, (0, W // 2)), y_up),
        net.plan(feats_slot(1, (W // 2, W)), feats_slot(2, (W // 2, W)), y_down),
    ]
    feats_cross = net.plan(feats_all.at[:, 0:512], feats_all.at[:, 512:1024], across)
    def feats_open():
        for copy in feats_near:
            copy.start()

    def feats_on():
        for near, far in zip(feats_near, feats_far):
            near.wait_recv()
            far.start()

    def feats_over():
        arrive(feats_far)
        feats_cross.start()

    pick = lax.broadcasted_iota(jnp.int32, (HALF, 128), 0) == lax.broadcasted_iota(
        jnp.int32, (HALF, 128), 1
    )

    def pack(dst, dst_row, full, unit):
        coefficient = jnp.sum(full * unit, axis=1, keepdims=True)
        dst[...] = (full - coefficient * unit).astype(BF16)
        row = jnp.sum(jnp.where(pick, coefficient, 0.0), axis=0, keepdims=True)
        dst_row[...] = jnp.broadcast_to(row, (8, 128))

    def unpack(src, src_row, unit):
        coefficient = jnp.sum(jnp.where(pick, src_row[0:1, :], 0.0), axis=1, keepdims=True)
        return src[...].astype(F32) + coefficient * unit

    class Side:
        def __init__(self, first, come, sends, recvs, send_rows, recv_rows, target):
            self.blocks, self.sends, self.recvs = (0, first, first + 2, first + 4), sends, recvs
            self.send_rows, self.recv_rows = send_rows, recv_rows
            self.rows = ((64 - come, 128 - come), (come, come + 64))
            self.copies = [
                (
                    net.plan(sends.at[i], recvs.at[i], target),
                    net.plan(send_rows.at[i], recv_rows.at[i], target),
                )
                for i in range(7)
            ]

        def take(self, i, unit):
            arrive(self.copies[i])
            return unpack(self.recvs.at[i], self.recv_rows.at[i], unit)

        def give(self, hop, late):
            i = 2 * hop - 1 + late
            base = self.blocks[hop] * PAIRS
            start, stop = self.rows[late]
            unit = images[base + start:base + stop, :].astype(F32)
            full = LOGIT_SCALE * acc[base + start:base + stop, :]
            if hop > 1 or (hop == 1 and late):
                full = full + self.take(i - 2, unit)
            pack(self.sends.at[i], self.send_rows.at[i], full, unit)
            for copy in self.copies[i]:
                copy.start()

    sides = (
        Side(2, 0, send_up, recv_up, send_up_row, recv_up_row, z_up),
        Side(3, 64, send_down, recv_down, send_down_row, recv_down_row, z_down),
    )

    def give(hop, late):
        for side in sides:
            side.give(hop, late)

    buffers = (weigh0, weigh1)

    def grid_step(rows, count, events):
        def weigh(n):
            cosine = lax.dot_general(
                images[rows, :], texts[n * CHUNK:(n + 1) * CHUNK, :],
                (((1,), (1,)), ((), ())), preferred_element_type=F32,
            )
            pair = 0.5 + 0.5 * jnp.tanh(0.5 * LOGIT_SCALE * cosine + 0.5 * LOGIT_BIAS)
            buffers[n % 2][0:count, :] = pair.astype(BF16)

        def fold(n):
            acc[rows, :] += jnp.dot(
                buffers[n % 2][0:count, :], texts[n * CHUNK:(n + 1) * CHUNK, :],
                preferred_element_type=F32,
            )

        for n in range(TEXTS // CHUNK):
            events(n)
            weigh(n)
            if n > 0:
                fold(n - 1)
        fold(TEXTS // CHUNK - 1)

    def open_events(n):
        if n == 0:
            feats_open()
            state_out.start()
        if n == 2:
            arrive(text_crossings)

    schedule = {
        (1, 2): [feats_on],
        (2, 0): [lambda: give(1, 0), lambda: give(1, 1)],
        (2, 2): [feats_over],
        (3, 0): [lambda: give(2, 0)],
        (3, 1): [lambda: give(2, 1)],
    }

    def pair_step(step, carry):
        def events(n):
            for (at, part), todo in schedule.items():
                if part == n:

                    @pl.when(step == at)
                    def _(todo=todo):
                        for event in todo:
                            event()

        grid_step(pl.ds(pl.multiple_of(step * IMAGES, IMAGES), IMAGES), IMAGES, events)
        return carry

    grid_step(slice(0, PAIRS), PAIRS, open_events)
    give(0, 1)
    lax.fori_loop(1, 4, pair_step, 0)
    give(3, 0)
    give(3, 1)
    grid_step(slice(PAIRS, 2 * PAIRS), PAIRS, lambda n: None)
    unit = images[PAIRS:2 * PAIRS, :].astype(F32)
    text = texts[0:PAIRS, :].astype(F32)
    cosine = jnp.sum(unit * text, axis=1, keepdims=True)
    sigmoid = 0.5 + 0.5 * jnp.tanh(0.5 * LOGIT_SCALE * cosine + 0.5 * LOGIT_BIAS)
    change = (sigmoid - 1.0).astype(BF16).astype(F32) - sigmoid.astype(BF16).astype(F32)
    own_grad[...] = LOGIT_SCALE * (acc[PAIRS:2 * PAIRS, :] + change * text)

    state_out.wait()
    state_tile[...] = jnp.zeros_like(state_tile)
    for piece in range(8):
        first = 11 * (piece // 2) + 5 * (piece % 2)
        for a in range(3):
            state_tile[a, first:first + 6, :] += state_recv[piece, a, 0:6, :]

    raw = raw_ref[...]
    unit = images[PAIRS:2 * PAIRS, :].astype(F32)
    for late in range(2):
        for side in sides:
            start, stop = side.rows[late]
            own_grad[start:stop, :] += side.take(5 + late, unit[start:stop])
    unit_grad = own_grad[...]
    inner = jnp.sum(raw * unit_grad, axis=1, keepdims=True)
    embed_grad = inverse * unit_grad - inverse * inverse * inverse * raw * inner
    grad_gram = lax.dot_general(
        embed_grad, embed_grad, (((1,), (1,)), ((), ())),
        precision=lax.Precision.HIGHEST, preferred_element_type=F32,
    )
    terms = jnp.sum(feat_gram * grad_gram, axis=0, keepdims=True)
    user_sq = jnp.sum(jnp.where(same_user, terms, 0.0), axis=1, keepdims=True)
    factor = bound / jnp.maximum(jnp.sqrt(user_sq), bound)
    clipped[...] = (factor * embed_grad).astype(BF16)

    def rows_of(core, ry):
        return clipped_all.at[(core * 4 + ry) * PAIRS:(core * 4 + ry + 1) * PAIRS, :]

    parts = []
    for o in range(1, Y):
        parts.append(net.push(clipped.at[:, lanes(c * 4 + shift(y, o, Y))], rows_of(0, 4 - o), at_y[o - 1]))
        parts.append(net.push(clipped.at[:, lanes(other * 4 + shift(y, o, Y))], rows_of(1, 4 - o), at_y_across[o - 1]))
    parts.append(net.push(clipped.at[:, lanes(other * 4 + y)], rows_of(1, 0), across))
    clipped_all[0:PAIRS, :] = clipped[:, lanes(k)]
    feats_cross.wait_recv()
    for copy in parts:
        copy.wait_recv()

    def rows(index):
        return pl.ds(pl.multiple_of(index * PADDED, 16), PADDED)

    x_moves = []
    for o in (1, 2, 3, 0):
        block = feats_all[pl.ds(pl.multiple_of(shift(x, o, X) * SHARE, 16), SHARE), :]
        part = jnp.dot(block, clipped_all[...], preferred_element_type=F32)
        for piece in range(Z):
            shares[o, piece, 0:BLOCK, :] = part[piece * BLOCK:(piece + 1) * BLOCK]
        shares_send[o] = shares[o].astype(BF16)
        if o:
            x_moves.append(net.push(shares_send.at[o, :, 0:32, :], x_recv.at[o - 1], at_x[o - 1]))
    z_moves = [
        net.push(shares_send.at[:, shift(z, o, Z), 32:PADDED, :], z_recv.at[o - 1], at_z[o - 1])
        for o in range(1, Z)
    ]
    total = shares[0, :, 0:32, :]
    for o in range(1, X):
        x_moves[o - 1].wait_recv()
        total = total + x_recv[o - 1].astype(F32)
    x_part[...] = total
    x_send[...] = total.astype(BF16)
    x_moves = [
        net.push(x_send.at[shift(z, o, Z)], x_recv_last.at[o - 1], at_z[o - 1]) for o in range(1, Z)
    ]
    total = shares[:, z, 32:PADDED, :]
    for o in range(1, Z):
        z_moves[o - 1].wait_recv()
        total = total + z_recv[o - 1].astype(F32)
    z_send[...] = total.astype(BF16)
    z_moves = [net.push(z_send.at[o], z_recv_last.at[o - 1], at_x[o - 1]) for o in range(1, X)]
    upper, lower = x_part[z], total[0]
    for o in range(1, X):
        z_moves[o - 1].wait_recv()
        lower = lower + z_recv_last[o - 1].astype(F32)
    for o in range(1, Z):
        x_moves[o - 1].wait_recv()
        upper = upper + x_recv_last[o - 1].astype(F32)
    grad = jnp.concatenate([upper, lower], axis=0)

    new_sum = state_tile[0] + grad
    update = new_sum + state_tile[1]
    for piece in range(8):
        first = 11 * (piece // 2) + 5 * (piece % 2)
        sums_send[piece] = new_sum[first:first + 8]

    square = jnp.sum((update * update).reshape(PADDED // 8, 8, 128), axis=0)
    at = 0
    for stage, targets in enumerate((at_z, at_x, at_y + [across] + at_y_across)):
        sq_send[stage] = square
        moves = [
            net.push(sq_send.at[stage], sq_recv.at[at + i], target)
            for i, target in enumerate(targets)
        ]
        for i, copy in enumerate(moves):
            copy.wait_recv()
            square = square + sq_recv[at + i]
        at += len(targets)
    norm = jnp.sqrt(jnp.sum(square, keepdims=True))
    cap = math.sqrt(W * E)
    shrink = cap / jnp.maximum(norm, cap)
    tile = (state_tile[2] - RATE * shrink * update).astype(BF16)

    z_tiles[rows(z), :] = tile
    moves = [net.push(z_tiles.at[rows(z), :], z_tiles.at[rows(z), :], target) for target in at_z]
    sums_out = Scatter(
        net, sums_send, sums_ref,
        [device(x, 2 * zl + i // 4, zh2 + (i // 2) % 2, i % 2) for i in range(8)],
        [
            jnp.logical_and(half_y == zl, owner_slot == i) for i in range(8)
        ],
        k,
    )
    sums_out.start()
    for copy in moves:
        copy.wait_recv()
    whole = z_tiles[...].astype(F32)
    whole = jnp.concatenate([whole[piece * PADDED:piece * PADDED + BLOCK] for piece in range(Z)], axis=0)
    weights_ref[x, :, lanes(k)] = whole.astype(BF16)

    half = SHARE // 2

    def low_piece(index, rows=(0, half)):
        return weights_ref.at[index, rows[0]:rows[1], lanes(c, 512)]

    def high_piece(away, shares=slice(0, X)):
        return weights_ref.at[shares, half:SHARE, lanes(c * 4 + shift(y, away, Y))]

    def send(piece, target):
        return net.push(piece, piece, target)

    moves_y = [send(weights_ref.at[x, 0:half, lanes(k)], target) for target in at_y]
    moves_x = [send(weights_ref.at[x, half:SHARE, lanes(k)], target) for target in at_x]
    arrive(moves_y)
    low_moves = [send(low_piece(x), target) for target in (x_up, x_down)]
    arrive(moves_x)
    high_moves = [send(high_piece(0), target) for target in (y_up, y_down)]
    given = [send(low_piece(x), across), send(high_piece(0), across)]
    far = []
    for copy, away, rows_sent, target in (
        (low_moves[0], 3, (0, 96), x_up), (low_moves[1], 1, (96, half), x_down)
    ):
        copy.wait_recv()
        index = shift(x, away, X)
        far.append(send(low_piece(index, rows_sent), target))
        given.append(send(low_piece(index), across))
    for copy, away, shares, target in (
        (high_moves[0], 3, slice(0, 2), y_up), (high_moves[1], 1, slice(2, 4), y_down)
    ):
        copy.wait_recv()
        far.append(send(high_piece(away, shares), target))
        given.append(send(high_piece(away), across))
    arrive(far)
    given += [send(low_piece(shift(x, 2, X)), across), send(high_piece(2), across)]
    arrive(given)
    sums_out.wait()
    state_out.wait_sent()
    sums_out.wait_sent()
    net.finish()


def body(
    image_feats, text_emb, projection, clip_norms, user_ids, grad_sum, init_weights, tree_noise
):
    c = lax.rem(lax.axis_index("col"), 2)
    state = jnp.pad(jnp.stack([grad_sum, tree_noise, init_weights]), ((0, 0), (4, 4), (0, 0)))
    state = lax.dynamic_slice(state, (0, 4 - 4 * c, 0), (3, 48, 128))
    state = state.reshape(3, 6, 8, 128).transpose(2, 0, 1, 3)
    state = jnp.pad(state, ((0, 0), (0, 0), (0, 2), (0, 0)))
    vmem = pl.BlockSpec(memory_space=pltpu.VMEM)
    weights, sums = pl.pallas_call(
        kernel,
        out_shape=(
            jax.ShapeDtypeStruct((X, SHARE, E), BF16),
            jax.ShapeDtypeStruct((8, 8, 128), F32),
        ),
        in_specs=[pl.BlockSpec(memory_space=pltpu.HBM)] * 6,
        out_specs=(vmem, vmem),
        scratch_shapes=[
            pltpu.VMEM((PAIRS, W), BF16),
            pltpu.VMEM((PAIRS, E), BF16),
            pltpu.VMEM((1, USERS), F32),
            pltpu.VMEM((1, PAIRS), jnp.int32),
            pltpu.VMEM((8, 3, 8, 128), F32),
            pltpu.VMEM((W, E), BF16),
            pltpu.VMEM((TEXTS, E), BF16),
            pltpu.VMEM((Z * PAIRS, E), BF16),
            pltpu.VMEM((PAIRS, E), F32),
            pltpu.VMEM((Z * PAIRS, E), F32),
            pltpu.VMEM((PAIRS, E), F32),
            pltpu.VMEM((IMAGES, CHUNK), BF16),
            pltpu.VMEM((IMAGES, CHUNK), BF16),
            pltpu.VMEM((7, HALF, E), BF16),
            pltpu.VMEM((7, HALF, E), BF16),
            pltpu.VMEM((7, HALF, E), BF16),
            pltpu.VMEM((7, HALF, E), BF16),
            pltpu.VMEM((7, 8, 128), F32),
            pltpu.VMEM((7, 8, 128), F32),
            pltpu.VMEM((7, 8, 128), F32),
            pltpu.VMEM((7, 8, 128), F32),
            pltpu.VMEM((W, 8 * PAIRS), BF16),
            pltpu.VMEM((PAIRS, E), BF16),
            pltpu.VMEM((8 * PAIRS, 128), BF16),
            pltpu.VMEM((X, Z, PADDED, 128), F32),
            pltpu.VMEM((X, Z, PADDED, 128), BF16),
            pltpu.VMEM((X - 1, Z, 32, 128), BF16),
            pltpu.VMEM((Z, 32, 128), F32),
            pltpu.VMEM((Z, 32, 128), BF16),
            pltpu.VMEM((Z - 1, 32, 128), BF16),
            pltpu.VMEM((Z - 1, X, 16, 128), BF16),
            pltpu.VMEM((X, 16, 128), BF16),
            pltpu.VMEM((X - 1, 16, 128), BF16),
            pltpu.VMEM((WIDE, 128), BF16),
            pltpu.VMEM((8, 3, 8, 128), F32),
            pltpu.VMEM((3, PADDED, 128), F32),
            pltpu.VMEM((8, 8, 128), F32),
            pltpu.VMEM((3, 8, 128), F32),
            pltpu.VMEM((17, 8, 128), F32),
            pltpu.SemaphoreType.DMA((6,)),
            pltpu.SemaphoreType.DMA((COPIES,)),
            pltpu.SemaphoreType.DMA((COPIES,)),
        ],
        compiler_params=pltpu.CompilerParams(
            collective_id=1, has_side_effects=True, vmem_limit_bytes=48 * 1024 * 1024
        ),
    )(
        image_feats, text_emb, projection, clip_norms.reshape(1, USERS),
        user_ids.reshape(1, PAIRS), state,
    )
    sums = sums[:, :6].transpose(1, 0, 2).reshape(48, 128)
    return weights.reshape(W, E), lax.dynamic_slice(sums, (4 * c, 0), (44, 128))


def solution(mesh):
    in_specs = (
        P(("row", "col"), None),
        P(("row", "col"), None),
        P(),
        P(("row", "col")),
        P(("row", "col")),
        P(("row", "col"), None),
        P(("row", "col"), None),
        P(("row", "col"), None),
    )
    out_specs = (P(), P(("row", "col"), None))
    return jax.shard_map(body, mesh=mesh, in_specs=in_specs, out_specs=out_specs, check_vma=False)
```

```python
import math

import jax
import jax.numpy as jnp
from jax import lax
from jax.experimental import pallas as pl
from jax.experimental.pallas import tpu as pltpu
from jax.sharding import PartitionSpec as P

LOGIT_SCALE = 32.0
LOGIT_BIAS = -5.0
RATE = 0.5
EPSILON = 1e-06

MESH = pl.DeviceIdType.MESH
X, Y, Z = 4, 4, 8
W, E, PAIRS, USERS = 1408, 1024, 128, 16
SHARE = W // X
BLOCK = SHARE // Z
PADDED = 48
WIDE = Z * PADDED
TEXTS = 2 * X * Y * PAIRS
CHUNK = 1024
IMAGES = 2 * PAIRS
HALF = PAIRS // 2
COPIES = 256
F32, BF16 = jnp.float32, jnp.bfloat16


def place():
    row, col = lax.axis_index("row"), lax.axis_index("col")
    x, zh = lax.div(row, 4), lax.rem(row, 4)
    y, zl, c = lax.div(col, 4), lax.rem(lax.div(col, 2), 2), lax.rem(col, 2)
    return x, y, zh * 2 + zl, c


def device(x, y, z, c):
    return (x * 4 + lax.div(z, 2), y * 4 + lax.rem(z, 2) * 2 + c)


def shift(value, by, size):
    return lax.rem(value + by, size)


class Copies:
    def __init__(self, send_sems, recv_sems):
        self.send_sems, self.recv_sems, self.used, self.all = send_sems, recv_sems, 0, []

    def reserve(self, count):
        self.used += count
        return self.used - count

    def make(self, src, dst, target, send_at, recv_at):
        return pltpu.make_async_remote_copy(
            src_ref=src,
            dst_ref=dst,
            send_sem=self.send_sems.at[send_at],
            recv_sem=self.recv_sems.at[recv_at],
            device_id=target,
            device_id_type=MESH,
        )

    def plan(self, src, dst, target):
        at = self.reserve(1)
        copy = self.make(src, dst, target, at, at)
        self.all.append(copy)
        return copy

    def push(self, src, dst, target):
        copy = self.plan(src, dst, target)
        copy.start()
        return copy

    def finish(self):
        for copy in self.all:
            copy.wait_send()


class Scatter:
    def __init__(self, net, src, dst, targets, is_self, mine):
        self.net, self.src, self.dst, self.targets, self.is_self, self.mine = net, src, dst, targets, is_self, mine
        self.at = net.reserve(8)

    def remote(self, i):
        return self.net.make(
            self.src.at[i], self.dst.at[self.mine], self.targets[i], self.at + i, self.at + self.mine
        )

    def local(self, i):
        sem = self.net.recv_sems.at[self.at + self.mine]
        return pltpu.make_async_copy(self.src.at[i], self.dst.at[self.mine], sem)

    def start(self):
        for i in range(8):
            pl.when(jnp.logical_not(self.is_self[i]))(self.remote(i).start)
            pl.when(self.is_self[i])(self.local(i).start)

    def wait(self):
        for i in range(8):
            self.net.make(self.src.at[i], self.dst.at[i], self.targets[i], self.at + i, self.at + i).wait_recv()

    def wait_sent(self):
        for i in range(8):
            pl.when(jnp.logical_not(self.is_self[i]))(self.remote(i).wait_send)


def kernel(
    feats_hbm, text_hbm, proj_hbm, norms_hbm, ids_hbm, state_hbm,
    weights_ref, sums_ref,
    feats_ref, text_ref, norms_ref, ids_row, state_ref, proj, texts, images, raw_ref, acc, own_grad, weigh0, weigh1,
    send_up, send_down, recv_up, recv_down, send_up_row, send_down_row, recv_up_row, recv_down_row,
    feats_all, clipped, clipped_all, shares, shares_send, x_recv, x_part, x_send, x_recv_last,
    z_recv, z_send, z_recv_last, z_tiles,
    state_recv, state_tile, sums_send, sq_send, sq_recv,
    load_sems, send_sems, recv_sems,
):
    x, y, z, c = place()
    col = lax.axis_index("col")
    k = c * 4 + y
    other = 1 - c
    zl = lax.rem(z, 2)
    at_x = [device(shift(x, o, X), y, z, c) for o in range(1, X)]
    at_y = [device(x, shift(y, o, Y), z, c) for o in range(1, Y)]
    at_z = [device(x, y, shift(z, o, Z), c) for o in range(1, Z)]
    across = device(x, y, z, other)
    at_y_across = [device(x, shift(y, o, Y), z, other) for o in range(1, Y)]
    flip = z + 1 - 2 * zl
    at_flip = [device(x, shift(y, o, Y), flip, cc) for o in range(Y) for cc in (c, other)][1:]
    x_up, x_down, y_up, y_down, z_up, z_down = at_x[0], at_x[2], at_y[0], at_y[2], at_z[0], at_z[6]

    loads = [
        pltpu.make_async_copy(src, dst, load_sems.at[i])
        for i, (src, dst) in enumerate((
            (feats_hbm, feats_ref), (proj_hbm, proj), (text_hbm, text_ref),
            (state_hbm, state_ref), (norms_hbm, norms_ref), (ids_hbm, ids_row),
        ))
    ]
    for load in loads:
        load.start()
    barrier = pltpu.get_barrier_semaphore()
    partners = at_x + at_y + at_z + [across] + at_y_across + at_flip
    for target in partners:
        pl.semaphore_signal(barrier, inc=1, device_id=target, device_id_type=MESH)
    pl.semaphore_wait(barrier, len(partners))
    net = Copies(send_sems, recv_sems)

    def lanes(index, width=128):
        return pl.ds(pl.multiple_of(index * width, width), width)

    for load in loads[:2]:
        load.wait()
    raw = jnp.dot(feats_ref[...], proj[...], preferred_element_type=F32)
    raw_ref[...] = raw
    inverse = lax.rsqrt(jnp.sum(raw * raw, axis=1, keepdims=True) + EPSILON)
    images[PAIRS:2 * PAIRS, :] = (raw * inverse).astype(BF16)

    def image_hop(source, target_slot, half, target):
        def rows_at(index):
            return images.at[index * PAIRS + half * HALF:index * PAIRS + (half + 1) * HALF, :]

        return net.plan(rows_at(source), rows_at(target_slot), target)

    up = [[image_hop(a, b, half, z_up) for half in (0, 1)] for a, b in ((1, 7), (7, 5), (5, 3))]
    down = [[image_hop(a, b, half, z_down) for half in (1, 0)] for a, b in ((1, 6), (6, 4), (4, 2))]
    up.append([image_hop(3, 0, 0, z_up)])
    down.append([image_hop(2, 0, 1, z_down)])
    for part in range(2):
        up[0][part].start()
        down[0][part].start()

    def turn(step, part):
        for ring in (up, down):
            ring[step][part].wait_recv()
            if part < len(ring[min(step + 1, 3)]) and step < 3:
                ring[step + 1][part].start()

    for load in loads[2:]:
        load.wait()
    text = text_ref[...].astype(F32)
    texts[0:PAIRS, :] = (
        text * lax.rsqrt(jnp.sum(text * text, axis=1, keepdims=True) + EPSILON)
    ).astype(BF16)

    def slot(rx, ry, rows, core=0):
        base = (core * 16 + rx * 4 + ry) * PAIRS
        return texts.at[base + rows[0]:base + rows[1], :]

    def hop(axis, up, rx, ry, rows):
        step = 3 if up else 1
        if axis == "x":
            return net.plan(slot(rx, ry, rows), slot((rx + step) % 4, ry, rows), x_up if up else x_down)
        return net.plan(slot(rx, ry, rows), slot(rx, (ry + step) % 4, rows), y_up if up else y_down)

    text_crossings = []

    def cross(rx, ry, rows):
        text_crossings.append(net.push(slot(rx, ry, rows), slot(rx, ry, rows, 1), across))

    class Half:
        def __init__(self, first, second, low):
            self.rows, self.swap = (low, low + 64), first == "y"
            self.parts = ((low, low + 32), (low + 32, low + 64))
            r, p = self.rows, self.parts
            self.first = [hop(first, up, 0, 0, r) for up in (True, False)]
            self.relay = [hop(first, up, *self.at(3 if up else 1, 0), p[0 if up else 1]) for up in (True, False)]
            self.second = [[hop(second, up, *self.at(a, 0), r) for up in (True, False)] for a in range(4)]
            self.last = [
                [hop(second, up, *self.at(a, 3 if up else 1), p[0 if up else 1]) for up in (True, False)]
                for a in range(4)
            ]

        def at(self, a, b):
            return (b, a) if self.swap else (a, b)

        def open(self, a):
            for copy in self.second[a]:
                copy.start()

        def got_first(self, i):
            a = (3, 1)[i]
            self.first[i].wait_recv()
            self.relay[i].start()
            self.open(a)
            cross(*self.at(a, 0), self.rows)

        def got_relay(self):
            for copy in self.relay:
                copy.wait_recv()
            self.open(2)
            cross(*self.at(2, 0), self.rows)

        def got_second(self, a):
            for i in range(2):
                self.second[a][i].wait_recv()
                self.last[a][i].start()
                cross(*self.at(a, (3, 1)[i]), self.rows)

        def got_last(self, a):
            for copy in self.last[a]:
                copy.wait_recv()
            cross(*self.at(a, 2), self.rows)

    def arrive(copies):
        for copy in copies:
            copy.wait_recv()

    low, high = Half("x", "y", 0), Half("y", "x", 64)
    halves = (low, high)
    for half in halves:
        for copy in half.first:
            copy.start()
    for half in halves:
        half.open(0)
    cross(0, 0, (0, PAIRS))

    feats_all[:, 0:PAIRS] = feats_ref[...].T
    acc[...] = jnp.zeros_like(acc)
    shares[...] = jnp.zeros_like(shares)
    feat_gram = lax.dot_general(
        feats_ref[...], feats_ref[...], (((1,), (1,)), ((), ())), preferred_element_type=F32
    )
    local_row = (ids_row[...] - (lax.axis_index("row") * 16 + col) * USERS).astype(F32)
    square_shape = (PAIRS, PAIRS)
    diagonal = lax.broadcasted_iota(jnp.int32, square_shape, 0) == lax.broadcasted_iota(
        jnp.int32, square_shape, 1
    )
    local_column = jnp.sum(jnp.where(diagonal, local_row, 0.0), axis=1, keepdims=True)
    same_user = local_column == local_row
    users = lax.broadcasted_iota(jnp.int32, (PAIRS, USERS), 1).astype(F32)
    bound = jnp.sum(jnp.where(local_column == users, norms_ref[...], 0.0), axis=1, keepdims=True)
    feat_gram = jnp.where(same_user, feat_gram, 0.0)

    owner_slot = (lax.rem(y, 2) * 2 + zl) * 2 + c
    zh2 = z - zl
    half_y = lax.div(y, 2)
    state_out = Scatter(
        net, state_ref, state_recv,
        [device(x, i % 4, zh2 + half_y, i // 4) for i in range(8)],
        [jnp.logical_and(zl == half_y, k == i) for i in range(8)],
        owner_slot,
    )

    def both(event, at):
        for half in halves:
            event(half, at)

    both(Half.got_first, 0)
    turn(0, 0)
    both(Half.got_first, 1)
    turn(0, 1)
    both(Half.got_second, 0)
    for half in halves:
        half.got_relay()
    turn(1, 0)
    both(Half.got_last, 0)
    both(Half.got_second, 3)
    turn(1, 1)
    both(Half.got_second, 1)
    turn(2, 0)
    both(Half.got_second, 2)
    both(Half.got_last, 3)
    both(Half.got_last, 1)
    turn(2, 1)
    both(Half.got_last, 2)

    def feats_slot(ry, rows=(0, W)):
        return feats_all.at[rows[0]:rows[1], ry * PAIRS:(ry + 1) * PAIRS]

    feats_near = [net.plan(feats_slot(0), feats_slot(3), y_up), net.plan(feats_slot(0), feats_slot(1), y_down)]
    feats_far = [
        net.plan(feats_slot(3, (0, W // 2)), feats_slot(2, (0, W // 2)), y_up),
        net.plan(feats_slot(1, (W // 2, W)), feats_slot(2, (W // 2, W)), y_down),
    ]
    feats_cross = net.plan(feats_all.at[:, 0:512], feats_all.at[:, 512:1024], across)
    def feats_open():
        for copy in feats_near:
            copy.start()

    def feats_on():
        for near, far in zip(feats_near, feats_far):
            near.wait_recv()
            far.start()

    def feats_over():
        arrive(feats_far)
        feats_cross.start()

    pick = lax.broadcasted_iota(jnp.int32, (HALF, 128), 0) == lax.broadcasted_iota(
        jnp.int32, (HALF, 128), 1
    )

    def pack(dst, dst_row, full, unit):
        coefficient = jnp.sum(full * unit, axis=1, keepdims=True)
        dst[...] = (full - coefficient * unit).astype(BF16)
        row = jnp.sum(jnp.where(pick, coefficient, 0.0), axis=0, keepdims=True)
        dst_row[...] = jnp.broadcast_to(row, (8, 128))

    def unpack(src, src_row, unit):
        coefficient = jnp.sum(jnp.where(pick, src_row[0:1, :], 0.0), axis=1, keepdims=True)
        return src[...].astype(F32) + coefficient * unit

    class Side:
        def __init__(self, first, come, sends, recvs, send_rows, recv_rows, target):
            self.blocks, self.sends, self.recvs = (0, first, first + 2, first + 4), sends, recvs
            self.send_rows, self.recv_rows = send_rows, recv_rows
            self.rows = ((64 - come, 128 - come), (come, come + 64))
            self.copies = [
                (
                    net.plan(sends.at[i], recvs.at[i], target),
                    net.plan(send_rows.at[i], recv_rows.at[i], target),
                )
                for i in range(7)
            ]

        def take(self, i, unit):
            arrive(self.copies[i])
            return unpack(self.recvs.at[i], self.recv_rows.at[i], unit)

        def give(self, hop, late):
            i = 2 * hop - 1 + late
            base = self.blocks[hop] * PAIRS
            start, stop = self.rows[late]
            unit = images[base + start:base + stop, :].astype(F32)
            full = LOGIT_SCALE * acc[base + start:base + stop, :]
            if hop > 1 or (hop == 1 and late):
                full = full + self.take(i - 2, unit)
            pack(self.sends.at[i], self.send_rows.at[i], full, unit)
            for copy in self.copies[i]:
                copy.start()

    sides = (
        Side(2, 0, send_up, recv_up, send_up_row, recv_up_row, z_up),
        Side(3, 64, send_down, recv_down, send_down_row, recv_down_row, z_down),
    )

    def give(hop, late):
        for side in sides:
            side.give(hop, late)

    buffers = (weigh0, weigh1)

    def grid_step(rows, count, events):
        def weigh(n):
            cosine = lax.dot_general(
                images[rows, :], texts[n * CHUNK:(n + 1) * CHUNK, :],
                (((1,), (1,)), ((), ())), preferred_element_type=F32,
            )
            pair = 0.5 + 0.5 * jnp.tanh(0.5 * LOGIT_SCALE * cosine + 0.5 * LOGIT_BIAS)
            buffers[n % 2][0:count, :] = pair.astype(BF16)

        def fold(n):
            acc[rows, :] += jnp.dot(
                buffers[n % 2][0:count, :], texts[n * CHUNK:(n + 1) * CHUNK, :],
                preferred_element_type=F32,
            )

        for n in range(TEXTS // CHUNK):
            events(n)
            weigh(n)
            if n > 0:
                fold(n - 1)
        fold(TEXTS // CHUNK - 1)

    def open_events(n):
        if n == 0:
            feats_open()
            state_out.start()
        if n == 2:
            arrive(text_crossings)

    schedule = {
        (2, 0): [lambda: give(1, 0), lambda: give(1, 1)],
        (2, 1): [feats_on],
        (3, 0): [lambda: give(2, 0)],
        (3, 2): [lambda: give(2, 1), feats_over],
    }

    def pair_step(step, carry):
        def events(n):
            for (at, part), todo in schedule.items():
                if part == n:

                    @pl.when(step == at)
                    def _(todo=todo):
                        for event in todo:
                            event()

        grid_step(pl.ds(pl.multiple_of(step * IMAGES, IMAGES), IMAGES), IMAGES, events)
        return carry

    grid_step(slice(PAIRS, 2 * PAIRS), PAIRS, open_events)
    turn(3, 0)
    grid_step(slice(0, PAIRS), PAIRS, lambda n: None)
    give(0, 1)
    lax.fori_loop(1, 4, pair_step, 0)
    give(3, 0)
    give(3, 1)
    unit = images[PAIRS:2 * PAIRS, :].astype(F32)
    text = texts[0:PAIRS, :].astype(F32)
    cosine = jnp.sum(unit * text, axis=1, keepdims=True)
    sigmoid = 0.5 + 0.5 * jnp.tanh(0.5 * LOGIT_SCALE * cosine + 0.5 * LOGIT_BIAS)
    change = (sigmoid - 1.0).astype(BF16).astype(F32) - sigmoid.astype(BF16).astype(F32)
    own_grad[...] = LOGIT_SCALE * (acc[PAIRS:2 * PAIRS, :] + change * text)

    state_out.wait()
    state_tile[...] = jnp.zeros_like(state_tile)
    for piece in range(8):
        first = 11 * (piece // 2) + 5 * (piece % 2)
        for a in range(3):
            state_tile[a, first:first + 6, :] += state_recv[piece, a, 0:6, :]

    raw = raw_ref[...]
    unit = images[PAIRS:2 * PAIRS, :].astype(F32)
    for late in range(2):
        for side in sides:
            start, stop = side.rows[late]
            own_grad[start:stop, :] += side.take(5 + late, unit[start:stop])
    unit_grad = own_grad[...]
    inner = jnp.sum(raw * unit_grad, axis=1, keepdims=True)
    embed_grad = inverse * unit_grad - inverse * inverse * inverse * raw * inner
    grad_gram = lax.dot_general(
        embed_grad, embed_grad, (((1,), (1,)), ((), ())),
        precision=lax.Precision.HIGHEST, preferred_element_type=F32,
    )
    terms = jnp.sum(feat_gram * grad_gram, axis=0, keepdims=True)
    user_sq = jnp.sum(jnp.where(same_user, terms, 0.0), axis=1, keepdims=True)
    factor = bound / jnp.maximum(jnp.sqrt(user_sq), bound)
    clipped[...] = (factor * embed_grad).astype(BF16)

    def rows_of(core, ry):
        return clipped_all.at[(core * 4 + ry) * PAIRS:(core * 4 + ry + 1) * PAIRS, :]

    parts = []
    for o in range(1, Y):
        parts.append(net.push(clipped.at[:, lanes(c * 4 + shift(y, o, Y))], rows_of(0, 4 - o), at_y[o - 1]))
        parts.append(net.push(clipped.at[:, lanes(other * 4 + shift(y, o, Y))], rows_of(1, 4 - o), at_y_across[o - 1]))
    parts.append(net.push(clipped.at[:, lanes(other * 4 + y)], rows_of(1, 0), across))
    clipped_all[0:PAIRS, :] = clipped[:, lanes(k)]
    feats_cross.wait_recv()
    for copy in parts:
        copy.wait_recv()

    def rows(index):
        return pl.ds(pl.multiple_of(index * PADDED, 16), PADDED)

    x_moves = []
    for o in (1, 2, 3, 0):
        block = feats_all[pl.ds(pl.multiple_of(shift(x, o, X) * SHARE, 16), SHARE), :]
        part = jnp.dot(block, clipped_all[...], preferred_element_type=F32)
        for piece in range(Z):
            shares[o, piece, 0:BLOCK, :] = part[piece * BLOCK:(piece + 1) * BLOCK]
        shares_send[o] = shares[o].astype(BF16)
        if o:
            x_moves.append(net.push(shares_send.at[o, :, 0:32, :], x_recv.at[o - 1], at_x[o - 1]))
    z_moves = [
        net.push(shares_send.at[:, shift(z, o, Z), 32:PADDED, :], z_recv.at[o - 1], at_z[o - 1])
        for o in range(1, Z)
    ]
    total = shares[0, :, 0:32, :]
    for o in range(1, X):
        x_moves[o - 1].wait_recv()
        total = total + x_recv[o - 1].astype(F32)
    x_part[...] = total
    x_send[...] = total.astype(BF16)
    x_moves = [
        net.push(x_send.at[shift(z, o, Z)], x_recv_last.at[o - 1], at_z[o - 1]) for o in range(1, Z)
    ]
    total = shares[:, z, 32:PADDED, :]
    for o in range(1, Z):
        z_moves[o - 1].wait_recv()
        total = total + z_recv[o - 1].astype(F32)
    z_send[...] = total.astype(BF16)
    z_moves = [net.push(z_send.at[o], z_recv_last.at[o - 1], at_x[o - 1]) for o in range(1, X)]
    upper, lower = x_part[z], total[0]
    for o in range(1, X):
        z_moves[o - 1].wait_recv()
        lower = lower + z_recv_last[o - 1].astype(F32)
    for o in range(1, Z):
        x_moves[o - 1].wait_recv()
        upper = upper + x_recv_last[o - 1].astype(F32)
    grad = jnp.concatenate([upper, lower], axis=0)

    new_sum = state_tile[0] + grad
    update = new_sum + state_tile[1]
    for piece in range(8):
        first = 11 * (piece // 2) + 5 * (piece % 2)
        sums_send[piece] = new_sum[first:first + 8]

    square = jnp.sum((update * update).reshape(PADDED // 8, 8, 128), axis=0)
    at = 0
    for stage, targets in enumerate((at_z, at_x, at_y + [across] + at_y_across)):
        sq_send[stage] = square
        moves = [
            net.push(sq_send.at[stage], sq_recv.at[at + i], target)
            for i, target in enumerate(targets)
        ]
        for i, copy in enumerate(moves):
            copy.wait_recv()
            square = square + sq_recv[at + i]
        at += len(targets)
    norm = jnp.sqrt(jnp.sum(square, keepdims=True))
    cap = math.sqrt(W * E)
    shrink = cap / jnp.maximum(norm, cap)
    tile = (state_tile[2] - RATE * shrink * update).astype(BF16)

    z_tiles[rows(z), :] = tile
    moves = [net.push(z_tiles.at[rows(z), :], z_tiles.at[rows(z), :], target) for target in at_z]
    sums_out = Scatter(
        net, sums_send, sums_ref,
        [device(x, 2 * zl + i // 4, zh2 + (i // 2) % 2, i % 2) for i in range(8)],
        [
            jnp.logical_and(half_y == zl, owner_slot == i) for i in range(8)
        ],
        k,
    )
    sums_out.start()
    for copy in moves:
        copy.wait_recv()
    whole = z_tiles[...].astype(F32)
    whole = jnp.concatenate([whole[piece * PADDED:piece * PADDED + BLOCK] for piece in range(Z)], axis=0)
    weights_ref[x, :, lanes(k)] = whole.astype(BF16)

    half = SHARE // 2

    def low_piece(index, rows=(0, half)):
        return weights_ref.at[index, rows[0]:rows[1], lanes(c, 512)]

    def high_piece(away, shares=slice(0, X)):
        return weights_ref.at[shares, half:SHARE, lanes(c * 4 + shift(y, away, Y))]

    def send(piece, target):
        return net.push(piece, piece, target)

    moves_y = [send(weights_ref.at[x, 0:half, lanes(k)], target) for target in at_y]
    moves_x = [send(weights_ref.at[x, half:SHARE, lanes(k)], target) for target in at_x]
    arrive(moves_y)
    low_moves = [send(low_piece(x), target) for target in (x_up, x_down)]
    arrive(moves_x)
    high_moves = [send(high_piece(0), target) for target in (y_up, y_down)]
    given = [send(low_piece(x), across), send(high_piece(0), across)]
    far = []
    for copy, away, rows_sent, target in (
        (low_moves[0], 3, (0, 96), x_up), (low_moves[1], 1, (96, half), x_down)
    ):
        copy.wait_recv()
        index = shift(x, away, X)
        far.append(send(low_piece(index, rows_sent), target))
        given.append(send(low_piece(index), across))
    for copy, away, shares, target in (
        (high_moves[0], 3, slice(0, 2), y_up), (high_moves[1], 1, slice(2, 4), y_down)
    ):
        copy.wait_recv()
        far.append(send(high_piece(away, shares), target))
        given.append(send(high_piece(away), across))
    arrive(far)
    given += [send(low_piece(shift(x, 2, X)), across), send(high_piece(2), across)]
    arrive(given)
    sums_out.wait()
    state_out.wait_sent()
    sums_out.wait_sent()
    net.finish()


def body(
    image_feats, text_emb, projection, clip_norms, user_ids, grad_sum, init_weights, tree_noise
):
    c = lax.rem(lax.axis_index("col"), 2)
    state = jnp.pad(jnp.stack([grad_sum, tree_noise, init_weights]), ((0, 0), (4, 4), (0, 0)))
    state = lax.dynamic_slice(state, (0, 4 - 4 * c, 0), (3, 48, 128))
    state = state.reshape(3, 6, 8, 128).transpose(2, 0, 1, 3)
    state = jnp.pad(state, ((0, 0), (0, 0), (0, 2), (0, 0)))
    vmem = pl.BlockSpec(memory_space=pltpu.VMEM)
    weights, sums = pl.pallas_call(
        kernel,
        out_shape=(
            jax.ShapeDtypeStruct((X, SHARE, E), BF16),
            jax.ShapeDtypeStruct((8, 8, 128), F32),
        ),
        in_specs=[pl.BlockSpec(memory_space=pltpu.HBM)] * 6,
        out_specs=(vmem, vmem),
        scratch_shapes=[
            pltpu.VMEM((PAIRS, W), BF16),
            pltpu.VMEM((PAIRS, E), BF16),
            pltpu.VMEM((1, USERS), F32),
            pltpu.VMEM((1, PAIRS), jnp.int32),
            pltpu.VMEM((8, 3, 8, 128), F32),
            pltpu.VMEM((W, E), BF16),
            pltpu.VMEM((TEXTS, E), BF16),
            pltpu.VMEM((Z * PAIRS, E), BF16),
            pltpu.VMEM((PAIRS, E), F32),
            pltpu.VMEM((Z * PAIRS, E), F32),
            pltpu.VMEM((PAIRS, E), F32),
            pltpu.VMEM((IMAGES, CHUNK), BF16),
            pltpu.VMEM((IMAGES, CHUNK), BF16),
            pltpu.VMEM((7, HALF, E), BF16),
            pltpu.VMEM((7, HALF, E), BF16),
            pltpu.VMEM((7, HALF, E), BF16),
            pltpu.VMEM((7, HALF, E), BF16),
            pltpu.VMEM((7, 8, 128), F32),
            pltpu.VMEM((7, 8, 128), F32),
            pltpu.VMEM((7, 8, 128), F32),
            pltpu.VMEM((7, 8, 128), F32),
            pltpu.VMEM((W, 8 * PAIRS), BF16),
            pltpu.VMEM((PAIRS, E), BF16),
            pltpu.VMEM((8 * PAIRS, 128), BF16),
            pltpu.VMEM((X, Z, PADDED, 128), F32),
            pltpu.VMEM((X, Z, PADDED, 128), BF16),
            pltpu.VMEM((X - 1, Z, 32, 128), BF16),
            pltpu.VMEM((Z, 32, 128), F32),
            pltpu.VMEM((Z, 32, 128), BF16),
            pltpu.VMEM((Z - 1, 32, 128), BF16),
            pltpu.VMEM((Z - 1, X, 16, 128), BF16),
            pltpu.VMEM((X, 16, 128), BF16),
            pltpu.VMEM((X - 1, 16, 128), BF16),
            pltpu.VMEM((WIDE, 128), BF16),
            pltpu.VMEM((8, 3, 8, 128), F32),
            pltpu.VMEM((3, PADDED, 128), F32),
            pltpu.VMEM((8, 8, 128), F32),
            pltpu.VMEM((3, 8, 128), F32),
            pltpu.VMEM((17, 8, 128), F32),
            pltpu.SemaphoreType.DMA((6,)),
            pltpu.SemaphoreType.DMA((COPIES,)),
            pltpu.SemaphoreType.DMA((COPIES,)),
        ],
        compiler_params=pltpu.CompilerParams(
            collective_id=1, has_side_effects=True, vmem_limit_bytes=48 * 1024 * 1024
        ),
    )(
        image_feats, text_emb, projection, clip_norms.reshape(1, USERS),
        user_ids.reshape(1, PAIRS), state,
    )
    sums = sums[:, :6].transpose(1, 0, 2).reshape(48, 128)
    return weights.reshape(W, E), lax.dynamic_slice(sums, (4 * c, 0), (44, 128))


def solution(mesh):
    in_specs = (
        P(("row", "col"), None),
        P(("row", "col"), None),
        P(),
        P(("row", "col")),
        P(("row", "col")),
        P(("row", "col"), None),
        P(("row", "col"), None),
        P(("row", "col"), None),
    )
    out_specs = (P(), P(("row", "col"), None))
    return jax.shard_map(body, mesh=mesh, in_specs=in_specs, out_specs=out_specs, check_vma=False)
```

```python
import math

import jax
import jax.numpy as jnp
from jax import lax
from jax.experimental import pallas as pl
from jax.experimental.pallas import tpu as pltpu
from jax.sharding import PartitionSpec as P

LOGIT_SCALE = 32.0
LOGIT_BIAS = -5.0
RATE = 0.5
EPSILON = 1e-06

MESH = pl.DeviceIdType.MESH
X, Y, Z = 4, 4, 8
W, E, PAIRS, USERS = 1408, 1024, 128, 16
SHARE = W // X
BLOCK = SHARE // Z
PADDED = 48
WIDE = Z * PADDED
TEXTS = 2 * X * Y * PAIRS
CHUNK = 1024
IMAGES = 2 * PAIRS
HALF = PAIRS // 2
COPIES = 256
F32, BF16 = jnp.float32, jnp.bfloat16


def place():
    row, col = lax.axis_index("row"), lax.axis_index("col")
    x, zh = lax.div(row, 4), lax.rem(row, 4)
    y, zl, c = lax.div(col, 4), lax.rem(lax.div(col, 2), 2), lax.rem(col, 2)
    return x, y, zh * 2 + zl, c


def device(x, y, z, c):
    return (x * 4 + lax.div(z, 2), y * 4 + lax.rem(z, 2) * 2 + c)


def shift(value, by, size):
    return lax.rem(value + by, size)


class Copies:
    def __init__(self, send_sems, recv_sems):
        self.send_sems, self.recv_sems, self.used, self.all = send_sems, recv_sems, 0, []

    def reserve(self, count):
        self.used += count
        return self.used - count

    def make(self, src, dst, target, send_at, recv_at):
        return pltpu.make_async_remote_copy(
            src_ref=src,
            dst_ref=dst,
            send_sem=self.send_sems.at[send_at],
            recv_sem=self.recv_sems.at[recv_at],
            device_id=target,
            device_id_type=MESH,
        )

    def plan(self, src, dst, target):
        at = self.reserve(1)
        copy = self.make(src, dst, target, at, at)
        self.all.append(copy)
        return copy

    def push(self, src, dst, target):
        copy = self.plan(src, dst, target)
        copy.start()
        return copy

    def finish(self):
        for copy in self.all:
            copy.wait_send()


class Scatter:
    def __init__(self, net, src, dst, targets, is_self, mine):
        self.net, self.src, self.dst, self.targets, self.is_self, self.mine = net, src, dst, targets, is_self, mine
        self.at = net.reserve(8)

    def remote(self, i):
        return self.net.make(
            self.src.at[i], self.dst.at[self.mine], self.targets[i], self.at + i, self.at + self.mine
        )

    def local(self, i):
        sem = self.net.recv_sems.at[self.at + self.mine]
        return pltpu.make_async_copy(self.src.at[i], self.dst.at[self.mine], sem)

    def start(self):
        for i in range(8):
            pl.when(jnp.logical_not(self.is_self[i]))(self.remote(i).start)
            pl.when(self.is_self[i])(self.local(i).start)

    def wait(self):
        for i in range(8):
            self.net.make(self.src.at[i], self.dst.at[i], self.targets[i], self.at + i, self.at + i).wait_recv()

    def wait_sent(self):
        for i in range(8):
            pl.when(jnp.logical_not(self.is_self[i]))(self.remote(i).wait_send)


def kernel(
    feats_hbm, text_hbm, proj_hbm, state_hbm,
    weights_ref, sums_ref,
    feats_ref, text_ref, state_ref, proj, texts, images, raw_ref, acc, own_grad, weigh0, weigh1,
    send_up, send_down, recv_up, recv_down, send_up_row, send_down_row, recv_up_row, recv_down_row,
    feats_all, clipped, clipped_all, shares, shares_send, x_recv, x_part, x_send, x_recv_last,
    z_recv, z_send, z_recv_last, start_all, update_all,
    state_recv, state_tile, sums_send, sq_send, sq_recv,
    load_sems, send_sems, recv_sems,
):
    x, y, z, c = place()
    col = lax.axis_index("col")
    k = c * 4 + y
    other = 1 - c
    zl = lax.rem(z, 2)
    at_x = [device(shift(x, o, X), y, z, c) for o in range(1, X)]
    at_y = [device(x, shift(y, o, Y), z, c) for o in range(1, Y)]
    at_z = [device(x, y, shift(z, o, Z), c) for o in range(1, Z)]
    across = device(x, y, z, other)
    at_y_across = [device(x, shift(y, o, Y), z, other) for o in range(1, Y)]
    flip = z + 1 - 2 * zl
    at_flip = [device(x, shift(y, o, Y), flip, cc) for o in range(Y) for cc in (c, other)][1:]
    x_up, x_down, y_up, y_down, z_up, z_down = at_x[0], at_x[2], at_y[0], at_y[2], at_z[0], at_z[6]

    loads = [
        pltpu.make_async_copy(src, dst, load_sems.at[i])
        for i, (src, dst) in enumerate((
            (feats_hbm, feats_ref), (proj_hbm, proj), (text_hbm, text_ref),
            (state_hbm, state_ref),
        ))
    ]
    for load in loads:
        load.start()
    barrier = pltpu.get_barrier_semaphore()
    partners = at_x + at_y + at_z + [across] + at_y_across + at_flip
    for target in partners:
        pl.semaphore_signal(barrier, inc=1, device_id=target, device_id_type=MESH)
    pl.semaphore_wait(barrier, len(partners))
    net = Copies(send_sems, recv_sems)

    def lanes(index, width=128):
        return pl.ds(pl.multiple_of(index * width, width), width)

    for load in loads[:2]:
        load.wait()
    raw = jnp.dot(feats_ref[...], proj[...], preferred_element_type=F32)
    raw_ref[...] = raw
    inverse = lax.rsqrt(jnp.sum(raw * raw, axis=1, keepdims=True) + EPSILON)
    images[PAIRS:2 * PAIRS, :] = (raw * inverse).astype(BF16)

    def image_hop(source, target_slot, half, target):
        def rows_at(index):
            return images.at[index * PAIRS + half * HALF:index * PAIRS + (half + 1) * HALF, :]

        return net.plan(rows_at(source), rows_at(target_slot), target)

    up = [[image_hop(a, b, half, z_up) for half in (0, 1)] for a, b in ((1, 7), (7, 5), (5, 3))]
    down = [[image_hop(a, b, half, z_down) for half in (1, 0)] for a, b in ((1, 6), (6, 4), (4, 2))]
    up.append([image_hop(3, 0, 0, z_up)])
    down.append([image_hop(2, 0, 1, z_down)])
    for part in range(2):
        up[0][part].start()
        down[0][part].start()

    def turn(step, part):
        for ring in (up, down):
            ring[step][part].wait_recv()
            if part < len(ring[min(step + 1, 3)]) and step < 3:
                ring[step + 1][part].start()

    for load in loads[2:]:
        load.wait()
    text = text_ref[...].astype(F32)
    texts[0:PAIRS, :] = (
        text * lax.rsqrt(jnp.sum(text * text, axis=1, keepdims=True) + EPSILON)
    ).astype(BF16)

    def slot(rx, ry, rows, core=0):
        base = (core * 16 + rx * 4 + ry) * PAIRS
        return texts.at[base + rows[0]:base + rows[1], :]

    def hop(axis, up, rx, ry, rows):
        step = 3 if up else 1
        if axis == "x":
            return net.plan(slot(rx, ry, rows), slot((rx + step) % 4, ry, rows), x_up if up else x_down)
        return net.plan(slot(rx, ry, rows), slot(rx, (ry + step) % 4, rows), y_up if up else y_down)

    text_crossings = []

    def cross(rx, ry, rows):
        text_crossings.append(net.push(slot(rx, ry, rows), slot(rx, ry, rows, 1), across))

    class Half:
        def __init__(self, first, second, low):
            self.rows, self.swap = (low, low + 64), first == "y"
            self.parts = ((low, low + 32), (low + 32, low + 64))
            r, p = self.rows, self.parts
            self.first = [hop(first, up, 0, 0, r) for up in (True, False)]
            self.relay = [hop(first, up, *self.at(3 if up else 1, 0), p[0 if up else 1]) for up in (True, False)]
            self.second = [[hop(second, up, *self.at(a, 0), r) for up in (True, False)] for a in range(4)]
            self.last = [
                [hop(second, up, *self.at(a, 3 if up else 1), p[0 if up else 1]) for up in (True, False)]
                for a in range(4)
            ]

        def at(self, a, b):
            return (b, a) if self.swap else (a, b)

        def open(self, a):
            for copy in self.second[a]:
                copy.start()

        def got_first(self, i):
            a = (3, 1)[i]
            self.first[i].wait_recv()
            self.relay[i].start()
            self.open(a)
            cross(*self.at(a, 0), self.rows)

        def got_relay(self):
            for copy in self.relay:
                copy.wait_recv()
            self.open(2)
            cross(*self.at(2, 0), self.rows)

        def got_second(self, a):
            for i in range(2):
                self.second[a][i].wait_recv()
                self.last[a][i].start()
                cross(*self.at(a, (3, 1)[i]), self.rows)

        def got_last(self, a):
            for copy in self.last[a]:
                copy.wait_recv()
            cross(*self.at(a, 2), self.rows)

    def arrive(copies):
        for copy in copies:
            copy.wait_recv()

    low, high = Half("x", "y", 0), Half("y", "x", 64)
    halves = (low, high)
    for half in halves:
        for copy in half.first:
            copy.start()
    for half in halves:
        half.open(0)
    cross(0, 0, (0, PAIRS))

    feats_all[:, 0:PAIRS] = feats_ref[...].T
    acc[...] = jnp.zeros_like(acc)
    shares[...] = jnp.zeros_like(shares)
    feat_gram = lax.dot_general(
        feats_ref[...], feats_ref[...], (((1,), (1,)), ((), ())), preferred_element_type=F32
    )
    local_row = state_ref[0, 0, 6:7, :] - ((lax.axis_index("row") * 16 + col) * USERS).astype(F32)
    square_shape = (PAIRS, PAIRS)
    diagonal = lax.broadcasted_iota(jnp.int32, square_shape, 0) == lax.broadcasted_iota(
        jnp.int32, square_shape, 1
    )
    local_column = jnp.sum(jnp.where(diagonal, local_row, 0.0), axis=1, keepdims=True)
    same_user = local_column == local_row
    users = lax.broadcasted_iota(jnp.int32, (PAIRS, USERS), 1).astype(F32)
    bound = jnp.sum(jnp.where(local_column == users, state_ref[0, 0, 7:8, 0:USERS], 0.0), axis=1, keepdims=True)
    feat_gram = jnp.where(same_user, feat_gram, 0.0)

    owner_slot = (lax.rem(y, 2) * 2 + zl) * 2 + c
    zh2 = z - zl
    half_y = lax.div(y, 2)
    state_out = Scatter(
        net, state_ref, state_recv,
        [device(x, i % 4, zh2 + half_y, i // 4) for i in range(8)],
        [jnp.logical_and(zl == half_y, k == i) for i in range(8)],
        owner_slot,
    )

    def both(event, at):
        for half in halves:
            event(half, at)

    both(Half.got_first, 0)
    turn(0, 0)
    both(Half.got_first, 1)
    turn(0, 1)
    both(Half.got_second, 0)
    for half in halves:
        half.got_relay()
    turn(1, 0)
    both(Half.got_last, 0)
    both(Half.got_second, 3)
    turn(1, 1)
    both(Half.got_second, 1)
    turn(2, 0)
    both(Half.got_second, 2)
    both(Half.got_last, 3)
    both(Half.got_last, 1)
    turn(2, 1)
    both(Half.got_last, 2)

    def feats_slot(ry, rows=(0, W)):
        return feats_all.at[rows[0]:rows[1], ry * PAIRS:(ry + 1) * PAIRS]

    feats_near = [net.plan(feats_slot(0), feats_slot(3), y_up), net.plan(feats_slot(0), feats_slot(1), y_down)]
    feats_far = [
        net.plan(feats_slot(3, (0, W // 2)), feats_slot(2, (0, W // 2)), y_up),
        net.plan(feats_slot(1, (W // 2, W)), feats_slot(2, (W // 2, W)), y_down),
    ]
    feats_cross = net.plan(feats_all.at[:, 0:512], feats_all.at[:, 512:1024], across)
    def feats_open():
        for copy in feats_near:
            copy.start()

    def feats_on():
        for near, far in zip(feats_near, feats_far):
            near.wait_recv()
            far.start()

    def feats_over():
        arrive(feats_far)
        feats_cross.start()

    pick = lax.broadcasted_iota(jnp.int32, (HALF, 128), 0) == lax.broadcasted_iota(
        jnp.int32, (HALF, 128), 1
    )

    def pack(dst, dst_row, full, unit):
        coefficient = jnp.sum(full * unit, axis=1, keepdims=True)
        dst[...] = (full - coefficient * unit).astype(BF16)
        row = jnp.sum(jnp.where(pick, coefficient, 0.0), axis=0, keepdims=True)
        dst_row[...] = jnp.broadcast_to(row, (8, 128))

    def unpack(src, src_row, unit):
        coefficient = jnp.sum(jnp.where(pick, src_row[0:1, :], 0.0), axis=1, keepdims=True)
        return src[...].astype(F32) + coefficient * unit

    class Side:
        def __init__(self, first, come, sends, recvs, send_rows, recv_rows, target):
            self.blocks, self.sends, self.recvs = (0, first, first + 2, first + 4), sends, recvs
            self.send_rows, self.recv_rows = send_rows, recv_rows
            self.rows = ((64 - come, 128 - come), (come, come + 64))
            self.copies = [
                (
                    net.plan(sends.at[i], recvs.at[i], target),
                    net.plan(send_rows.at[i], recv_rows.at[i], target),
                )
                for i in range(7)
            ]

        def take(self, i, unit):
            arrive(self.copies[i])
            return unpack(self.recvs.at[i], self.recv_rows.at[i], unit)

        def give(self, hop, late):
            i = 2 * hop - 1 + late
            base = self.blocks[hop] * PAIRS
            start, stop = self.rows[late]
            unit = images[base + start:base + stop, :].astype(F32)
            full = LOGIT_SCALE * acc[base + start:base + stop, :]
            if hop > 1 or (hop == 1 and late):
                full = full + self.take(i - 2, unit)
            pack(self.sends.at[i], self.send_rows.at[i], full, unit)
            for copy in self.copies[i]:
                copy.start()

    sides = (
        Side(2, 0, send_up, recv_up, send_up_row, recv_up_row, z_up),
        Side(3, 64, send_down, recv_down, send_down_row, recv_down_row, z_down),
    )

    def give(hop, late):
        for side in sides:
            side.give(hop, late)

    buffers = (weigh0, weigh1)

    def grid_step(rows, count, events):
        def weigh(n):
            cosine = lax.dot_general(
                images[rows, :], texts[n * CHUNK:(n + 1) * CHUNK, :],
                (((1,), (1,)), ((), ())), preferred_element_type=F32,
            )
            pair = 0.5 + 0.5 * jnp.tanh(0.5 * LOGIT_SCALE * cosine + 0.5 * LOGIT_BIAS)
            buffers[n % 2][0:count, :] = pair.astype(BF16)

        def fold(n):
            acc[rows, :] += jnp.dot(
                buffers[n % 2][0:count, :], texts[n * CHUNK:(n + 1) * CHUNK, :],
                preferred_element_type=F32,
            )

        for n in range(TEXTS // CHUNK):
            events(n)
            weigh(n)
            if n > 0:
                fold(n - 1)
        fold(TEXTS // CHUNK - 1)

    def open_events(n):
        if n == 0:
            feats_open()
            state_out.start()
        if n == 2:
            arrive(text_crossings)

    schedule = {
        (2, 0): [lambda: give(1, 0), lambda: give(1, 1)],
        (2, 1): [feats_on],
        (3, 0): [lambda: give(2, 0)],
        (3, 2): [lambda: give(2, 1), feats_over],
    }

    def pair_step(step, carry):
        def events(n):
            for (at, part), todo in schedule.items():
                if part == n:

                    @pl.when(step == at)
                    def _(todo=todo):
                        for event in todo:
                            event()

        grid_step(pl.ds(pl.multiple_of(step * IMAGES, IMAGES), IMAGES), IMAGES, events)
        return carry

    grid_step(slice(PAIRS, 2 * PAIRS), PAIRS, open_events)
    turn(3, 0)
    grid_step(slice(0, PAIRS), PAIRS, lambda n: None)
    give(0, 1)
    lax.fori_loop(1, 4, pair_step, 0)
    give(3, 0)
    give(3, 1)
    unit = images[PAIRS:2 * PAIRS, :].astype(F32)
    text = texts[0:PAIRS, :].astype(F32)
    cosine = jnp.sum(unit * text, axis=1, keepdims=True)
    sigmoid = 0.5 + 0.5 * jnp.tanh(0.5 * LOGIT_SCALE * cosine + 0.5 * LOGIT_BIAS)
    change = (sigmoid - 1.0).astype(BF16).astype(F32) - sigmoid.astype(BF16).astype(F32)
    own_grad[...] = LOGIT_SCALE * (acc[PAIRS:2 * PAIRS, :] + change * text)

    state_out.wait()
    state_tile[...] = jnp.zeros_like(state_tile)
    for piece in range(8):
        first = 11 * (piece // 2) + 5 * (piece % 2)
        for a in range(3):
            state_tile[a, first:first + 6, :] += state_recv[piece, a, 0:6, :]

    def rows(index):
        return pl.ds(pl.multiple_of(index * PADDED, 16), PADDED)

    start_all[rows(z), :] = state_tile[2]
    start_moves = [net.push(start_all.at[rows(z), :], start_all.at[rows(z), :], target) for target in at_z]

    raw = raw_ref[...]
    unit = images[PAIRS:2 * PAIRS, :].astype(F32)
    for late in range(2):
        for side in sides:
            start, stop = side.rows[late]
            own_grad[start:stop, :] += side.take(5 + late, unit[start:stop])
    unit_grad = own_grad[...]
    inner = jnp.sum(raw * unit_grad, axis=1, keepdims=True)
    embed_grad = inverse * unit_grad - inverse * inverse * inverse * raw * inner
    grad_gram = lax.dot_general(
        embed_grad, embed_grad, (((1,), (1,)), ((), ())),
        precision=lax.Precision.HIGHEST, preferred_element_type=F32,
    )
    terms = jnp.sum(feat_gram * grad_gram, axis=0, keepdims=True)
    user_sq = jnp.sum(jnp.where(same_user, terms, 0.0), axis=1, keepdims=True)
    factor = bound / jnp.maximum(jnp.sqrt(user_sq), bound)
    clipped[...] = (factor * embed_grad).astype(BF16)

    def rows_of(core, ry):
        return clipped_all.at[(core * 4 + ry) * PAIRS:(core * 4 + ry + 1) * PAIRS, :]

    parts = []
    for o in range(1, Y):
        parts.append(net.push(clipped.at[:, lanes(c * 4 + shift(y, o, Y))], rows_of(0, 4 - o), at_y[o - 1]))
        parts.append(net.push(clipped.at[:, lanes(other * 4 + shift(y, o, Y))], rows_of(1, 4 - o), at_y_across[o - 1]))
    parts.append(net.push(clipped.at[:, lanes(other * 4 + y)], rows_of(1, 0), across))
    clipped_all[0:PAIRS, :] = clipped[:, lanes(k)]
    feats_cross.wait_recv()
    for copy in parts:
        copy.wait_recv()

    x_moves = []
    for o in (1, 2, 3, 0):
        block = feats_all[pl.ds(pl.multiple_of(shift(x, o, X) * SHARE, 16), SHARE), :]
        part = jnp.dot(block, clipped_all[...], preferred_element_type=F32)
        for piece in range(Z):
            shares[o, piece, 0:BLOCK, :] = part[piece * BLOCK:(piece + 1) * BLOCK]
        shares_send[o] = shares[o].astype(BF16)
        if o:
            x_moves.append(net.push(shares_send.at[o, :, 0:32, :], x_recv.at[o - 1], at_x[o - 1]))
    z_moves = [
        net.push(shares_send.at[:, shift(z, o, Z), 32:PADDED, :], z_recv.at[o - 1], at_z[o - 1])
        for o in range(1, Z)
    ]
    total = shares[0, :, 0:32, :]
    for o in range(1, X):
        x_moves[o - 1].wait_recv()
        total = total + x_recv[o - 1].astype(F32)
    x_part[...] = total
    x_send[...] = total.astype(BF16)
    x_moves = [
        net.push(x_send.at[shift(z, o, Z)], x_recv_last.at[o - 1], at_z[o - 1]) for o in range(1, Z)
    ]
    total = shares[:, z, 32:PADDED, :]
    for o in range(1, Z):
        z_moves[o - 1].wait_recv()
        total = total + z_recv[o - 1].astype(F32)
    z_send[...] = total.astype(BF16)
    z_moves = [net.push(z_send.at[o], z_recv_last.at[o - 1], at_x[o - 1]) for o in range(1, X)]
    upper, lower = x_part[z], total[0]
    for o in range(1, X):
        z_moves[o - 1].wait_recv()
        lower = lower + z_recv_last[o - 1].astype(F32)
    for o in range(1, Z):
        x_moves[o - 1].wait_recv()
        upper = upper + x_recv_last[o - 1].astype(F32)
    grad = jnp.concatenate([upper, lower], axis=0)

    new_sum = state_tile[0] + grad
    update_all[rows(z), :] = new_sum + state_tile[1]
    moves = [net.push(update_all.at[rows(z), :], update_all.at[rows(z), :], target) for target in at_z]
    for piece in range(8):
        first = 11 * (piece // 2) + 5 * (piece % 2)
        sums_send[piece] = new_sum[first:first + 8]
    arrive(start_moves)
    arrive(moves)

    update = update_all[...]
    square = jnp.sum((update * update).reshape(WIDE // 8, 8, 128), axis=0)
    at = 0
    for stage, targets in enumerate((at_x, at_y + [across] + at_y_across)):
        sq_send[stage] = square
        moves = [
            net.push(sq_send.at[stage], sq_recv.at[at + i], target)
            for i, target in enumerate(targets)
        ]
        for i, copy in enumerate(moves):
            copy.wait_recv()
            square = square + sq_recv[at + i]
        at += len(targets)
    norm = jnp.sqrt(jnp.sum(square, keepdims=True))
    cap = math.sqrt(W * E)
    shrink = cap / jnp.maximum(norm, cap)

    whole = start_all[...] - RATE * shrink * update
    whole = jnp.concatenate([whole[piece * PADDED:piece * PADDED + BLOCK] for piece in range(Z)], axis=0)
    weights_ref[x, :, lanes(k)] = whole.astype(BF16)

    half = SHARE // 2

    def low_piece(index, rows=(0, half)):
        return weights_ref.at[index, rows[0]:rows[1], lanes(c, 512)]

    def high_piece(away, shares=slice(0, X)):
        return weights_ref.at[shares, half:SHARE, lanes(c * 4 + shift(y, away, Y))]

    def send(piece, target):
        return net.push(piece, piece, target)

    moves_y = [send(weights_ref.at[x, 0:half, lanes(k)], target) for target in at_y]
    moves_x = [send(weights_ref.at[x, half:SHARE, lanes(k)], target) for target in at_x]
    sums_out = Scatter(
        net, sums_send, sums_ref,
        [device(x, 2 * zl + i // 4, zh2 + (i // 2) % 2, i % 2) for i in range(8)],
        [jnp.logical_and(half_y == zl, owner_slot == i) for i in range(8)],
        k,
    )
    sums_out.start()
    arrive(moves_y)
    low_moves = [send(low_piece(x), target) for target in (x_up, x_down)]
    arrive(moves_x)
    high_moves = [send(high_piece(0), target) for target in (y_up, y_down)]
    given = [send(low_piece(x), across), send(high_piece(0), across)]
    far = []
    for copy, away, rows_sent, target in (
        (low_moves[0], 3, (0, 96), x_up), (low_moves[1], 1, (96, half), x_down)
    ):
        copy.wait_recv()
        index = shift(x, away, X)
        far.append(send(low_piece(index, rows_sent), target))
        given.append(send(low_piece(index), across))
    for copy, away, shares, target in (
        (high_moves[0], 3, slice(0, 2), y_up), (high_moves[1], 1, slice(2, 4), y_down)
    ):
        copy.wait_recv()
        far.append(send(high_piece(away, shares), target))
        given.append(send(high_piece(away), across))
    arrive(far)
    given += [send(low_piece(shift(x, 2, X)), across), send(high_piece(2), across)]
    arrive(given)
    sums_out.wait()
    state_out.wait_sent()
    sums_out.wait_sent()
    net.finish()


def body(
    image_feats, text_emb, projection, clip_norms, user_ids, grad_sum, init_weights, tree_noise
):
    c = lax.rem(lax.axis_index("col"), 2)
    state = jnp.pad(jnp.stack([grad_sum, tree_noise, init_weights]), ((0, 0), (4, 4), (0, 0)))
    state = lax.dynamic_slice(state, (0, 4 - 4 * c, 0), (3, 48, 128))
    state = state.reshape(3, 6, 8, 128).transpose(2, 0, 1, 3)
    users = jnp.stack([user_ids.astype(F32), jnp.pad(clip_norms, (0, PAIRS - USERS))])
    users = jnp.pad(users[None, None], ((0, 7), (0, 2), (0, 0), (0, 0)))
    state = jnp.concatenate([state, users], axis=2)
    vmem = pl.BlockSpec(memory_space=pltpu.VMEM)
    weights, sums = pl.pallas_call(
        kernel,
        out_shape=(
            jax.ShapeDtypeStruct((X, SHARE, E), BF16),
            jax.ShapeDtypeStruct((8, 8, 128), F32),
        ),
        in_specs=[pl.BlockSpec(memory_space=pltpu.HBM)] * 4,
        out_specs=(vmem, vmem),
        scratch_shapes=[
            pltpu.VMEM((PAIRS, W), BF16),
            pltpu.VMEM((PAIRS, E), BF16),
            pltpu.VMEM((8, 3, 8, 128), F32),
            pltpu.VMEM((W, E), BF16),
            pltpu.VMEM((TEXTS, E), BF16),
            pltpu.VMEM((Z * PAIRS, E), BF16),
            pltpu.VMEM((PAIRS, E), F32),
            pltpu.VMEM((Z * PAIRS, E), F32),
            pltpu.VMEM((PAIRS, E), F32),
            pltpu.VMEM((IMAGES, CHUNK), BF16),
            pltpu.VMEM((IMAGES, CHUNK), BF16),
            pltpu.VMEM((7, HALF, E), BF16),
            pltpu.VMEM((7, HALF, E), BF16),
            pltpu.VMEM((7, HALF, E), BF16),
            pltpu.VMEM((7, HALF, E), BF16),
            pltpu.VMEM((7, 8, 128), F32),
            pltpu.VMEM((7, 8, 128), F32),
            pltpu.VMEM((7, 8, 128), F32),
            pltpu.VMEM((7, 8, 128), F32),
            pltpu.VMEM((W, 8 * PAIRS), BF16),
            pltpu.VMEM((PAIRS, E), BF16),
            pltpu.VMEM((8 * PAIRS, 128), BF16),
            pltpu.VMEM((X, Z, PADDED, 128), F32),
            pltpu.VMEM((X, Z, PADDED, 128), BF16),
            pltpu.VMEM((X - 1, Z, 32, 128), BF16),
            pltpu.VMEM((Z, 32, 128), F32),
            pltpu.VMEM((Z, 32, 128), BF16),
            pltpu.VMEM((Z - 1, 32, 128), BF16),
            pltpu.VMEM((Z - 1, X, 16, 128), BF16),
            pltpu.VMEM((X, 16, 128), BF16),
            pltpu.VMEM((X - 1, 16, 128), BF16),
            pltpu.VMEM((WIDE, 128), F32),
            pltpu.VMEM((WIDE, 128), F32),
            pltpu.VMEM((8, 3, 8, 128), F32),
            pltpu.VMEM((3, PADDED, 128), F32),
            pltpu.VMEM((8, 8, 128), F32),
            pltpu.VMEM((3, 8, 128), F32),
            pltpu.VMEM((17, 8, 128), F32),
            pltpu.SemaphoreType.DMA((4,)),
            pltpu.SemaphoreType.DMA((COPIES,)),
            pltpu.SemaphoreType.DMA((COPIES,)),
        ],
        compiler_params=pltpu.CompilerParams(
            collective_id=1, has_side_effects=True, vmem_limit_bytes=48 * 1024 * 1024
        ),
    )(
        image_feats, text_emb, projection, state,
    )
    sums = sums[:, :6].transpose(1, 0, 2).reshape(48, 128)
    return weights.reshape(W, E), lax.dynamic_slice(sums, (4 * c, 0), (44, 128))


def solution(mesh):
    in_specs = (
        P(("row", "col"), None),
        P(("row", "col"), None),
        P(),
        P(("row", "col")),
        P(("row", "col")),
        P(("row", "col"), None),
        P(("row", "col"), None),
        P(("row", "col"), None),
    )
    out_specs = (P(), P(("row", "col"), None))
    return jax.shard_map(body, mesh=mesh, in_specs=in_specs, out_specs=out_specs, check_vma=False)
```

```python
import math

import jax
import jax.numpy as jnp
from jax import lax
from jax.experimental import pallas as pl
from jax.experimental.pallas import tpu as pltpu
from jax.sharding import PartitionSpec as P

LOGIT_SCALE = 32.0
LOGIT_BIAS = -5.0
RATE = 0.5
EPSILON = 1e-06

MESH = pl.DeviceIdType.MESH
X, Y, Z = 4, 4, 8
W, E, PAIRS, USERS = 1408, 1024, 128, 16
SHARE = W // X
BLOCK = SHARE // Z
PADDED = 48
WIDE = Z * PADDED
TEXTS = 2 * X * Y * PAIRS
CHUNK = 1024
IMAGES = 2 * PAIRS
HALF = PAIRS // 2
COPIES = 256
F32, BF16 = jnp.float32, jnp.bfloat16


def place():
    row, col = lax.axis_index("row"), lax.axis_index("col")
    x, zh = lax.div(row, 4), lax.rem(row, 4)
    y, zl, c = lax.div(col, 4), lax.rem(lax.div(col, 2), 2), lax.rem(col, 2)
    return x, y, zh * 2 + zl, c


def device(x, y, z, c):
    return (x * 4 + lax.div(z, 2), y * 4 + lax.rem(z, 2) * 2 + c)


def shift(value, by, size):
    return lax.rem(value + by, size)


class Copies:
    def __init__(self, send_sems, recv_sems):
        self.send_sems, self.recv_sems, self.used, self.all = send_sems, recv_sems, 0, []

    def reserve(self, count):
        self.used += count
        return self.used - count

    def make(self, src, dst, target, send_at, recv_at):
        return pltpu.make_async_remote_copy(
            src_ref=src,
            dst_ref=dst,
            send_sem=self.send_sems.at[send_at],
            recv_sem=self.recv_sems.at[recv_at],
            device_id=target,
            device_id_type=MESH,
        )

    def plan(self, src, dst, target):
        at = self.reserve(1)
        copy = self.make(src, dst, target, at, at)
        self.all.append(copy)
        return copy

    def push(self, src, dst, target):
        copy = self.plan(src, dst, target)
        copy.start()
        return copy

    def finish(self):
        for copy in self.all:
            copy.wait_send()


class Scatter:
    def __init__(self, net, src, dst, targets, is_self, mine):
        self.net, self.src, self.dst, self.targets, self.is_self, self.mine = net, src, dst, targets, is_self, mine
        self.at = net.reserve(8)

    def remote(self, i):
        return self.net.make(
            self.src.at[i], self.dst.at[self.mine], self.targets[i], self.at + i, self.at + self.mine
        )

    def local(self, i):
        sem = self.net.recv_sems.at[self.at + self.mine]
        return pltpu.make_async_copy(self.src.at[i], self.dst.at[self.mine], sem)

    def start(self):
        for i in range(8):
            pl.when(jnp.logical_not(self.is_self[i]))(self.remote(i).start)
            pl.when(self.is_self[i])(self.local(i).start)

    def wait(self):
        for i in range(8):
            self.net.make(self.src.at[i], self.dst.at[i], self.targets[i], self.at + i, self.at + i).wait_recv()

    def wait_sent(self):
        for i in range(8):
            pl.when(jnp.logical_not(self.is_self[i]))(self.remote(i).wait_send)


def kernel(
    feats_hbm, text_hbm, proj_hbm, state_hbm,
    weights_ref, sums_ref,
    feats_ref, text_ref, state_ref, proj, texts, images, raw_ref, acc, own_grad, weigh0, weigh1,
    send_up, send_down, recv_up, recv_down, send_up_row, send_down_row, recv_up_row, recv_down_row,
    feats_all, clipped, clipped_all, shares, shares_send, x_recv, x_part, x_send, x_recv_last,
    z_recv, z_send, z_recv_last, start_all, update_all,
    state_recv, state_tile, sums_send, sq_send, sq_recv,
    load_sems, send_sems, recv_sems,
):
    x, y, z, c = place()
    col = lax.axis_index("col")
    k = c * 4 + y
    other = 1 - c
    zl = lax.rem(z, 2)
    at_x = [device(shift(x, o, X), y, z, c) for o in range(1, X)]
    at_y = [device(x, shift(y, o, Y), z, c) for o in range(1, Y)]
    at_z = [device(x, y, shift(z, o, Z), c) for o in range(1, Z)]
    across = device(x, y, z, other)
    at_y_across = [device(x, shift(y, o, Y), z, other) for o in range(1, Y)]
    flip = z + 1 - 2 * zl
    at_flip = [device(x, shift(y, o, Y), flip, cc) for o in range(Y) for cc in (c, other)][1:]
    x_up, x_down, y_up, y_down, z_up, z_down = at_x[0], at_x[2], at_y[0], at_y[2], at_z[0], at_z[6]

    loads = [
        pltpu.make_async_copy(src, dst, load_sems.at[i])
        for i, (src, dst) in enumerate((
            (feats_hbm, feats_ref), (proj_hbm, proj), (text_hbm, text_ref),
            (state_hbm, state_ref),
        ))
    ]
    for load in loads:
        load.start()
    barrier = pltpu.get_barrier_semaphore()
    partners = at_x + at_y + at_z + [across] + at_y_across + at_flip
    for target in partners:
        pl.semaphore_signal(barrier, inc=1, device_id=target, device_id_type=MESH)
    pl.semaphore_wait(barrier, len(partners))
    net = Copies(send_sems, recv_sems)

    def lanes(index, width=128):
        return pl.ds(pl.multiple_of(index * width, width), width)

    for load in loads[:2]:
        load.wait()
    raw = jnp.dot(feats_ref[...], proj[...], preferred_element_type=F32)
    raw_ref[...] = raw
    inverse = lax.rsqrt(jnp.sum(raw * raw, axis=1, keepdims=True) + EPSILON)
    images[PAIRS:2 * PAIRS, :] = (raw * inverse).astype(BF16)

    def image_hop(source, target_slot, half, target):
        def rows_at(index):
            return images.at[index * PAIRS + half * HALF:index * PAIRS + (half + 1) * HALF, :]

        return net.plan(rows_at(source), rows_at(target_slot), target)

    up = [[image_hop(a, b, half, z_up) for half in (0, 1)] for a, b in ((1, 7), (7, 5), (5, 3))]
    down = [[image_hop(a, b, half, z_down) for half in (1, 0)] for a, b in ((1, 6), (6, 4), (4, 2))]
    up.append([image_hop(3, 0, 0, z_up)])
    down.append([image_hop(2, 0, 1, z_down)])
    for part in range(2):
        up[0][part].start()
        down[0][part].start()

    def turn(step, part):
        for ring in (up, down):
            ring[step][part].wait_recv()
            if part < len(ring[min(step + 1, 3)]) and step < 3:
                ring[step + 1][part].start()

    for load in loads[2:]:
        load.wait()
    text = text_ref[...].astype(F32)
    texts[0:PAIRS, :] = (
        text * lax.rsqrt(jnp.sum(text * text, axis=1, keepdims=True) + EPSILON)
    ).astype(BF16)

    def slot(rx, ry, rows, core=0):
        base = (core * 16 + rx * 4 + ry) * PAIRS
        return texts.at[base + rows[0]:base + rows[1], :]

    def hop(axis, up, rx, ry, rows):
        step = 3 if up else 1
        if axis == "x":
            return net.plan(slot(rx, ry, rows), slot((rx + step) % 4, ry, rows), x_up if up else x_down)
        return net.plan(slot(rx, ry, rows), slot(rx, (ry + step) % 4, rows), y_up if up else y_down)

    text_crossings = []

    def cross(rx, ry, rows):
        text_crossings.append(net.push(slot(rx, ry, rows), slot(rx, ry, rows, 1), across))

    class Half:
        def __init__(self, first, second, low):
            self.rows, self.swap = (low, low + 64), first == "y"
            self.parts = ((low, low + 32), (low + 32, low + 64))
            r, p = self.rows, self.parts
            self.first = [hop(first, up, 0, 0, r) for up in (True, False)]
            self.relay = [hop(first, up, *self.at(3 if up else 1, 0), p[0 if up else 1]) for up in (True, False)]
            self.second = [[hop(second, up, *self.at(a, 0), r) for up in (True, False)] for a in range(4)]
            self.last = [
                [hop(second, up, *self.at(a, 3 if up else 1), p[0 if up else 1]) for up in (True, False)]
                for a in range(4)
            ]

        def at(self, a, b):
            return (b, a) if self.swap else (a, b)

        def open(self, a):
            for copy in self.second[a]:
                copy.start()

        def got_first(self, i):
            a = (3, 1)[i]
            self.first[i].wait_recv()
            self.relay[i].start()
            self.open(a)
            cross(*self.at(a, 0), self.rows)

        def got_relay(self):
            for copy in self.relay:
                copy.wait_recv()
            self.open(2)
            cross(*self.at(2, 0), self.rows)

        def got_second(self, a):
            for i in range(2):
                self.second[a][i].wait_recv()
                self.last[a][i].start()
                cross(*self.at(a, (3, 1)[i]), self.rows)

        def got_last(self, a):
            for copy in self.last[a]:
                copy.wait_recv()
            cross(*self.at(a, 2), self.rows)

    def arrive(copies):
        for copy in copies:
            copy.wait_recv()

    low, high = Half("x", "y", 0), Half("y", "x", 64)
    halves = (low, high)
    for half in halves:
        for copy in half.first:
            copy.start()
    for half in halves:
        half.open(0)
    cross(0, 0, (0, PAIRS))

    feats_all[:, 0:PAIRS] = feats_ref[...].T
    acc[...] = jnp.zeros_like(acc)
    shares[...] = jnp.zeros_like(shares)
    feat_gram = lax.dot_general(
        feats_ref[...], feats_ref[...], (((1,), (1,)), ((), ())), preferred_element_type=F32
    )
    local_row = state_ref[0, 0, 6:7, :] - ((lax.axis_index("row") * 16 + col) * USERS).astype(F32)
    square_shape = (PAIRS, PAIRS)
    diagonal = lax.broadcasted_iota(jnp.int32, square_shape, 0) == lax.broadcasted_iota(
        jnp.int32, square_shape, 1
    )
    local_column = jnp.sum(jnp.where(diagonal, local_row, 0.0), axis=1, keepdims=True)
    same_user = local_column == local_row
    users = lax.broadcasted_iota(jnp.int32, (PAIRS, USERS), 1).astype(F32)
    bound = jnp.sum(jnp.where(local_column == users, state_ref[0, 0, 7:8, 0:USERS], 0.0), axis=1, keepdims=True)
    feat_gram = jnp.where(same_user, feat_gram, 0.0)

    owner_slot = (lax.rem(y, 2) * 2 + zl) * 2 + c
    zh2 = z - zl
    half_y = lax.div(y, 2)
    state_out = Scatter(
        net, state_ref, state_recv,
        [device(x, i % 4, zh2 + half_y, i // 4) for i in range(8)],
        [jnp.logical_and(zl == half_y, k == i) for i in range(8)],
        owner_slot,
    )

    def both(event, at):
        for half in halves:
            event(half, at)

    both(Half.got_first, 0)
    turn(0, 0)
    both(Half.got_first, 1)
    turn(0, 1)
    both(Half.got_second, 0)
    for half in halves:
        half.got_relay()
    turn(1, 0)
    both(Half.got_last, 0)
    both(Half.got_second, 3)
    turn(1, 1)
    both(Half.got_second, 1)
    turn(2, 0)
    both(Half.got_second, 2)
    both(Half.got_last, 3)
    both(Half.got_last, 1)
    turn(2, 1)
    both(Half.got_last, 2)

    def feats_slot(ry, rows=(0, W)):
        return feats_all.at[rows[0]:rows[1], ry * PAIRS:(ry + 1) * PAIRS]

    feats_near = [net.plan(feats_slot(0), feats_slot(3), y_up), net.plan(feats_slot(0), feats_slot(1), y_down)]
    feats_far = [
        net.plan(feats_slot(3, (0, W // 2)), feats_slot(2, (0, W // 2)), y_up),
        net.plan(feats_slot(1, (W // 2, W)), feats_slot(2, (W // 2, W)), y_down),
    ]
    feats_cross = net.plan(feats_all.at[:, 0:512], feats_all.at[:, 512:1024], across)
    def feats_open():
        for copy in feats_near:
            copy.start()

    def feats_on():
        for near, far in zip(feats_near, feats_far):
            near.wait_recv()
            far.start()

    def feats_over():
        arrive(feats_far)
        feats_cross.start()

    pick = lax.broadcasted_iota(jnp.int32, (HALF, 128), 0) == lax.broadcasted_iota(
        jnp.int32, (HALF, 128), 1
    )

    def pack(dst, dst_row, full, unit):
        coefficient = jnp.sum(full * unit, axis=1, keepdims=True)
        dst[...] = (full - coefficient * unit).astype(BF16)
        row = jnp.sum(jnp.where(pick, coefficient, 0.0), axis=0, keepdims=True)
        dst_row[...] = jnp.broadcast_to(row, (8, 128))

    def unpack(src, src_row, unit):
        coefficient = jnp.sum(jnp.where(pick, src_row[0:1, :], 0.0), axis=1, keepdims=True)
        return src[...].astype(F32) + coefficient * unit

    class Side:
        def __init__(self, first, come, sends, recvs, send_rows, recv_rows, target):
            self.blocks, self.sends, self.recvs = (0, first, first + 2, first + 4), sends, recvs
            self.send_rows, self.recv_rows = send_rows, recv_rows
            self.rows = ((64 - come, 128 - come), (come, come + 64))
            self.copies = [
                (
                    net.plan(sends.at[i], recvs.at[i], target),
                    net.plan(send_rows.at[i], recv_rows.at[i], target),
                )
                for i in range(7)
            ]

        def take(self, i, unit):
            arrive(self.copies[i])
            return unpack(self.recvs.at[i], self.recv_rows.at[i], unit)

        def give(self, hop, late):
            i = 2 * hop - 1 + late
            base = self.blocks[hop] * PAIRS
            start, stop = self.rows[late]
            unit = images[base + start:base + stop, :].astype(F32)
            full = LOGIT_SCALE * acc[base + start:base + stop, :]
            if hop > 1 or (hop == 1 and late):
                full = full + self.take(i - 2, unit)
            pack(self.sends.at[i], self.send_rows.at[i], full, unit)
            for copy in self.copies[i]:
                copy.start()

    sides = (
        Side(2, 0, send_up, recv_up, send_up_row, recv_up_row, z_up),
        Side(3, 64, send_down, recv_down, send_down_row, recv_down_row, z_down),
    )

    def give(hop, late):
        for side in sides:
            side.give(hop, late)

    buffers = (weigh0, weigh1)

    def grid_step(rows, count, events):
        def weigh(n):
            cosine = lax.dot_general(
                images[rows, :], texts[n * CHUNK:(n + 1) * CHUNK, :],
                (((1,), (1,)), ((), ())), preferred_element_type=F32,
            )
            pair = 0.5 + 0.5 * jnp.tanh(0.5 * LOGIT_SCALE * cosine + 0.5 * LOGIT_BIAS)
            buffers[n % 2][0:count, :] = pair.astype(BF16)

        def fold(n):
            acc[rows, :] += jnp.dot(
                buffers[n % 2][0:count, :], texts[n * CHUNK:(n + 1) * CHUNK, :],
                preferred_element_type=F32,
            )

        for n in range(TEXTS // CHUNK):
            events(n)
            weigh(n)
            if n > 0:
                fold(n - 1)
        fold(TEXTS // CHUNK - 1)

    def open_events(n):
        if n == 0:
            feats_open()
            state_out.start()
        if n == 2:
            arrive(text_crossings)

    schedule = {
        (2, 0): [lambda: give(1, 0), lambda: give(1, 1)],
        (2, 1): [feats_on],
        (3, 0): [lambda: give(2, 0)],
        (3, 2): [lambda: give(2, 1), feats_over],
    }

    def pair_step(step, carry):
        def events(n):
            for (at, part), todo in schedule.items():
                if part == n:

                    @pl.when(step == at)
                    def _(todo=todo):
                        for event in todo:
                            event()

        grid_step(pl.ds(pl.multiple_of(step * IMAGES, IMAGES), IMAGES), IMAGES, events)
        return carry

    turn(3, 0)
    grid_step(slice(0, IMAGES), IMAGES, open_events)
    give(0, 1)
    lax.fori_loop(1, 4, pair_step, 0)
    give(3, 0)
    give(3, 1)
    unit = images[PAIRS:2 * PAIRS, :].astype(F32)
    text = texts[0:PAIRS, :].astype(F32)
    cosine = jnp.sum(unit * text, axis=1, keepdims=True)
    sigmoid = 0.5 + 0.5 * jnp.tanh(0.5 * LOGIT_SCALE * cosine + 0.5 * LOGIT_BIAS)
    change = (sigmoid - 1.0).astype(BF16).astype(F32) - sigmoid.astype(BF16).astype(F32)
    own_grad[...] = LOGIT_SCALE * (acc[PAIRS:2 * PAIRS, :] + change * text)

    state_out.wait()
    state_tile[...] = jnp.zeros_like(state_tile)
    for piece in range(8):
        first = 11 * (piece // 2) + 5 * (piece % 2)
        for a in range(3):
            state_tile[a, first:first + 6, :] += state_recv[piece, a, 0:6, :]

    def rows(index):
        return pl.ds(pl.multiple_of(index * PADDED, 16), PADDED)

    start_all[rows(z), :] = state_tile[2]
    start_moves = [net.push(start_all.at[rows(z), :], start_all.at[rows(z), :], target) for target in at_z]

    raw = raw_ref[...]
    unit = images[PAIRS:2 * PAIRS, :].astype(F32)
    for late in range(2):
        for side in sides:
            start, stop = side.rows[late]
            own_grad[start:stop, :] += side.take(5 + late, unit[start:stop])
    unit_grad = own_grad[...]
    inner = jnp.sum(raw * unit_grad, axis=1, keepdims=True)
    embed_grad = inverse * unit_grad - inverse * inverse * inverse * raw * inner
    grad_gram = lax.dot_general(
        embed_grad, embed_grad, (((1,), (1,)), ((), ())),
        precision=lax.Precision.HIGHEST, preferred_element_type=F32,
    )
    terms = jnp.sum(feat_gram * grad_gram, axis=0, keepdims=True)
    user_sq = jnp.sum(jnp.where(same_user, terms, 0.0), axis=1, keepdims=True)
    factor = bound / jnp.maximum(jnp.sqrt(user_sq), bound)
    clipped[...] = (factor * embed_grad).astype(BF16)

    def rows_of(core, ry):
        return clipped_all.at[(core * 4 + ry) * PAIRS:(core * 4 + ry + 1) * PAIRS, :]

    parts = []
    for o in range(1, Y):
        parts.append(net.push(clipped.at[:, lanes(c * 4 + shift(y, o, Y))], rows_of(0, 4 - o), at_y[o - 1]))
        parts.append(net.push(clipped.at[:, lanes(other * 4 + shift(y, o, Y))], rows_of(1, 4 - o), at_y_across[o - 1]))
    parts.append(net.push(clipped.at[:, lanes(other * 4 + y)], rows_of(1, 0), across))
    clipped_all[0:PAIRS, :] = clipped[:, lanes(k)]
    feats_cross.wait_recv()
    for copy in parts:
        copy.wait_recv()

    x_moves = []
    for o in (1, 2, 3, 0):
        block = feats_all[pl.ds(pl.multiple_of(shift(x, o, X) * SHARE, 16), SHARE), :]
        part = jnp.dot(block, clipped_all[...], preferred_element_type=F32)
        for piece in range(Z):
            shares[o, piece, 0:BLOCK, :] = part[piece * BLOCK:(piece + 1) * BLOCK]
        shares_send[o] = shares[o].astype(BF16)
        if o:
            x_moves.append(net.push(shares_send.at[o, :, 0:32, :], x_recv.at[o - 1], at_x[o - 1]))
    z_moves = [
        net.push(shares_send.at[:, shift(z, o, Z), 32:PADDED, :], z_recv.at[o - 1], at_z[o - 1])
        for o in range(1, Z)
    ]
    total = shares[0, :, 0:32, :]
    for o in range(1, X):
        x_moves[o - 1].wait_recv()
        total = total + x_recv[o - 1].astype(F32)
    x_part[...] = total
    x_send[...] = total.astype(BF16)
    x_moves = [
        net.push(x_send.at[shift(z, o, Z)], x_recv_last.at[o - 1], at_z[o - 1]) for o in range(1, Z)
    ]
    total = shares[:, z, 32:PADDED, :]
    for o in range(1, Z):
        z_moves[o - 1].wait_recv()
        total = total + z_recv[o - 1].astype(F32)
    z_send[...] = total.astype(BF16)
    z_moves = [net.push(z_send.at[o], z_recv_last.at[o - 1], at_x[o - 1]) for o in range(1, X)]
    upper, lower = x_part[z], total[0]
    for o in range(1, X):
        z_moves[o - 1].wait_recv()
        lower = lower + z_recv_last[o - 1].astype(F32)
    for o in range(1, Z):
        x_moves[o - 1].wait_recv()
        upper = upper + x_recv_last[o - 1].astype(F32)
    grad = jnp.concatenate([upper, lower], axis=0)

    new_sum = state_tile[0] + grad
    update_all[rows(z), :] = new_sum + state_tile[1]
    moves = [net.push(update_all.at[rows(z), :], update_all.at[rows(z), :], target) for target in at_z]
    for piece in range(8):
        first = 11 * (piece // 2) + 5 * (piece % 2)
        sums_send[piece] = new_sum[first:first + 8]
    arrive(start_moves)
    arrive(moves)

    update = update_all[...]
    square = jnp.sum((update * update).reshape(WIDE // 8, 8, 128), axis=0)
    at = 0
    for stage, targets in enumerate((at_x, at_y + [across] + at_y_across)):
        sq_send[stage] = square
        moves = [
            net.push(sq_send.at[stage], sq_recv.at[at + i], target)
            for i, target in enumerate(targets)
        ]
        for i, copy in enumerate(moves):
            copy.wait_recv()
            square = square + sq_recv[at + i]
        at += len(targets)
    norm = jnp.sqrt(jnp.sum(square, keepdims=True))
    cap = math.sqrt(W * E)
    shrink = cap / jnp.maximum(norm, cap)

    whole = start_all[...] - RATE * shrink * update
    whole = jnp.concatenate([whole[piece * PADDED:piece * PADDED + BLOCK] for piece in range(Z)], axis=0)
    weights_ref[x, :, lanes(k)] = whole.astype(BF16)

    half = SHARE // 2

    def low_piece(index, rows=(0, half)):
        return weights_ref.at[index, rows[0]:rows[1], lanes(c, 512)]

    def high_piece(away, shares=slice(0, X)):
        return weights_ref.at[shares, half:SHARE, lanes(c * 4 + shift(y, away, Y))]

    def send(piece, target):
        return net.push(piece, piece, target)

    moves_y = [send(weights_ref.at[x, 0:half, lanes(k)], target) for target in at_y]
    moves_x = [send(weights_ref.at[x, half:SHARE, lanes(k)], target) for target in at_x]
    sums_out = Scatter(
        net, sums_send, sums_ref,
        [device(x, 2 * zl + i // 4, zh2 + (i // 2) % 2, i % 2) for i in range(8)],
        [jnp.logical_and(half_y == zl, owner_slot == i) for i in range(8)],
        k,
    )
    sums_out.start()
    arrive(moves_y)
    low_moves = [send(low_piece(x), target) for target in (x_up, x_down)]
    arrive(moves_x)
    high_moves = [send(high_piece(0), target) for target in (y_up, y_down)]
    given = [send(low_piece(x), across), send(high_piece(0), across)]
    far = []
    for copy, away, rows_sent, target in (
        (low_moves[0], 3, (0, 96), x_up), (low_moves[1], 1, (96, half), x_down)
    ):
        copy.wait_recv()
        index = shift(x, away, X)
        far.append(send(low_piece(index, rows_sent), target))
        given.append(send(low_piece(index), across))
    for copy, away, shares, target in (
        (high_moves[0], 3, slice(0, 2), y_up), (high_moves[1], 1, slice(2, 4), y_down)
    ):
        copy.wait_recv()
        far.append(send(high_piece(away, shares), target))
        given.append(send(high_piece(away), across))
    arrive(far)
    given += [send(low_piece(shift(x, 2, X)), across), send(high_piece(2), across)]
    arrive(given)
    sums_out.wait()
    state_out.wait_sent()
    sums_out.wait_sent()
    net.finish()


def body(
    image_feats, text_emb, projection, clip_norms, user_ids, grad_sum, init_weights, tree_noise
):
    c = lax.rem(lax.axis_index("col"), 2)
    state = jnp.pad(jnp.stack([grad_sum, tree_noise, init_weights]), ((0, 0), (4, 4), (0, 0)))
    state = lax.dynamic_slice(state, (0, 4 - 4 * c, 0), (3, 48, 128))
    state = state.reshape(3, 6, 8, 128).transpose(2, 0, 1, 3)
    users = jnp.stack([user_ids.astype(F32), jnp.pad(clip_norms, (0, PAIRS - USERS))])
    users = jnp.pad(users[None, None], ((0, 7), (0, 2), (0, 0), (0, 0)))
    state = jnp.concatenate([state, users], axis=2)
    vmem = pl.BlockSpec(memory_space=pltpu.VMEM)
    weights, sums = pl.pallas_call(
        kernel,
        out_shape=(
            jax.ShapeDtypeStruct((X, SHARE, E), BF16),
            jax.ShapeDtypeStruct((8, 8, 128), F32),
        ),
        in_specs=[pl.BlockSpec(memory_space=pltpu.HBM)] * 4,
        out_specs=(vmem, vmem),
        scratch_shapes=[
            pltpu.VMEM((PAIRS, W), BF16),
            pltpu.VMEM((PAIRS, E), BF16),
            pltpu.VMEM((8, 3, 8, 128), F32),
            pltpu.VMEM((W, E), BF16),
            pltpu.VMEM((TEXTS, E), BF16),
            pltpu.VMEM((Z * PAIRS, E), BF16),
            pltpu.VMEM((PAIRS, E), F32),
            pltpu.VMEM((Z * PAIRS, E), F32),
            pltpu.VMEM((PAIRS, E), F32),
            pltpu.VMEM((IMAGES, CHUNK), BF16),
            pltpu.VMEM((IMAGES, CHUNK), BF16),
            pltpu.VMEM((7, HALF, E), BF16),
            pltpu.VMEM((7, HALF, E), BF16),
            pltpu.VMEM((7, HALF, E), BF16),
            pltpu.VMEM((7, HALF, E), BF16),
            pltpu.VMEM((7, 8, 128), F32),
            pltpu.VMEM((7, 8, 128), F32),
            pltpu.VMEM((7, 8, 128), F32),
            pltpu.VMEM((7, 8, 128), F32),
            pltpu.VMEM((W, 8 * PAIRS), BF16),
            pltpu.VMEM((PAIRS, E), BF16),
            pltpu.VMEM((8 * PAIRS, 128), BF16),
            pltpu.VMEM((X, Z, PADDED, 128), F32),
            pltpu.VMEM((X, Z, PADDED, 128), BF16),
            pltpu.VMEM((X - 1, Z, 32, 128), BF16),
            pltpu.VMEM((Z, 32, 128), F32),
            pltpu.VMEM((Z, 32, 128), BF16),
            pltpu.VMEM((Z - 1, 32, 128), BF16),
            pltpu.VMEM((Z - 1, X, 16, 128), BF16),
            pltpu.VMEM((X, 16, 128), BF16),
            pltpu.VMEM((X - 1, 16, 128), BF16),
            pltpu.VMEM((WIDE, 128), F32),
            pltpu.VMEM((WIDE, 128), F32),
            pltpu.VMEM((8, 3, 8, 128), F32),
            pltpu.VMEM((3, PADDED, 128), F32),
            pltpu.VMEM((8, 8, 128), F32),
            pltpu.VMEM((3, 8, 128), F32),
            pltpu.VMEM((17, 8, 128), F32),
            pltpu.SemaphoreType.DMA((4,)),
            pltpu.SemaphoreType.DMA((COPIES,)),
            pltpu.SemaphoreType.DMA((COPIES,)),
        ],
        compiler_params=pltpu.CompilerParams(
            collective_id=1, has_side_effects=True, vmem_limit_bytes=48 * 1024 * 1024
        ),
    )(
        image_feats, text_emb, projection, state,
    )
    sums = sums[:, :6].transpose(1, 0, 2).reshape(48, 128)
    return weights.reshape(W, E), lax.dynamic_slice(sums, (4 * c, 0), (44, 128))


def solution(mesh):
    in_specs = (
        P(("row", "col"), None),
        P(("row", "col"), None),
        P(),
        P(("row", "col")),
        P(("row", "col")),
        P(("row", "col"), None),
        P(("row", "col"), None),
        P(("row", "col"), None),
    )
    out_specs = (P(), P(("row", "col"), None))
    return jax.shard_map(body, mesh=mesh, in_specs=in_specs, out_specs=out_specs, check_vma=False)
```

```python
import math

import jax
import jax.numpy as jnp
from jax import lax
from jax.experimental import pallas as pl
from jax.experimental.pallas import tpu as pltpu
from jax.sharding import PartitionSpec as P

LOGIT_SCALE = 32.0
LOGIT_BIAS = -5.0
RATE = 0.5
EPSILON = 1e-06

MESH = pl.DeviceIdType.MESH
X, Y, Z = 4, 4, 8
W, E, PAIRS, USERS = 1408, 1024, 128, 16
SHARE = W // X
BLOCK = SHARE // Z
PADDED = 48
WIDE = Z * PADDED
TEXTS = 2 * X * Y * PAIRS
CHUNK = 1024
IMAGES = 2 * PAIRS
HALF = PAIRS // 2
COPIES = 256
F32, BF16 = jnp.float32, jnp.bfloat16


def place():
    row, col = lax.axis_index("row"), lax.axis_index("col")
    x, zh = lax.div(row, 4), lax.rem(row, 4)
    y, zl, c = lax.div(col, 4), lax.rem(lax.div(col, 2), 2), lax.rem(col, 2)
    return x, y, zh * 2 + zl, c


def device(x, y, z, c):
    return (x * 4 + lax.div(z, 2), y * 4 + lax.rem(z, 2) * 2 + c)


def shift(value, by, size):
    return lax.rem(value + by, size)


class Copies:
    def __init__(self, send_sems, recv_sems):
        self.send_sems, self.recv_sems, self.used, self.all = send_sems, recv_sems, 0, []

    def reserve(self, count):
        self.used += count
        return self.used - count

    def make(self, src, dst, target, send_at, recv_at):
        return pltpu.make_async_remote_copy(
            src_ref=src,
            dst_ref=dst,
            send_sem=self.send_sems.at[send_at],
            recv_sem=self.recv_sems.at[recv_at],
            device_id=target,
            device_id_type=MESH,
        )

    def plan(self, src, dst, target):
        at = self.reserve(1)
        copy = self.make(src, dst, target, at, at)
        self.all.append(copy)
        return copy

    def push(self, src, dst, target):
        copy = self.plan(src, dst, target)
        copy.start()
        return copy

    def finish(self):
        for copy in self.all:
            copy.wait_send()


class Scatter:
    def __init__(self, net, src, dst, targets, is_self, mine):
        self.net, self.src, self.dst, self.targets, self.is_self, self.mine = net, src, dst, targets, is_self, mine
        self.at = net.reserve(8)

    def remote(self, i):
        return self.net.make(
            self.src.at[i], self.dst.at[self.mine], self.targets[i], self.at + i, self.at + self.mine
        )

    def local(self, i):
        sem = self.net.recv_sems.at[self.at + self.mine]
        return pltpu.make_async_copy(self.src.at[i], self.dst.at[self.mine], sem)

    def start(self):
        for i in range(8):
            pl.when(jnp.logical_not(self.is_self[i]))(self.remote(i).start)
            pl.when(self.is_self[i])(self.local(i).start)

    def wait(self):
        for i in range(8):
            self.net.make(self.src.at[i], self.dst.at[i], self.targets[i], self.at + i, self.at + i).wait_recv()

    def wait_sent(self):
        for i in range(8):
            pl.when(jnp.logical_not(self.is_self[i]))(self.remote(i).wait_send)


def kernel(
    feats_hbm, text_hbm, proj_hbm, state_hbm,
    weights_ref, sums_ref,
    feats_ref, text_ref, state_ref, proj, texts, images, raw_ref, acc, own_grad, weigh0, weigh1,
    send_up, send_down, recv_up, recv_down, send_up_row, send_down_row, recv_up_row, recv_down_row,
    feats_all, clipped, clipped_all, shares, shares_send, x_recv, x_part, x_send, x_recv_last,
    z_recv, z_send, z_recv_last, start_all, update_all,
    state_recv, state_tile, sums_send, sq_send, sq_recv,
    load_sems, send_sems, recv_sems,
):
    x, y, z, c = place()
    col = lax.axis_index("col")
    k = c * 4 + y
    other = 1 - c
    zl = lax.rem(z, 2)
    at_x = [device(shift(x, o, X), y, z, c) for o in range(1, X)]
    at_y = [device(x, shift(y, o, Y), z, c) for o in range(1, Y)]
    at_z = [device(x, y, shift(z, o, Z), c) for o in range(1, Z)]
    across = device(x, y, z, other)
    at_y_across = [device(x, shift(y, o, Y), z, other) for o in range(1, Y)]
    flip = z + 1 - 2 * zl
    at_flip = [device(x, shift(y, o, Y), flip, cc) for o in range(Y) for cc in (c, other)][1:]
    x_up, x_down, y_up, y_down, z_up, z_down = at_x[0], at_x[2], at_y[0], at_y[2], at_z[0], at_z[6]

    loads = [
        pltpu.make_async_copy(src, dst, load_sems.at[i])
        for i, (src, dst) in enumerate((
            (feats_hbm, feats_ref), (proj_hbm, proj), (text_hbm, text_ref),
            (state_hbm, state_ref),
        ))
    ]
    for load in loads:
        load.start()
    barrier = pltpu.get_barrier_semaphore()
    partners = at_x + at_y + at_z + [across] + at_y_across + at_flip
    for target in partners:
        pl.semaphore_signal(barrier, inc=1, device_id=target, device_id_type=MESH)
    pl.semaphore_wait(barrier, len(partners))
    net = Copies(send_sems, recv_sems)

    def lanes(index, width=128):
        return pl.ds(pl.multiple_of(index * width, width), width)

    for load in loads[:2]:
        load.wait()
    raw = jnp.dot(feats_ref[...], proj[...], preferred_element_type=F32)
    raw_ref[...] = raw
    inverse = lax.rsqrt(jnp.sum(raw * raw, axis=1, keepdims=True) + EPSILON)
    images[PAIRS:2 * PAIRS, :] = (raw * inverse).astype(BF16)

    def image_hop(source, target_slot, half, target):
        def rows_at(index):
            return images.at[index * PAIRS + half * HALF:index * PAIRS + (half + 1) * HALF, :]

        return net.plan(rows_at(source), rows_at(target_slot), target)

    up = [[image_hop(a, b, half, z_up) for half in (0, 1)] for a, b in ((1, 7), (7, 5), (5, 3))]
    down = [[image_hop(a, b, half, z_down) for half in (1, 0)] for a, b in ((1, 6), (6, 4), (4, 2))]
    up.append([image_hop(3, 0, 0, z_up)])
    down.append([image_hop(2, 0, 1, z_down)])
    for part in range(2):
        up[0][part].start()
        down[0][part].start()

    def turn(step, part):
        for ring in (up, down):
            ring[step][part].wait_recv()
            if part < len(ring[min(step + 1, 3)]) and step < 3:
                ring[step + 1][part].start()

    for load in loads[2:]:
        load.wait()
    text = text_ref[...].astype(F32)
    texts[0:PAIRS, :] = (
        text * lax.rsqrt(jnp.sum(text * text, axis=1, keepdims=True) + EPSILON)
    ).astype(BF16)

    def slot(rx, ry, rows, core=0):
        base = (core * 16 + rx * 4 + ry) * PAIRS
        return texts.at[base + rows[0]:base + rows[1], :]

    def hop(axis, up, rx, ry, rows):
        step = 3 if up else 1
        if axis == "x":
            return net.plan(slot(rx, ry, rows), slot((rx + step) % 4, ry, rows), x_up if up else x_down)
        return net.plan(slot(rx, ry, rows), slot(rx, (ry + step) % 4, rows), y_up if up else y_down)

    text_crossings = []

    def cross(rx, ry, rows):
        text_crossings.append(net.push(slot(rx, ry, rows), slot(rx, ry, rows, 1), across))

    class Half:
        def __init__(self, first, second, low):
            self.rows, self.swap = (low, low + 64), first == "y"
            self.parts = ((low, low + 32), (low + 32, low + 64))
            r, p = self.rows, self.parts
            self.first = [hop(first, up, 0, 0, r) for up in (True, False)]
            self.relay = [hop(first, up, *self.at(3 if up else 1, 0), p[0 if up else 1]) for up in (True, False)]
            self.second = [[hop(second, up, *self.at(a, 0), r) for up in (True, False)] for a in range(4)]
            self.last = [
                [hop(second, up, *self.at(a, 3 if up else 1), p[0 if up else 1]) for up in (True, False)]
                for a in range(4)
            ]

        def at(self, a, b):
            return (b, a) if self.swap else (a, b)

        def open(self, a):
            for copy in self.second[a]:
                copy.start()

        def got_first(self, i):
            a = (3, 1)[i]
            self.first[i].wait_recv()
            self.relay[i].start()
            self.open(a)
            cross(*self.at(a, 0), self.rows)

        def got_relay(self):
            for copy in self.relay:
                copy.wait_recv()
            self.open(2)
            cross(*self.at(2, 0), self.rows)

        def got_second(self, a):
            for i in range(2):
                self.second[a][i].wait_recv()
                self.last[a][i].start()
                cross(*self.at(a, (3, 1)[i]), self.rows)

        def got_last(self, a):
            for copy in self.last[a]:
                copy.wait_recv()
            cross(*self.at(a, 2), self.rows)

    def arrive(copies):
        for copy in copies:
            copy.wait_recv()

    low, high = Half("x", "y", 0), Half("y", "x", 64)
    halves = (low, high)
    for half in halves:
        for copy in half.first:
            copy.start()
    for half in halves:
        half.open(0)
    cross(0, 0, (0, PAIRS))

    feats_all[:, 0:PAIRS] = feats_ref[...].T
    acc[...] = jnp.zeros_like(acc)
    shares[...] = jnp.zeros_like(shares)
    feat_gram = lax.dot_general(
        feats_ref[...], feats_ref[...], (((1,), (1,)), ((), ())), preferred_element_type=F32
    )
    local_row = state_ref[0, 0, 6:7, :] - ((lax.axis_index("row") * 16 + col) * USERS).astype(F32)
    square_shape = (PAIRS, PAIRS)
    diagonal = lax.broadcasted_iota(jnp.int32, square_shape, 0) == lax.broadcasted_iota(
        jnp.int32, square_shape, 1
    )
    local_column = jnp.sum(jnp.where(diagonal, local_row, 0.0), axis=1, keepdims=True)
    same_user = local_column == local_row
    users = lax.broadcasted_iota(jnp.int32, (PAIRS, USERS), 1).astype(F32)
    bound = jnp.sum(jnp.where(local_column == users, state_ref[0, 0, 7:8, 0:USERS], 0.0), axis=1, keepdims=True)
    feat_gram = jnp.where(same_user, feat_gram, 0.0)

    owner_slot = (lax.rem(y, 2) * 2 + zl) * 2 + c
    zh2 = z - zl
    half_y = lax.div(y, 2)
    state_out = Scatter(
        net, state_ref, state_recv,
        [device(x, i % 4, zh2 + half_y, i // 4) for i in range(8)],
        [jnp.logical_and(zl == half_y, k == i) for i in range(8)],
        owner_slot,
    )

    def both(event, at):
        for half in halves:
            event(half, at)

    both(Half.got_first, 0)
    turn(0, 0)
    both(Half.got_first, 1)
    turn(0, 1)
    both(Half.got_second, 0)
    for half in halves:
        half.got_relay()
    turn(1, 0)
    both(Half.got_last, 0)
    both(Half.got_second, 3)
    turn(1, 1)
    both(Half.got_second, 1)
    turn(2, 0)
    both(Half.got_second, 2)
    both(Half.got_last, 3)
    both(Half.got_last, 1)
    turn(2, 1)
    both(Half.got_last, 2)

    def feats_slot(ry, rows=(0, W)):
        return feats_all.at[rows[0]:rows[1], ry * PAIRS:(ry + 1) * PAIRS]

    feats_near = [net.plan(feats_slot(0), feats_slot(3), y_up), net.plan(feats_slot(0), feats_slot(1), y_down)]
    feats_far = [
        net.plan(feats_slot(3, (0, W // 2)), feats_slot(2, (0, W // 2)), y_up),
        net.plan(feats_slot(1, (W // 2, W)), feats_slot(2, (W // 2, W)), y_down),
    ]
    feats_cross = net.plan(feats_all.at[:, 0:512], feats_all.at[:, 512:1024], across)
    def feats_open():
        for copy in feats_near:
            copy.start()

    def feats_on():
        for near, far in zip(feats_near, feats_far):
            near.wait_recv()
            far.start()

    def feats_over():
        arrive(feats_far)
        feats_cross.start()

    pick = lax.broadcasted_iota(jnp.int32, (HALF, 128), 0) == lax.broadcasted_iota(
        jnp.int32, (HALF, 128), 1
    )

    def pack(dst, dst_row, full, unit):
        coefficient = jnp.sum(full * unit, axis=1, keepdims=True)
        dst[...] = (full - coefficient * unit).astype(BF16)
        row = jnp.sum(jnp.where(pick, coefficient, 0.0), axis=0, keepdims=True)
        dst_row[...] = jnp.broadcast_to(row, (8, 128))

    def unpack(src, src_row, unit):
        coefficient = jnp.sum(jnp.where(pick, src_row[0:1, :], 0.0), axis=1, keepdims=True)
        return src[...].astype(F32) + coefficient * unit

    class Side:
        def __init__(self, first, come, sends, recvs, send_rows, recv_rows, target):
            self.blocks, self.sends, self.recvs = (0, first, first + 2, first + 4), sends, recvs
            self.send_rows, self.recv_rows = send_rows, recv_rows
            self.rows = ((64 - come, 128 - come), (come, come + 64))
            self.copies = [
                (
                    net.plan(sends.at[i], recvs.at[i], target),
                    net.plan(send_rows.at[i], recv_rows.at[i], target),
                )
                for i in range(7)
            ]

        def take(self, i, unit):
            arrive(self.copies[i])
            return unpack(self.recvs.at[i], self.recv_rows.at[i], unit)

        def give(self, hop, late):
            i = 2 * hop - 1 + late
            base = self.blocks[hop] * PAIRS
            start, stop = self.rows[late]
            unit = images[base + start:base + stop, :].astype(F32)
            full = LOGIT_SCALE * acc[base + start:base + stop, :]
            if hop > 1 or (hop == 1 and late):
                full = full + self.take(i - 2, unit)
            pack(self.sends.at[i], self.send_rows.at[i], full, unit)
            for copy in self.copies[i]:
                copy.start()

    sides = (
        Side(2, 0, send_up, recv_up, send_up_row, recv_up_row, z_up),
        Side(3, 64, send_down, recv_down, send_down_row, recv_down_row, z_down),
    )

    def give(hop, late):
        for side in sides:
            side.give(hop, late)

    buffers = (weigh0, weigh1)

    def grid_step(rows, count, events):
        def weigh(n):
            cosine = lax.dot_general(
                images[rows, :], texts[n * CHUNK:(n + 1) * CHUNK, :],
                (((1,), (1,)), ((), ())), preferred_element_type=F32,
            )
            pair = 0.5 + 0.5 * jnp.tanh(0.5 * LOGIT_SCALE * cosine + 0.5 * LOGIT_BIAS)
            buffers[n % 2][0:count, :] = pair.astype(BF16)

        def fold(n):
            acc[rows, :] += jnp.dot(
                buffers[n % 2][0:count, :], texts[n * CHUNK:(n + 1) * CHUNK, :],
                preferred_element_type=F32,
            )

        for n in range(TEXTS // CHUNK):
            events(n)
            weigh(n)
            if n > 0:
                fold(n - 1)
        fold(TEXTS // CHUNK - 1)

    def open_events(n):
        if n == 0:
            feats_open()
            state_out.start()
        if n == 2:
            arrive(text_crossings)

    def middle_events(n):
        if n == 2:
            feats_on()

    def last_events(n):
        if n == 2:
            give(2, 0)
            feats_over()
        if n == 3:
            give(2, 1)

    turn(3, 0)
    grid_step(slice(0, IMAGES), IMAGES, open_events)
    give(0, 1)
    grid_step(slice(IMAGES, 3 * IMAGES), 2 * IMAGES, middle_events)
    give(1, 0)
    give(1, 1)
    grid_step(slice(3 * IMAGES, 4 * IMAGES), IMAGES, last_events)
    give(3, 0)
    give(3, 1)
    unit = images[PAIRS:2 * PAIRS, :].astype(F32)
    text = texts[0:PAIRS, :].astype(F32)
    cosine = jnp.sum(unit * text, axis=1, keepdims=True)
    sigmoid = 0.5 + 0.5 * jnp.tanh(0.5 * LOGIT_SCALE * cosine + 0.5 * LOGIT_BIAS)
    change = (sigmoid - 1.0).astype(BF16).astype(F32) - sigmoid.astype(BF16).astype(F32)
    own_grad[...] = LOGIT_SCALE * (acc[PAIRS:2 * PAIRS, :] + change * text)

    state_out.wait()
    state_tile[...] = jnp.zeros_like(state_tile)
    for piece in range(8):
        first = 11 * (piece // 2) + 5 * (piece % 2)
        for a in range(3):
            state_tile[a, first:first + 6, :] += state_recv[piece, a, 0:6, :]

    def rows(index):
        return pl.ds(pl.multiple_of(index * PADDED, 16), PADDED)

    start_all[rows(z), :] = state_tile[2]
    start_moves = [net.push(start_all.at[rows(z), :], start_all.at[rows(z), :], target) for target in at_z]

    raw = raw_ref[...]
    unit = images[PAIRS:2 * PAIRS, :].astype(F32)
    for late in range(2):
        for side in sides:
            start, stop = side.rows[late]
            own_grad[start:stop, :] += side.take(5 + late, unit[start:stop])
    unit_grad = own_grad[...]
    inner = jnp.sum(raw * unit_grad, axis=1, keepdims=True)
    embed_grad = inverse * unit_grad - inverse * inverse * inverse * raw * inner
    grad_gram = lax.dot_general(
        embed_grad, embed_grad, (((1,), (1,)), ((), ())),
        precision=lax.Precision.HIGHEST, preferred_element_type=F32,
    )
    terms = jnp.sum(feat_gram * grad_gram, axis=0, keepdims=True)
    user_sq = jnp.sum(jnp.where(same_user, terms, 0.0), axis=1, keepdims=True)
    factor = bound / jnp.maximum(jnp.sqrt(user_sq), bound)
    clipped[...] = (factor * embed_grad).astype(BF16)

    def rows_of(core, ry):
        return clipped_all.at[(core * 4 + ry) * PAIRS:(core * 4 + ry + 1) * PAIRS, :]

    parts = []
    for o in range(1, Y):
        parts.append(net.push(clipped.at[:, lanes(c * 4 + shift(y, o, Y))], rows_of(0, 4 - o), at_y[o - 1]))
        parts.append(net.push(clipped.at[:, lanes(other * 4 + shift(y, o, Y))], rows_of(1, 4 - o), at_y_across[o - 1]))
    parts.append(net.push(clipped.at[:, lanes(other * 4 + y)], rows_of(1, 0), across))
    clipped_all[0:PAIRS, :] = clipped[:, lanes(k)]
    feats_cross.wait_recv()
    for copy in parts:
        copy.wait_recv()

    x_moves = []
    for o in (1, 2, 3, 0):
        block = feats_all[pl.ds(pl.multiple_of(shift(x, o, X) * SHARE, 16), SHARE), :]
        part = jnp.dot(block, clipped_all[...], preferred_element_type=F32)
        for piece in range(Z):
            shares[o, piece, 0:BLOCK, :] = part[piece * BLOCK:(piece + 1) * BLOCK]
        shares_send[o] = shares[o].astype(BF16)
        if o:
            x_moves.append(net.push(shares_send.at[o, :, 0:32, :], x_recv.at[o - 1], at_x[o - 1]))
    z_moves = [
        net.push(shares_send.at[:, shift(z, o, Z), 32:PADDED, :], z_recv.at[o - 1], at_z[o - 1])
        for o in range(1, Z)
    ]
    total = shares[0, :, 0:32, :]
    for o in range(1, X):
        x_moves[o - 1].wait_recv()
        total = total + x_recv[o - 1].astype(F32)
    x_part[...] = total
    x_send[...] = total.astype(BF16)
    x_moves = [
        net.push(x_send.at[shift(z, o, Z)], x_recv_last.at[o - 1], at_z[o - 1]) for o in range(1, Z)
    ]
    total = shares[:, z, 32:PADDED, :]
    for o in range(1, Z):
        z_moves[o - 1].wait_recv()
        total = total + z_recv[o - 1].astype(F32)
    z_send[...] = total.astype(BF16)
    z_moves = [net.push(z_send.at[o], z_recv_last.at[o - 1], at_x[o - 1]) for o in range(1, X)]
    upper, lower = x_part[z], total[0]
    for o in range(1, X):
        z_moves[o - 1].wait_recv()
        lower = lower + z_recv_last[o - 1].astype(F32)
    for o in range(1, Z):
        x_moves[o - 1].wait_recv()
        upper = upper + x_recv_last[o - 1].astype(F32)
    grad = jnp.concatenate([upper, lower], axis=0)

    new_sum = state_tile[0] + grad
    update_all[rows(z), :] = new_sum + state_tile[1]
    moves = [net.push(update_all.at[rows(z), :], update_all.at[rows(z), :], target) for target in at_z]
    for piece in range(8):
        first = 11 * (piece // 2) + 5 * (piece % 2)
        sums_send[piece] = new_sum[first:first + 8]
    arrive(start_moves)
    arrive(moves)

    update = update_all[...]
    square = jnp.sum((update * update).reshape(WIDE // 8, 8, 128), axis=0)
    at = 0
    for stage, targets in enumerate((at_x, at_y + [across] + at_y_across)):
        sq_send[stage] = square
        moves = [
            net.push(sq_send.at[stage], sq_recv.at[at + i], target)
            for i, target in enumerate(targets)
        ]
        for i, copy in enumerate(moves):
            copy.wait_recv()
            square = square + sq_recv[at + i]
        at += len(targets)
    norm = jnp.sqrt(jnp.sum(square, keepdims=True))
    cap = math.sqrt(W * E)
    shrink = cap / jnp.maximum(norm, cap)

    whole = start_all[...] - RATE * shrink * update
    whole = jnp.concatenate([whole[piece * PADDED:piece * PADDED + BLOCK] for piece in range(Z)], axis=0)
    weights_ref[x, :, lanes(k)] = whole.astype(BF16)

    half = SHARE // 2

    def low_piece(index, rows=(0, half)):
        return weights_ref.at[index, rows[0]:rows[1], lanes(c, 512)]

    def high_piece(away, shares=slice(0, X)):
        return weights_ref.at[shares, half:SHARE, lanes(c * 4 + shift(y, away, Y))]

    def send(piece, target):
        return net.push(piece, piece, target)

    moves_y = [send(weights_ref.at[x, 0:half, lanes(k)], target) for target in at_y]
    moves_x = [send(weights_ref.at[x, half:SHARE, lanes(k)], target) for target in at_x]
    sums_out = Scatter(
        net, sums_send, sums_ref,
        [device(x, 2 * zl + i // 4, zh2 + (i // 2) % 2, i % 2) for i in range(8)],
        [jnp.logical_and(half_y == zl, owner_slot == i) for i in range(8)],
        k,
    )
    sums_out.start()
    arrive(moves_y)
    low_moves = [send(low_piece(x), target) for target in (x_up, x_down)]
    arrive(moves_x)
    high_moves = [send(high_piece(0), target) for target in (y_up, y_down)]
    given = [send(low_piece(x), across), send(high_piece(0), across)]
    far = []
    for copy, away, rows_sent, target in (
        (low_moves[0], 3, (0, 96), x_up), (low_moves[1], 1, (96, half), x_down)
    ):
        copy.wait_recv()
        index = shift(x, away, X)
        far.append(send(low_piece(index, rows_sent), target))
        given.append(send(low_piece(index), across))
    for copy, away, shares, target in (
        (high_moves[0], 3, slice(0, 2), y_up), (high_moves[1], 1, slice(2, 4), y_down)
    ):
        copy.wait_recv()
        far.append(send(high_piece(away, shares), target))
        given.append(send(high_piece(away), across))
    arrive(far)
    given += [send(low_piece(shift(x, 2, X)), across), send(high_piece(2), across)]
    arrive(given)
    sums_out.wait()
    state_out.wait_sent()
    sums_out.wait_sent()
    net.finish()


def body(
    image_feats, text_emb, projection, clip_norms, user_ids, grad_sum, init_weights, tree_noise
):
    c = lax.rem(lax.axis_index("col"), 2)
    state = jnp.pad(jnp.stack([grad_sum, tree_noise, init_weights]), ((0, 0), (4, 4), (0, 0)))
    state = lax.dynamic_slice(state, (0, 4 - 4 * c, 0), (3, 48, 128))
    state = state.reshape(3, 6, 8, 128).transpose(2, 0, 1, 3)
    users = jnp.stack([user_ids.astype(F32), jnp.pad(clip_norms, (0, PAIRS - USERS))])
    users = jnp.pad(users[None, None], ((0, 7), (0, 2), (0, 0), (0, 0)))
    state = jnp.concatenate([state, users], axis=2)
    vmem = pl.BlockSpec(memory_space=pltpu.VMEM)
    weights, sums = pl.pallas_call(
        kernel,
        out_shape=(
            jax.ShapeDtypeStruct((X, SHARE, E), BF16),
            jax.ShapeDtypeStruct((8, 8, 128), F32),
        ),
        in_specs=[pl.BlockSpec(memory_space=pltpu.HBM)] * 4,
        out_specs=(vmem, vmem),
        scratch_shapes=[
            pltpu.VMEM((PAIRS, W), BF16),
            pltpu.VMEM((PAIRS, E), BF16),
            pltpu.VMEM((8, 3, 8, 128), F32),
            pltpu.VMEM((W, E), BF16),
            pltpu.VMEM((TEXTS, E), BF16),
            pltpu.VMEM((Z * PAIRS, E), BF16),
            pltpu.VMEM((PAIRS, E), F32),
            pltpu.VMEM((Z * PAIRS, E), F32),
            pltpu.VMEM((PAIRS, E), F32),
            pltpu.VMEM((2 * IMAGES, CHUNK), BF16),
            pltpu.VMEM((2 * IMAGES, CHUNK), BF16),
            pltpu.VMEM((7, HALF, E), BF16),
            pltpu.VMEM((7, HALF, E), BF16),
            pltpu.VMEM((7, HALF, E), BF16),
            pltpu.VMEM((7, HALF, E), BF16),
            pltpu.VMEM((7, 8, 128), F32),
            pltpu.VMEM((7, 8, 128), F32),
            pltpu.VMEM((7, 8, 128), F32),
            pltpu.VMEM((7, 8, 128), F32),
            pltpu.VMEM((W, 8 * PAIRS), BF16),
            pltpu.VMEM((PAIRS, E), BF16),
            pltpu.VMEM((8 * PAIRS, 128), BF16),
            pltpu.VMEM((X, Z, PADDED, 128), F32),
            pltpu.VMEM((X, Z, PADDED, 128), BF16),
            pltpu.VMEM((X - 1, Z, 32, 128), BF16),
            pltpu.VMEM((Z, 32, 128), F32),
            pltpu.VMEM((Z, 32, 128), BF16),
            pltpu.VMEM((Z - 1, 32, 128), BF16),
            pltpu.VMEM((Z - 1, X, 16, 128), BF16),
            pltpu.VMEM((X, 16, 128), BF16),
            pltpu.VMEM((X - 1, 16, 128), BF16),
            pltpu.VMEM((WIDE, 128), F32),
            pltpu.VMEM((WIDE, 128), F32),
            pltpu.VMEM((8, 3, 8, 128), F32),
            pltpu.VMEM((3, PADDED, 128), F32),
            pltpu.VMEM((8, 8, 128), F32),
            pltpu.VMEM((3, 8, 128), F32),
            pltpu.VMEM((17, 8, 128), F32),
            pltpu.SemaphoreType.DMA((4,)),
            pltpu.SemaphoreType.DMA((COPIES,)),
            pltpu.SemaphoreType.DMA((COPIES,)),
        ],
        compiler_params=pltpu.CompilerParams(
            collective_id=1, has_side_effects=True, vmem_limit_bytes=48 * 1024 * 1024
        ),
    )(
        image_feats, text_emb, projection, state,
    )
    sums = sums[:, :6].transpose(1, 0, 2).reshape(48, 128)
    return weights.reshape(W, E), lax.dynamic_slice(sums, (4 * c, 0), (44, 128))


def solution(mesh):
    in_specs = (
        P(("row", "col"), None),
        P(("row", "col"), None),
        P(),
        P(("row", "col")),
        P(("row", "col")),
        P(("row", "col"), None),
        P(("row", "col"), None),
        P(("row", "col"), None),
    )
    out_specs = (P(), P(("row", "col"), None))
    return jax.shard_map(body, mesh=mesh, in_specs=in_specs, out_specs=out_specs, check_vma=False)
```
